32 devices in a mesh: groups: 2 (over y), seq: 4 (over z), tp: 2 (over x), kv: 2 (over core).
Axes of the slice: x: 2, y: 2, z: 4, core: 2. Of those that a mesh axis runs over, the one named last changes fastest.
Arguments:
- events: bfloat16 [8, 512, 2048], P('groups', 'seq', ('tp', 'kv')), parts along dimension 0, may hold values from -6 to 6
- history_cache: bfloat16 [2, 8, 512, 1024], P(None, ('groups', 'seq'), None, ('tp', 'kv')), parts along dimension 1, may hold values from -6 to 6
- block_counts: int32 [8], P(('groups', 'seq')), parts along dimension 0, may hold values from 1 to 4
- semantic_ids: int32 [4, 128], P(None, ('groups', 'seq')), parts along dimension 1, may hold values from 0 to 4095
- beam_parents: int32 [3, 128], P(None, ('groups', 'seq')), parts along dimension 1, may hold values from 0 to 15
- query_weight: bfloat16 [2048, 2048], P('seq', ('tp', 'kv')), may hold values from -0.125 to 0.125
- keyval_weight: bfloat16 [2, 2048, 1024], P(None, 'seq', ('tp', 'kv')), may hold values from -0.125 to 0.125
- out_weight: bfloat16 [2048, 2048], P('seq', ('tp', 'kv')), may hold values from -0.125 to 0.125
- cross_weight: bfloat16 [2, 2048, 1024], P(None, 'seq', ('tp', 'kv')), may hold values from -0.125 to 0.125
- decoder_query: bfloat16 [2048, 2048], P(None, ('tp', 'kv')), may hold values from -0.125 to 0.125
- decoder_out: bfloat16 [2048, 2048], P(None, ('tp', 'kv')), may hold values from -0.125 to 0.125
- code_table: bfloat16 [4096, 2048], P(('tp', 'kv')), may hold values from -6 to 6
- encoder_gain: float32 [2048], replicated, may hold values from 0.25 to 1.75
- cross_gain: float32 [2048], replicated, may hold values from 0.25 to 1.75
- decoder_gain: float32 [2048], replicated, may hold values from 0.25 to 1.75
Outputs:
- encoded: bfloat16 [8, 512, 2048], P(('groups', 'seq'), ('tp', 'kv')), parts along dimension 0
- beam_state: bfloat16 [128, 2048], P(('groups', 'seq'), ('tp', 'kv')), parts along dimension 0
The draws below stay inside these ranges and needn't reach their ends.
There are 2 independent parts, one for each index of `groups`. The reference program is written for one: setup_inputs(seed, part) draws one part's arguments, and reference() takes and returns one part's arrays. A program takes and returns all parts, laid end to end along the dimension named above; an argument that names none is the same for every part. Nothing has to cross between parts.
Inputs may be any that keep to these rules, and one draw needn't show every extreme that they name: A user's first 128 * block_counts new events are real; the rest are padding. `semantic_ids`: the codebook entry decoded for each beam row. `beam_parents`: the beam of the previous step that each beam row continues, counted among its user's 16 beams.
All inputs are finite; a program needn't handle non-finite values.
Results may differ from the reference program's by a relative error of at most 0.014.
Values may be sent and summed in bfloat16 or wider, within the bound.
No kernel may reach another device: no remote copies, remote signals or barrier semaphores. Data moves between devices by JAX's collectives and lax.ppermute only.
A program may use at most 64 MiB of HBM per device.

```python
import jax
import jax.numpy as jnp
from jax import lax

D = 2048
H = 16
DH = 128
KVH = 8
V = 4096
EV = 512
BLK = 128
HIST = 512
BEAMS = 16
STEPS = 4
USERS = 4
N_TP = 2
N_KV = 2


def touch_ends(array, stream_key, low, largest):
    longest = array.shape.index(max(array.shape))
    spots = []
    for shift in (0, 1):
        where = [jax.random.randint(jax.random.fold_in(stream_key, axis), (), 0, length) for axis, length in enumerate(array.shape)]
        where[longest] = (where[longest] + shift) % array.shape[longest]
        spots.append(tuple(where))
    return array.at[spots[0]].set(low).at[spots[1]].set(largest)


def levels(rng, dims, cuts, smallest, top_value):
    gain, own = 1.0, jax.random.fold_in(rng, 6)
    for dim, blocks in cuts:
        heights = jnp.exp(jax.random.uniform(jax.random.fold_in(own, dim), (blocks,), jnp.float32, smallest / len(cuts), top_value / len(cuts)))
        gain = gain * jnp.repeat(heights, dims[dim] // blocks).reshape([-1 if axis == dim else 1 for axis in range(len(dims))])
    return gain


def scatter_about(rng, dims, scale, limit, split=(), held_as=jnp.bfloat16):
    values = jax.random.normal(rng, dims, jnp.float32) * scale
    if len(split) > 0:
        values = levels(rng, dims, split, -0.22, 0.18) * values
    return jnp.clip(values, min=-limit, max=limit).astype(held_as)


def setup_inputs(seed: int = 0, part: int = 0) -> dict:
    keys = jax.random.split(jax.random.key(seed), 16)
    part_keys = jax.random.split(jax.random.fold_in(keys[15], part), 16)
    return {
        "events": scatter_about(part_keys[0], (USERS, EV, D), 1.0, 6.0, ((1, 4), (2, 4))),
        "history_cache": scatter_about(part_keys[1], (2, USERS, HIST, KVH * DH), 1.0, 6.0, ((1, 4), (3, 4))),
        "block_counts": touch_ends(jax.random.randint(part_keys[2], (USERS,), 1, EV // BLK + 1), jax.random.fold_in(part_keys[2], 1), 1, (EV // BLK + 1) - 1).astype(jnp.int32),
        "semantic_ids": touch_ends(jax.random.randint(part_keys[3], (STEPS, USERS * BEAMS), 0, V), jax.random.fold_in(part_keys[3], 1), 0, V - 1).astype(jnp.int32),
        "beam_parents": touch_ends(jax.random.randint(part_keys[4], (STEPS - 1, USERS * BEAMS), 0, BEAMS), jax.random.fold_in(part_keys[4], 1), 0, BEAMS - 1).astype(jnp.int32),
        "query_weight": scatter_about(keys[5], (D, H * DH), D ** -0.5, 0.125, ((0, 4), (1, 4))),
        "keyval_weight": scatter_about(keys[6], (2, D, KVH * DH), D ** -0.5, 0.125, ((1, 4), (2, 4))),
        "out_weight": scatter_about(keys[7], (D, H * DH), (H * DH) ** -0.5, 0.125, ((0, 4), (1, 4))),
        "cross_weight": scatter_about(keys[8], (2, D, KVH * DH), D ** -0.5, 0.125, ((1, 4), (2, 4))),
        "decoder_query": scatter_about(keys[9], (D, H * DH), D ** -0.5, 0.125, ((1, 4),)),
        "decoder_out": scatter_about(keys[10], (D, H * DH), (H * DH) ** -0.5, 0.125, ((1, 4),)),
        "code_table": scatter_about(keys[11], (V, D), 1.0, 6.0, ((0, 4),)),
        "encoder_gain": jnp.clip(1.0 + 0.15 * jax.random.normal(keys[12], (D,), jnp.float32), 0.25, 1.75),
        "cross_gain": jnp.clip(1.0 + 0.15 * jax.random.normal(keys[13], (D,), jnp.float32), 0.25, 1.75),
        "decoder_gain": jnp.clip(1.0 + 0.15 * jax.random.normal(keys[14], (D,), jnp.float32), 0.25, 1.75),
    }


eps = 1e-06

def root_norm(values, scale_gain):
    mean_square = lax.optimization_barrier(jnp.mean(values * values, axis=-1, keepdims=True))
    return values * lax.rsqrt(mean_square + eps) * scale_gain.astype(jnp.float32)

def encode_user(item, query_weight, keyval_weight, out_weight, cross_weight, encoder_gain, cross_gain):
    user_events, user_cache, user_blocks = item
    groups = N_TP * N_KV
    per_group = H // groups
    group_ratio = H // KVH
    source = user_events.astype(jnp.float32)
    normed = root_norm(source, encoder_gain).astype(jnp.bfloat16)
    queries = jnp.dot(normed, query_weight, preferred_element_type=jnp.float32).astype(jnp.bfloat16)
    keys_new = jnp.dot(normed, keyval_weight[0], preferred_element_type=jnp.float32).astype(jnp.bfloat16)
    values_new = jnp.dot(normed, keyval_weight[1], preferred_element_type=jnp.float32).astype(jnp.bfloat16)
    keys_all = jnp.concatenate([user_cache[0], keys_new], axis=0)
    values_all = jnp.concatenate([user_cache[1], values_new], axis=0)
    query_heads = queries.reshape(EV, KVH, group_ratio, DH).astype(jnp.float32)
    key_heads = keys_all.reshape(HIST + EV, KVH, DH).astype(jnp.float32)
    value_heads = values_all.reshape(HIST + EV, KVH, DH).astype(jnp.float32)
    scores = jnp.einsum('igad,jgd->gaij', query_heads, key_heads) * DH ** (-0.5)
    query_index = jnp.arange(EV, dtype=jnp.int32)[:, None]
    key_index = jnp.arange(HIST + EV, dtype=jnp.int32)[None, :] - HIST
    visible = (key_index < 0) | (key_index <= query_index) & (key_index < user_blocks * BLK)
    raised = jnp.where(visible, jnp.exp(scores), jnp.float32(0.0))
    denominator = lax.optimization_barrier(jnp.sum(raised, axis=-1, keepdims=True))
    softened = (raised / denominator).astype(jnp.bfloat16)
    attended = jnp.einsum('gaij,jgd->igad', softened.astype(jnp.float32), value_heads)
    attended = attended.reshape(EV, H * DH).astype(jnp.bfloat16)
    grouped = attended.reshape(EV, groups, per_group * DH).astype(jnp.float32)
    out_grouped = out_weight.reshape(D, groups, per_group * DH).astype(jnp.float32)
    group_terms = jnp.einsum('igc,ogc->gio', grouped, out_grouped).astype(jnp.bfloat16)
    encoded_full = source + lax.optimization_barrier(jnp.sum(group_terms.astype(jnp.float32), axis=0))
    cross_in = root_norm(encoded_full, cross_gain).astype(jnp.bfloat16)
    cross_keys = jnp.dot(cross_in, cross_weight[0], preferred_element_type=jnp.float32).astype(jnp.bfloat16)
    cross_values = jnp.dot(cross_in, cross_weight[1], preferred_element_type=jnp.float32).astype(jnp.bfloat16)
    return (encoded_full.astype(jnp.bfloat16), cross_keys, cross_values)

def reference(events, history_cache, block_counts, semantic_ids, beam_parents, query_weight, keyval_weight, out_weight, cross_weight, decoder_query, decoder_out, code_table, encoder_gain, cross_gain, decoder_gain):
    cache_users = jnp.moveaxis(history_cache, 1, 0)
    encoded, cross_keys, cross_values = lax.map(lambda item: encode_user(item, query_weight, keyval_weight, out_weight, cross_weight, encoder_gain, cross_gain), (events, cache_users, block_counts))
    group_ratio = H // KVH
    key_heads = cross_keys.reshape(USERS, EV, KVH, DH).astype(jnp.float32)
    value_heads = cross_values.reshape(USERS, EV, KVH, DH).astype(jnp.float32)
    live_events = jnp.arange(EV, dtype=jnp.int32)[None, :] < (block_counts * BLK)[:, None]
    live_mask = live_events[:, None, None, None, :]

    def attend(beam_hidden):
        normed = root_norm(beam_hidden, decoder_gain).astype(jnp.bfloat16)
        beam_queries = jnp.dot(normed, decoder_query, preferred_element_type=jnp.float32).astype(jnp.bfloat16)
        query_heads = beam_queries.reshape(USERS, BEAMS, KVH, group_ratio, DH).astype(jnp.float32)
        beam_scores = jnp.einsum('ubgad,ujgd->ugabj', query_heads, key_heads) * DH ** (-0.5)
        raised = jnp.where(live_mask, jnp.exp(beam_scores), jnp.float32(0.0))
        denominator = lax.optimization_barrier(jnp.sum(raised, axis=-1, keepdims=True))
        softened = (raised / denominator).astype(jnp.bfloat16)
        attended = jnp.einsum('ugabj,ujgd->ubgad', softened.astype(jnp.float32), value_heads)
        attended = attended.reshape(USERS * BEAMS, H * DH).astype(jnp.bfloat16)
        return lax.dot_general(attended, decoder_out, (((1,), (1,)), ((), ())), preferred_element_type=jnp.float32)
    code_rows = code_table.astype(jnp.float32)
    all_rows = jnp.arange(USERS * BEAMS, dtype=jnp.int32)
    beam_hidden = jnp.take(code_rows, semantic_ids[0], axis=0)
    mixed_state = attend(beam_hidden)
    for level in range(1, STEPS):
        source_rows = all_rows // BEAMS * BEAMS + beam_parents[level - 1]
        beam_hidden = jnp.take(beam_hidden + mixed_state, source_rows, axis=0) + jnp.take(code_rows, semantic_ids[level], axis=0)
        mixed_state = attend(beam_hidden)
    return (encoded, (beam_hidden + mixed_state).astype(jnp.bfloat16))
```

```python
import functools

import jax
import jax.numpy as jnp
from jax import lax
from jax.experimental import pallas as pl
from jax.experimental.pallas import tpu as pltpu
from jax.sharding import PartitionSpec as P

H = 16
DH = 128
KVH = 8
BLK = 128
STEPS = 4
RING_LIMIT = 8
VMEM_BYTES = 56 * 1024 * 1024

eps = 1e-06

VM = pl.BlockSpec(memory_space=pltpu.VMEM)
SM = pl.BlockSpec(memory_space=pltpu.SMEM)
HB = pl.BlockSpec(memory_space=pl.ANY)


def params():
    return pltpu.CompilerParams(vmem_limit_bytes=VMEM_BYTES)


def partner(index, step, size):
    if size & (size - 1) == 0:
        return index ^ step
    return (index + step) % size


def origin(index, step, size):
    if size & (size - 1) == 0:
        return index ^ step
    return (index - step) % size


def exchange(value, axis, step):
    size = lax.axis_size(axis)
    return lax.ppermute(value, axis, [(i, partner(i, step, size)) for i in range(size)])


def shift(value, axis, step):
    size = lax.axis_size(axis)
    return lax.ppermute(value, axis, [(i, (i + step) % size) for i in range(size)])


def after(value, *others):
    return lax.optimization_barrier((value, *others))[0]


def gather_rows(value):
    size = lax.axis_size("seq")
    rows = value.shape[0]
    here = lax.axis_index("seq")
    if size > RING_LIMIT:
        return [(lax.all_gather(value, "seq", axis=0, tiled=True), jnp.int32(0))], []
    twins = lax.axis_size("groups")
    share = twins == 2 and rows % 32 == 0
    twin = lax.axis_index("groups")
    half = rows // 2
    moving = lax.dynamic_slice_in_dim(value, twin * half, half, 0) if share else value
    pieces = [(value, here * rows)]
    arrivals = []
    for step in range(1, size):
        moving = shift(moving, "seq", 1)
        arrivals.append(moving)
        first = (here - step) % size * rows
        if share:
            pieces.append((moving, first + twin * half))
            pieces.append((exchange(moving, "groups", 1), first + (1 - twin) * half))
        else:
            pieces.append((moving, first))
    return pieces, arrivals


def gather_heads(value):
    tp, kv = lax.axis_size("tp"), lax.axis_size("kv")
    my_tp, my_kv = lax.axis_index("tp"), lax.axis_index("kv")
    along = [(value, my_tp)]
    for step in range(1, tp):
        along.append((exchange(value, "tp", step), origin(my_tp, step, tp)))
    pieces = []
    for piece, where in along:
        pieces.append((piece, where * kv + my_kv))
    for piece, where in along:
        for step in range(1, kv):
            pieces.append((exchange(piece, "kv", step), where * kv + origin(my_kv, step, kv)))
    return pieces


def collect_events(events):
    size = lax.axis_size("seq")
    here = lax.axis_index("seq")
    rows = events.shape[1]
    if size > RING_LIMIT:
        mine = lax.all_to_all(events, "seq", split_axis=0, concat_axis=1, tiled=True)[0]
        return gather_heads(mine), [jnp.int32(0)]
    blocks = [lax.dynamic_index_in_dim(events, here, 0, False)]
    firsts = [here * rows]
    for step in range(1, size):
        block = lax.dynamic_index_in_dim(events, (here + step) % size, 0, False)
        blocks.append(shift(block, "seq", step))
        firsts.append((here - step) % size * rows)
    return gather_heads(jnp.concatenate(blocks, axis=0)), firsts


def norm_kernel(count, blocks, col_ref, row_ref, gain_ref, *refs):
    pieces, (normed_ref, source_ref) = refs[:count], refs[count:]
    width = normed_ref.shape[1]
    cols = pieces[0].shape[1]
    rows = pieces[0].shape[0] // blocks
    for block in range(blocks):
        first = pl.multiple_of(row_ref[block], rows)
        parts = [p[block * rows : (block + 1) * rows, :].astype(jnp.float32) for p in pieces]
        square = sum(jnp.sum(v * v, axis=-1, keepdims=True) for v in parts)
        scale = lax.rsqrt(square / width + eps)
        for index in range(count):
            col = pl.ds(pl.multiple_of(col_ref[index], cols), cols)
            source_ref[pl.ds(first, rows), col] = parts[index].astype(jnp.bfloat16)
            normed_ref[pl.ds(first, rows), col] = (
                parts[index] * scale * gain_ref[:, col]
            ).astype(jnp.bfloat16)


def norm_events(pieces, firsts, gain):
    cols = pieces[0][0].shape[1]
    length = pieces[0][0].shape[0]
    width = gain.shape[0]
    shape = jax.ShapeDtypeStruct((length, width), jnp.bfloat16)
    return pl.pallas_call(
        functools.partial(norm_kernel, len(pieces), len(firsts)),
        out_shape=(shape, shape),
        in_specs=[SM, SM] + [VM] * (1 + len(pieces)),
        out_specs=(VM, VM),
        compiler_params=params(),
        name="norm_events",
    )(
        jnp.stack([where * cols for _, where in pieces]),
        jnp.stack(firsts),
        gain[None, :],
        *[piece for piece, _ in pieces],
    )


def load_pieces(pieces, first_ref, base, whole, columns, sems):
    copies = []
    for index, piece in enumerate(pieces):
        rows = piece.shape[0]
        first = pl.multiple_of(first_ref[base + index], rows)
        copy = pltpu.make_async_copy(
            piece, whole.at[pl.ds(first, rows), columns], sems.at[base + index]
        )
        copy.start()
        copies.append(copy)
    return copies


def encoder_kernel(
    counts, ratio, first_ref, live_ref, normed_ref, history_ref, *refs
):
    query_count, keyval_count = counts
    total = query_count + keyval_count
    pieces, (out_ref, whole, projected, sems) = refs[:total], refs[total:]
    length = normed_ref.shape[0]
    heads = out_ref.shape[1] // DH
    kv_heads = heads // ratio
    query_cols = heads * DH
    key_cols = kv_heads * DH
    past = history_ref.shape[1]
    copies = load_pieces(
        pieces[:query_count], first_ref, 0, whole, pl.ds(0, query_cols), sems
    ) + load_pieces(
        pieces[query_count:], first_ref, query_count, whole, pl.ds(query_cols, 2 * key_cols), sems
    )
    for copy in copies:
        copy.wait()
    tile = min(256, length)
    for row in range(0, length, tile):
        projected[row : row + tile, :] = jnp.dot(
            normed_ref[row : row + tile, :], whole[...], preferred_element_type=jnp.float32
        ).astype(jnp.bfloat16)
    live = live_ref[0] * BLK
    contract = (((1,), (1,)), ((), ()))
    for group in range(kv_heads):
        keys = slice(query_cols + group * DH, query_cols + (group + 1) * DH)
        values = slice(query_cols + key_cols + group * DH, query_cols + key_cols + (group + 1) * DH)
        cached = slice(group * DH, (group + 1) * DH)
        for row in range(0, length, tile):
            reach = row + tile
            for head in range(group * ratio, (group + 1) * ratio):
                query = projected[row:reach, head * DH : (head + 1) * DH]
                old = lax.dot_general(
                    query, history_ref[0, :, cached], contract, preferred_element_type=jnp.float32
                )
                new = lax.dot_general(
                    query, projected[:reach, keys], contract, preferred_element_type=jnp.float32
                )
                query_index = row + lax.broadcasted_iota(jnp.int32, (tile, reach), 0)
                key_index = lax.broadcasted_iota(jnp.int32, (tile, reach), 1)
                new = jnp.where((key_index <= query_index) & (key_index < live), new, -1e30)
                top = jnp.maximum(
                    jnp.max(old, axis=-1, keepdims=True), jnp.max(new, axis=-1, keepdims=True)
                )
                scale = DH ** (-0.5)
                old = jnp.exp((old - top) * scale)
                new = jnp.exp((new - top) * scale)
                total_weight = jnp.sum(old, axis=-1, keepdims=True) + jnp.sum(
                    new, axis=-1, keepdims=True
                )
                mixed = jnp.dot(
                    old.astype(jnp.bfloat16),
                    history_ref[1, :, cached],
                    preferred_element_type=jnp.float32,
                ) + jnp.dot(
                    new.astype(jnp.bfloat16),
                    projected[:reach, values],
                    preferred_element_type=jnp.float32,
                )
                out_ref[row:reach, head * DH : (head + 1) * DH] = (mixed / total_weight).astype(
                    jnp.bfloat16
                )


def encoder_attention(normed, history, block_counts, query_pieces, keyval_pieces):
    length, width = normed.shape
    key_cols = history.shape[2]
    query_cols = query_pieces[0][0].shape[1]
    counts = (len(query_pieces), len(keyval_pieces))
    pieces = query_pieces + keyval_pieces
    joined = query_cols + 2 * key_cols
    return pl.pallas_call(
        functools.partial(encoder_kernel, counts, query_cols // key_cols),
        out_shape=jax.ShapeDtypeStruct((length, query_cols), jnp.bfloat16),
        in_specs=[SM, SM, VM, VM] + [HB] * len(pieces),
        out_specs=VM,
        scratch_shapes=[
            pltpu.VMEM((width, joined), jnp.bfloat16),
            pltpu.VMEM((length, joined), jnp.bfloat16),
            pltpu.SemaphoreType.DMA((len(pieces),)),
        ],
        compiler_params=params(),
        name="encoder_attention",
    )(
        jnp.stack([first for _, first in pieces]),
        block_counts,
        normed,
        history,
        *[piece for piece, _ in pieces],
    )


def project_kernel(count, groups, first_ref, share_ref, attended_ref, *refs):
    pieces, outs, (whole, sems) = refs[:count], refs[count:-2], refs[-2:]
    copies = load_pieces(pieces, first_ref, 0, whole, slice(None), sems)
    share = outs[0].shape[0] // groups
    for copy in copies:
        copy.wait()
    for index, out_ref in enumerate(outs):
        parts = []
        for group in range(groups):
            first = pl.multiple_of(share_ref[index * groups + group] * share, share)
            parts.append(attended_ref[pl.ds(first, share), :])
        rows = jnp.concatenate(parts, axis=0)
        out_ref[...] = lax.dot_general(
            rows, whole[...], (((1,), (1,)), ((), ())), preferred_element_type=jnp.float32
        ).astype(jnp.bfloat16)


def project_out(attended, pieces, orders):
    length, cols = attended.shape
    groups = lax.axis_size("tp")
    share = length // (groups * len(orders))
    width = sum(piece.shape[0] for piece, _ in pieces)
    shape = jax.ShapeDtypeStruct((groups * share, width), jnp.bfloat16)
    return pl.pallas_call(
        functools.partial(project_kernel, len(pieces), groups),
        out_shape=tuple([shape] * len(orders)),
        in_specs=[SM, SM, VM] + [HB] * len(pieces),
        out_specs=tuple([VM] * len(orders)),
        scratch_shapes=[
            pltpu.VMEM((width, cols), jnp.bfloat16),
            pltpu.SemaphoreType.DMA((len(pieces),)),
        ],
        compiler_params=params(),
        name="project_out",
    )(
        jnp.stack([first for _, first in pieces]),
        jnp.stack([where for order in orders for where in order]),
        attended,
        *[piece for piece, _ in pieces],
    )


def merge_kernel(count, place_ref, gain_ref, source_ref, *refs):
    terms, (encoded_ref, crossed_ref) = refs[:count], refs[count:]
    rows = encoded_ref.shape[0]
    first = pl.multiple_of(place_ref[0], rows)
    total = source_ref[pl.ds(first, rows), :].astype(jnp.float32)
    for term in terms:
        total = total + term[...].astype(jnp.float32)
    encoded_ref[...] = total.astype(jnp.bfloat16)
    square = jnp.mean(total * total, axis=-1, keepdims=True)
    crossed_ref[...] = (total * lax.rsqrt(square + eps) * gain_ref[...]).astype(jnp.bfloat16)


def merge_terms(source, terms, place, gain):
    shape = jax.ShapeDtypeStruct(terms[0].shape, jnp.bfloat16)
    return pl.pallas_call(
        functools.partial(merge_kernel, len(terms)),
        out_shape=(shape, shape),
        in_specs=[SM] + [VM] * (2 + len(terms)),
        out_specs=(VM, VM),
        compiler_params=params(),
        name="merge_terms",
    )(place[None], gain[None, :], source, *terms)


def cross_kernel(row_count, count, first_ref, place_ref, *refs):
    rows_refs, pieces = refs[:row_count], refs[row_count : row_count + count]
    out_ref, whole, sems = refs[row_count + count :]
    copies = load_pieces(pieces, first_ref, 0, whole, slice(None), sems)
    for copy in copies:
        copy.wait()
    rows = rows_refs[0].shape[0]
    for index, rows_ref in enumerate(rows_refs):
        first = pl.multiple_of(place_ref[index] * rows, rows)
        out_ref[pl.ds(first, rows), :] = jnp.dot(
            rows_ref[...], whole[...], preferred_element_type=jnp.float32
        ).astype(jnp.bfloat16)


def cross_project(row_pieces, pieces):
    width = row_pieces[0][0].shape[1]
    rows = row_pieces[0][0].shape[0]
    cols = pieces[0][0].shape[1]
    return pl.pallas_call(
        functools.partial(cross_kernel, len(row_pieces), len(pieces)),
        out_shape=jax.ShapeDtypeStruct((rows * len(row_pieces), cols), jnp.bfloat16),
        in_specs=[SM, SM] + [VM] * len(row_pieces) + [HB] * len(pieces),
        out_specs=VM,
        scratch_shapes=[
            pltpu.VMEM((width, cols), jnp.bfloat16),
            pltpu.SemaphoreType.DMA((len(pieces),)),
        ],
        compiler_params=params(),
        name="cross_project",
    )(
        jnp.stack([first for _, first in pieces]),
        jnp.stack([where for _, where in row_pieces]),
        *[rows for rows, _ in row_pieces],
        *[piece for piece, _ in pieces],
    )


def beam_kernel(
    level, count, last, ratio,
    live_ref, parent_ref, place_ref, gain_ref, query_ref, out_weight_ref, cross_ref, code_ref,
    *refs,
):
    inputs, outs, moved = refs[: count + 1 if level else 0], refs[count + 1 if level else 0 : -1], refs[-1]
    beams = code_ref.shape[0]
    code = code_ref[...].astype(jnp.float32)
    if level:
        total = inputs[0][...]
        for term in inputs[1:]:
            total = total + term[...].astype(jnp.float32)
        moved[...] = total
        rows = [moved[pl.ds(parent_ref[level - 1, row], 1), :] for row in range(beams)]
        hidden = jnp.concatenate(rows, axis=0) + code
    else:
        hidden = code
    square = jnp.mean(hidden * hidden, axis=-1, keepdims=True)
    normed = (hidden * lax.rsqrt(square + eps) * gain_ref[...]).astype(jnp.bfloat16)
    queries = jnp.dot(normed, query_ref[...], preferred_element_type=jnp.float32)
    queries = queries.astype(jnp.bfloat16)
    key_cols = cross_ref.shape[1] // 2
    events = cross_ref.shape[0]
    live = live_ref[0] * BLK
    attended = []
    for group in range(key_cols // DH):
        first = group * ratio
        stacked = jnp.concatenate(
            [queries[:, h * DH : (h + 1) * DH] for h in range(first, first + ratio)], axis=0
        )
        scores = lax.dot_general(
            stacked,
            cross_ref[:, group * DH : (group + 1) * DH],
            (((1,), (1,)), ((), ())),
            preferred_element_type=jnp.float32,
        )
        index = lax.broadcasted_iota(jnp.int32, scores.shape, 1)
        scores = jnp.where(index < live, scores, -1e30)
        top = jnp.max(scores, axis=-1, keepdims=True)
        raised = jnp.exp((scores - top) * DH ** (-0.5))
        weight = jnp.sum(raised, axis=-1, keepdims=True)
        mixed = jnp.dot(
            raised.astype(jnp.bfloat16),
            cross_ref[:, key_cols + group * DH : key_cols + (group + 1) * DH],
            preferred_element_type=jnp.float32,
        )
        mixed = (mixed / weight).astype(jnp.bfloat16)
        attended += [mixed[h * beams : (h + 1) * beams, :] for h in range(ratio)]
    terms = jnp.dot(
        jnp.concatenate(attended, axis=1), out_weight_ref[...], preferred_element_type=jnp.float32
    )
    if not last:
        outs[0][...] = hidden
        outs[1][...] = terms.astype(jnp.bfloat16)
    else:
        cols = outs[0].shape[1]
        moved[...] = terms
        for index in range(1, len(outs)):
            col = pl.ds(pl.multiple_of(place_ref[index] * cols, cols), cols)
            outs[index][...] = moved[:, col].astype(jnp.bfloat16)
        moved[...] = hidden + terms
        outs[0][...] = moved[:, pl.ds(pl.multiple_of(place_ref[0] * cols, cols), cols)]


def beam_step(level, live, parents, places, gain, query, out_weight, cross, code, inputs, last):
    beams, width = code.shape
    ratio = H // KVH
    if last:
        cols = width // len(places)
        outs = [jax.ShapeDtypeStruct((beams, cols), jnp.float32)] + [
            jax.ShapeDtypeStruct((beams, cols), jnp.bfloat16)
        ] * (len(places) - 1)
    else:
        outs = [
            jax.ShapeDtypeStruct((beams, width), jnp.float32),
            jax.ShapeDtypeStruct((beams, width), jnp.bfloat16),
        ]
    return pl.pallas_call(
        functools.partial(beam_kernel, level, max(len(inputs) - 1, 0), last, ratio),
        out_shape=tuple(outs),
        in_specs=[SM, SM, SM] + [VM] * (5 + len(inputs)),
        out_specs=tuple([VM] * len(outs)),
        scratch_shapes=[pltpu.VMEM((beams, width), jnp.float32)],
        compiler_params=params(),
        name=f"beam_step_{level}",
    )(live, parents, jnp.stack(places), gain[None, :], query, out_weight, cross, code, *inputs)


def shards(
    events,
    history_cache,
    block_counts,
    semantic_ids,
    beam_parents,
    query_weight,
    keyval_weight,
    out_weight,
    cross_weight,
    decoder_query,
    decoder_out,
    code_table,
    encoder_gain,
    cross_gain,
    decoder_gain,
):
    tp, kv = lax.axis_size("tp"), lax.axis_size("kv")
    my_tp, my_kv = lax.axis_index("tp"), lax.axis_index("kv")
    group, groups = my_tp * kv + my_kv, tp * kv

    keyval = jnp.concatenate([keyval_weight[0], keyval_weight[1]], axis=1)
    crossing = jnp.concatenate([cross_weight[0], cross_weight[1]], axis=1)
    query_pieces, query_steps = gather_rows(query_weight)
    keyval_pieces, keyval_steps = gather_rows(keyval)
    event_pieces, firsts = collect_events(events)
    normed, source = norm_events(event_pieces, firsts, encoder_gain)
    out_pieces, out_steps = gather_rows(after(out_weight, *query_steps[-1:]))
    cross_pieces, _ = gather_rows(after(crossing, *keyval_steps[-1:]))

    vocab_rows = code_table.shape[0]
    vocab_ids = group * vocab_rows + lax.broadcasted_iota(jnp.int32, (1, vocab_rows), 1)
    onehot = (semantic_ids.reshape(-1)[:, None] == vocab_ids).astype(jnp.bfloat16)
    codes = jnp.dot(onehot, code_table, preferred_element_type=jnp.float32).astype(jnp.bfloat16)
    for axis, size in (("kv", kv), ("tp", tp)):
        codes = sum([exchange(codes, axis, step) for step in range(1, size)], codes)
    steps, beams = semantic_ids.shape
    codes = codes.reshape(steps, beams, codes.shape[1])
    out_turned = decoder_out.T

    attended = encoder_attention(
        normed, history_cache[:, 0], block_counts, query_pieces, keyval_pieces
    )
    orders = [
        [partner(my_tp, d, tp) * kv + partner(my_kv, e, kv) for d in range(tp)] for e in range(kv)
    ]
    kept, *sent = project_out(attended, out_pieces, orders)
    arrived = [exchange(terms, "kv", e + 1) for e, terms in enumerate(sent)]
    share = attended.shape[0] // groups

    def summed(d):
        rows = slice(d * share, (d + 1) * share)
        return sum([a[rows].astype(jnp.float32) for a in arrived], kept[rows].astype(jnp.float32))

    terms = [exchange(summed(d).astype(jnp.bfloat16), "tp", d) for d in range(1, tp)]
    terms = [kept[:share]] + [a[:share] for a in arrived] + terms
    encoded, crossed = merge_terms(source, terms, group * share, cross_gain)
    cross = cross_project(gather_heads(crossed), cross_pieces)

    places = [group]
    moves = []
    for d in range(tp):
        for e in range(kv):
            if d or e:
                places.append(partner(my_tp, d, tp) * kv + partner(my_kv, e, kv))
                moves.append(
                    [
                        (a * kv + b, partner(a, d, tp) * kv + partner(b, e, kv))
                        for a in range(tp)
                        for b in range(kv)
                    ]
                )
    inputs = []
    for level in range(steps):
        last = level == steps - 1
        kept, *sent = beam_step(
            level, block_counts, beam_parents, places, decoder_gain, decoder_query, out_turned,
            cross, codes[level], inputs, last,
        )
        if not last:
            sent = sent * len(moves)
        arrived = [lax.ppermute(v, ("tp", "kv"), move) for v, move in zip(sent, moves)]
        inputs = [kept] + sent[:1] + arrived
    beam_out = sum([a.astype(jnp.float32) for a in arrived], kept).astype(jnp.bfloat16)
    return (encoded[None], beam_out)


def solution(mesh):
    in_specs = (
        P("groups", "seq", ("tp", "kv")),
        P(None, ("groups", "seq"), None, ("tp", "kv")),
        P(("groups", "seq")),
        P(None, ("groups", "seq")),
        P(None, ("groups", "seq")),
        P("seq", ("tp", "kv")),
        P(None, "seq", ("tp", "kv")),
        P("seq", ("tp", "kv")),
        P(None, "seq", ("tp", "kv")),
        P(None, ("tp", "kv")),
        P(None, ("tp", "kv")),
        P(("tp", "kv"), None),
        P(),
        P(),
        P(),
    )
    out_specs = (P(("groups", "seq"), ("tp", "kv"), None), P(("groups", "seq"), ("tp", "kv")))
    return jax.shard_map(shards, mesh=mesh, in_specs=in_specs, out_specs=out_specs, check_vma=False)
```

```python
import functools

import jax
import jax.numpy as jnp
from jax import lax
from jax.experimental import pallas as pl
from jax.experimental.pallas import tpu as pltpu
from jax.sharding import PartitionSpec as P

H = 16
DH = 128
KVH = 8
BLK = 128
STEPS = 4
RING_LIMIT = 8
RING_WAYS = (1, -1)
VMEM_BYTES = 56 * 1024 * 1024

eps = 1e-06

VM = pl.BlockSpec(memory_space=pltpu.VMEM)
SM = pl.BlockSpec(memory_space=pltpu.SMEM)
HB = pl.BlockSpec(memory_space=pl.ANY)


def params():
    return pltpu.CompilerParams(vmem_limit_bytes=VMEM_BYTES)


def cost(micros):
    return pl.CostEstimate(flops=0, bytes_accessed=int(micros * 3.0e6), transcendentals=0)


def partner(index, step, size):
    if size & (size - 1) == 0:
        return index ^ step
    return (index + step) % size


def origin(index, step, size):
    if size & (size - 1) == 0:
        return index ^ step
    return (index - step) % size


def exchange(value, axis, step):
    size = lax.axis_size(axis)
    return lax.ppermute(value, axis, [(i, partner(i, step, size)) for i in range(size)])


def shift(value, axis, step):
    size = lax.axis_size(axis)
    return lax.ppermute(value, axis, [(i, (i + step) % size) for i in range(size)])


def after(value, *others):
    return lax.optimization_barrier((value, *others))[0]


def position():
    return jnp.stack([lax.axis_index(axis) for axis in ("seq", "groups", "tp", "kv")])


def gather_heads(value, beside=None):
    tp, kv = lax.axis_size("tp"), lax.axis_size("kv")
    along = [(value, lambda at: at[2])]
    for step in range(1, tp):
        along.append(
            (exchange(value, "tp", step), functools.partial(lambda d, at: origin(at[2], d, tp), step))
        )
    waits = beside() if beside else []
    if waits:
        along = along[:1] + [(after(piece, *waits), where) for piece, where in along[1:]]
    pieces = []
    for piece, where in along:
        pieces.append((piece, functools.partial(lambda f, at: f(at) * kv + at[3], where)))
    for piece, where in along:
        for step in range(1, kv):
            pieces.append(
                (
                    exchange(piece, "kv", step),
                    functools.partial(
                        lambda f, e, at: f(at) * kv + origin(at[3], e, kv), where, step
                    ),
                )
            )
    return pieces


class Rows:
    def __init__(self, value, *waits):
        self.size = lax.axis_size("seq")
        self.rows = value.shape[0]
        self.shared = lax.axis_size("groups") == 2 and self.rows % 32 == 0
        self.pieces = [(value, [functools.partial(lambda r, at: at[0] * r, self.rows)])]
        half = self.rows // 2
        if self.shared:
            value = lax.dynamic_slice_in_dim(value, lax.axis_index("groups") * half, half, 0)
        if waits:
            value = after(value, *waits)
        self.last = {1: value, -1: value}
        self.hops = {1: 0, -1: 0}
        self.fresh = []

    def hop(self, way, *waits):
        arrived = shift(after(self.last[way], *waits) if waits else self.last[way], "seq", way)
        self.last[way] = arrived
        self.hops[way] += 1
        self.fresh.append((arrived, way * self.hops[way]))

    def place(self, distance, twin):
        size, rows = self.size, self.rows

        def first(at):
            row = lax.rem(at[0] + size - distance, size) * rows
            return row + (at[1] ^ twin) * (rows // 2) if self.shared else row

        return [first]

    def keep(self):
        for arrived, distance in self.fresh:
            self.pieces.append((arrived, self.place(distance, 0)))
        self.fresh = []

    def swap(self, *waits):
        for arrived, distance in self.fresh:
            self.pieces.append((arrived, self.place(distance, 0)))
            if self.shared:
                other = exchange(after(arrived, *waits) if waits else arrived, "groups", 1)
                self.pieces.append((other, self.place(distance, 1)))
        self.fresh = []

    def direct(self, distance, *waits):
        if self.shared:
            half = self.rows // 2
            rest = 1 - lax.axis_index("groups")
            other = lax.dynamic_slice_in_dim(self.pieces[0][0], rest * half, half, 0)
            other = shift(after(other, *waits) if waits else other, "seq", distance)
            self.pieces.append((other, self.place(distance, 1)))

    def start(self, *waits):
        for way in RING_WAYS[: self.size - 1]:
            self.hop(way, *waits)

    def swapped(self):
        return self.pieces[-1][0]

    def end(self, *waits):
        for hop in range(len(RING_WAYS), self.size - 1):
            self.hop(RING_WAYS[hop % len(RING_WAYS)], *waits)

    def held(self, *waits):
        arrays = lax.optimization_barrier((*[piece for piece, _ in self.pieces], *waits))
        self.pieces = [(piece, places) for piece, (_, places) in zip(arrays, self.pieces)]
        return arrays[len(self.pieces) :]


def whole_rows(value):
    return [(lax.all_gather(value, "seq", axis=0, tiled=True), [lambda at: 0])]


def collect_events(events):
    size = lax.axis_size("seq")
    here = lax.axis_index("seq")
    rows = events.shape[1]
    if size > RING_LIMIT:
        return [lax.all_to_all(events, "seq", split_axis=0, concat_axis=1, tiled=True)[0]], [lambda at: 0]
    blocks = [lax.dynamic_index_in_dim(events, here, 0, False)]
    firsts = [lambda at: at[0] * rows]
    for step in range(1, size):
        block = lax.dynamic_index_in_dim(events, (here + step) % size, 0, False)
        blocks.append(shift(block, "seq", step))
        firsts.append(
            functools.partial(lambda d, at: lax.rem(at[0] + size - d, size) * rows, step)
        )
    return blocks, firsts


def norm_kernel(places, firsts, at_ref, gain_ref, *refs):
    count, blocks = len(places), len(firsts)
    pieces, (normed_ref, source_ref) = refs[:count], refs[count:]
    width = normed_ref.shape[1]
    cols = pieces[0].shape[1]
    rows = pieces[0].shape[0] // blocks
    for block in range(blocks):
        first = pl.multiple_of(firsts[block](at_ref), rows)
        parts = [p[block * rows : (block + 1) * rows, :].astype(jnp.float32) for p in pieces]
        square = sum(jnp.sum(v * v, axis=-1, keepdims=True) for v in parts)
        scale = lax.rsqrt(square / width + eps)
        for index in range(count):
            col = pl.ds(pl.multiple_of(places[index](at_ref) * cols, cols), cols)
            source_ref[pl.ds(first, rows), col] = parts[index].astype(jnp.bfloat16)
            normed_ref[pl.ds(first, rows), col] = (
                parts[index] * scale * gain_ref[:, col]
            ).astype(jnp.bfloat16)


def norm_events(at, pieces, firsts, gain):
    length = pieces[0][0].shape[0]
    width = gain.shape[0]
    shape = jax.ShapeDtypeStruct((length, width), jnp.bfloat16)
    return pl.pallas_call(
        functools.partial(norm_kernel, [where for _, where in pieces], firsts),
        out_shape=(shape, shape),
        in_specs=[SM] + [VM] * (1 + len(pieces)),
        out_specs=(VM, VM),
        compiler_params=params(),
        cost_estimate=cost(4),
        name="norm_events",
    )(
        at,
        gain[None, :],
        *[piece for piece, _ in pieces],
    )


def load_pieces(pieces, firsts, at_ref, base, whole, columns, sems):
    copies = []
    for piece, places in zip(pieces, firsts):
        rows = piece.shape[0] // len(places)
        for block, place in enumerate(places):
            first = pl.multiple_of(place(at_ref), rows)
            copy = pltpu.make_async_copy(
                piece.at[pl.ds(block * rows, rows)],
                whole.at[pl.ds(first, rows), columns],
                sems.at[base + len(copies)],
            )
            copy.start()
            copies.append(copy)
    return copies


def block_count(pieces):
    return sum(len(places) for _, places in pieces)


def encoder_kernel(
    firsts, ratio, at_ref, live_ref, normed_ref, history_ref, *refs
):
    pieces, (out_ref, whole, projected, sems) = refs[:-4], refs[-4:]
    length = normed_ref.shape[0]
    heads = out_ref.shape[1] // DH
    kv_heads = heads // ratio
    query_cols = heads * DH
    key_cols = kv_heads * DH
    past = history_ref.shape[1]
    copies = load_pieces(pieces, firsts, at_ref, 0, whole, slice(None), sems)
    for copy in copies:
        copy.wait()
    tile = min(256, length)
    for row in range(0, length, tile):
        projected[row : row + tile, :] = jnp.dot(
            normed_ref[row : row + tile, :], whole[...], preferred_element_type=jnp.float32
        ).astype(jnp.bfloat16)
    live = live_ref[0] * BLK
    contract = (((1,), (1,)), ((), ()))
    for group in range(kv_heads):
        keys = slice(query_cols + group * DH, query_cols + (group + 1) * DH)
        values = slice(query_cols + key_cols + group * DH, query_cols + key_cols + (group + 1) * DH)
        cached = slice(group * DH, (group + 1) * DH)
        for row in range(0, length, tile):
            reach = row + tile
            for head in range(group * ratio, (group + 1) * ratio):
                query = projected[row:reach, head * DH : (head + 1) * DH]
                old = lax.dot_general(
                    query, history_ref[0, :, cached], contract, preferred_element_type=jnp.float32
                )
                new = lax.dot_general(
                    query, projected[:reach, keys], contract, preferred_element_type=jnp.float32
                )
                query_index = row + lax.broadcasted_iota(jnp.int32, (tile, reach), 0)
                key_index = lax.broadcasted_iota(jnp.int32, (tile, reach), 1)
                new = jnp.where((key_index <= query_index) & (key_index < live), new, -1e30)
                top = jnp.maximum(
                    jnp.max(old, axis=-1, keepdims=True), jnp.max(new, axis=-1, keepdims=True)
                )
                scale = DH ** (-0.5)
                old = jnp.exp((old - top) * scale)
                new = jnp.exp((new - top) * scale)
                total_weight = jnp.sum(old, axis=-1, keepdims=True) + jnp.sum(
                    new, axis=-1, keepdims=True
                )
                mixed = jnp.dot(
                    old.astype(jnp.bfloat16),
                    history_ref[1, :, cached],
                    preferred_element_type=jnp.float32,
                ) + jnp.dot(
                    new.astype(jnp.bfloat16),
                    projected[:reach, values],
                    preferred_element_type=jnp.float32,
                )
                out_ref[row:reach, head * DH : (head + 1) * DH] = (mixed / total_weight).astype(
                    jnp.bfloat16
                )


def encoder_attention(at, normed, history, block_counts, pieces):
    length, width = normed.shape
    key_cols = history.shape[2]
    joined = pieces[0][0].shape[1]
    query_cols = joined - 2 * key_cols
    return pl.pallas_call(
        functools.partial(
            encoder_kernel, [places for _, places in pieces], query_cols // key_cols
        ),
        out_shape=jax.ShapeDtypeStruct((length, query_cols), jnp.bfloat16),
        in_specs=[SM, SM, VM, VM] + [HB] * len(pieces),
        out_specs=VM,
        scratch_shapes=[
            pltpu.VMEM((width, joined), jnp.bfloat16),
            pltpu.VMEM((length, joined), jnp.bfloat16),
            pltpu.SemaphoreType.DMA((block_count(pieces),)),
        ],
        compiler_params=params(),
        cost_estimate=cost(11),
        name="encoder_attention",
    )(
        at,
        block_counts,
        normed,
        history,
        *[piece for piece, _ in pieces],
    )


def project_kernel(firsts, orders, at_ref, attended_ref, *refs):
    count = len(firsts)
    pieces, outs, (whole, sems) = refs[:count], refs[count:-2], refs[-2:]
    copies = load_pieces(pieces, firsts, at_ref, 0, whole, slice(None), sems)
    share = outs[0].shape[0] // len(orders[0])
    for copy in copies:
        copy.wait()
    for index, out_ref in enumerate(outs):
        parts = []
        for where in orders[index]:
            first = pl.multiple_of(where(at_ref) * share, share)
            parts.append(attended_ref[pl.ds(first, share), :])
        rows = jnp.concatenate(parts, axis=0)
        out_ref[...] = lax.dot_general(
            rows, whole[...], (((1,), (1,)), ((), ())), preferred_element_type=jnp.float32
        ).astype(jnp.bfloat16)


def project_out(at, attended, pieces, orders):
    length, cols = attended.shape
    groups = lax.axis_size("tp")
    share = length // (groups * len(orders))
    width = sum(piece.shape[0] for piece, _ in pieces)
    shape = jax.ShapeDtypeStruct((groups * share, width), jnp.bfloat16)
    return pl.pallas_call(
        functools.partial(project_kernel, [first for _, first in pieces], orders),
        out_shape=tuple([shape] * len(orders)),
        in_specs=[SM, VM] + [HB] * len(pieces),
        out_specs=tuple([VM] * len(orders)),
        scratch_shapes=[
            pltpu.VMEM((width, cols), jnp.bfloat16),
            pltpu.SemaphoreType.DMA((block_count(pieces),)),
        ],
        compiler_params=params(),
        cost_estimate=cost(5),
        name="project_out",
    )(
        at,
        attended,
        *[piece for piece, _ in pieces],
    )


def merge_kernel(count, at_ref, gain_ref, source_ref, *refs):
    terms, (encoded_ref, crossed_ref) = refs[:count], refs[count:]
    rows = encoded_ref.shape[0]
    first = pl.multiple_of((at_ref[2] * lax.axis_size("kv") + at_ref[3]) * rows, rows)
    total = source_ref[pl.ds(first, rows), :].astype(jnp.float32)
    for term in terms:
        total = total + term[...].astype(jnp.float32)
    encoded_ref[...] = total.astype(jnp.bfloat16)
    square = jnp.mean(total * total, axis=-1, keepdims=True)
    crossed_ref[...] = (total * lax.rsqrt(square + eps) * gain_ref[...]).astype(jnp.bfloat16)


def merge_terms(at, source, terms, gain):
    shape = jax.ShapeDtypeStruct(terms[0].shape, jnp.bfloat16)
    return pl.pallas_call(
        functools.partial(merge_kernel, len(terms)),
        out_shape=(shape, shape),
        in_specs=[SM] + [VM] * (2 + len(terms)),
        out_specs=(VM, VM),
        compiler_params=params(),
        cost_estimate=cost(3),
        name="merge_terms",
    )(at, gain[None, :], source, *terms)


def cross_kernel(places, firsts, at_ref, *refs):
    row_count, count = len(places), len(firsts)
    rows_refs, pieces = refs[:row_count], refs[row_count : row_count + count]
    out_ref, whole, sems = refs[row_count + count :]
    copies = load_pieces(pieces, firsts, at_ref, 0, whole, slice(None), sems)
    for copy in copies:
        copy.wait()
    rows = rows_refs[0].shape[0]
    for index, rows_ref in enumerate(rows_refs):
        first = pl.multiple_of(places[index](at_ref) * rows, rows)
        out_ref[pl.ds(first, rows), :] = jnp.dot(
            rows_ref[...], whole[...], preferred_element_type=jnp.float32
        ).astype(jnp.bfloat16)


def cross_project(at, row_pieces, pieces):
    width = row_pieces[0][0].shape[1]
    rows = row_pieces[0][0].shape[0]
    cols = pieces[0][0].shape[1]
    return pl.pallas_call(
        functools.partial(
            cross_kernel, [where for _, where in row_pieces], [first for _, first in pieces]
        ),
        out_shape=jax.ShapeDtypeStruct((rows * len(row_pieces), cols), jnp.bfloat16),
        in_specs=[SM] + [VM] * len(row_pieces) + [HB] * len(pieces),
        out_specs=VM,
        scratch_shapes=[
            pltpu.VMEM((width, cols), jnp.bfloat16),
            pltpu.SemaphoreType.DMA((block_count(pieces),)),
        ],
        compiler_params=params(),
        cost_estimate=cost(5),
        name="cross_project",
    )(
        at,
        *[rows for rows, _ in row_pieces],
        *[piece for piece, _ in pieces],
    )


def beam_kernel(
    level, count, last, ratio, places,
    at_ref, live_ref, parent_ref, gain_ref, query_ref, out_weight_ref, cross_ref, code_ref,
    *refs,
):
    inputs, outs, moved = refs[: count + 1 if level else 0], refs[count + 1 if level else 0 : -1], refs[-1]
    beams = code_ref.shape[0]
    code = code_ref[...].astype(jnp.float32)
    if level:
        total = inputs[0][...]
        for term in inputs[1:]:
            total = total + term[...].astype(jnp.float32)
        moved[...] = total
        rows = [moved[pl.ds(parent_ref[level - 1, row], 1), :] for row in range(beams)]
        hidden = jnp.concatenate(rows, axis=0) + code
    else:
        hidden = code
    square = jnp.mean(hidden * hidden, axis=-1, keepdims=True)
    normed = (hidden * lax.rsqrt(square + eps) * gain_ref[...]).astype(jnp.bfloat16)
    queries = jnp.dot(normed, query_ref[...], preferred_element_type=jnp.float32)
    queries = queries.astype(jnp.bfloat16)
    key_cols = cross_ref.shape[1] // 2
    events = cross_ref.shape[0]
    live = live_ref[0] * BLK
    attended = []
    for group in range(key_cols // DH):
        first = group * ratio
        stacked = jnp.concatenate(
            [queries[:, h * DH : (h + 1) * DH] for h in range(first, first + ratio)], axis=0
        )
        scores = lax.dot_general(
            stacked,
            cross_ref[:, group * DH : (group + 1) * DH],
            (((1,), (1,)), ((), ())),
            preferred_element_type=jnp.float32,
        )
        index = lax.broadcasted_iota(jnp.int32, scores.shape, 1)
        scores = jnp.where(index < live, scores, -1e30)
        top = jnp.max(scores, axis=-1, keepdims=True)
        raised = jnp.exp((scores - top) * DH ** (-0.5))
        weight = jnp.sum(raised, axis=-1, keepdims=True)
        mixed = jnp.dot(
            raised.astype(jnp.bfloat16),
            cross_ref[:, key_cols + group * DH : key_cols + (group + 1) * DH],
            preferred_element_type=jnp.float32,
        )
        mixed = (mixed / weight).astype(jnp.bfloat16)
        attended += [mixed[h * beams : (h + 1) * beams, :] for h in range(ratio)]
    terms = jnp.dot(
        jnp.concatenate(attended, axis=1), out_weight_ref[...], preferred_element_type=jnp.float32
    )
    if not last:
        outs[0][...] = hidden
        outs[1][...] = terms.astype(jnp.bfloat16)
    else:
        cols = outs[0].shape[1]
        moved[...] = terms
        for index in range(1, len(outs)):
            col = pl.ds(pl.multiple_of(places[index](at_ref) * cols, cols), cols)
            outs[index][...] = moved[:, col].astype(jnp.bfloat16)
        moved[...] = hidden + terms
        outs[0][...] = moved[:, pl.ds(pl.multiple_of(places[0](at_ref) * cols, cols), cols)]


def beam_step(at, level, live, parents, places, gain, query, out_weight, cross, code, inputs, last):
    beams, width = code.shape
    ratio = H // KVH
    if last:
        cols = width // len(places)
        outs = [jax.ShapeDtypeStruct((beams, cols), jnp.float32)] + [
            jax.ShapeDtypeStruct((beams, cols), jnp.bfloat16)
        ] * (len(places) - 1)
    else:
        outs = [
            jax.ShapeDtypeStruct((beams, width), jnp.float32),
            jax.ShapeDtypeStruct((beams, width), jnp.bfloat16),
        ]
    return pl.pallas_call(
        functools.partial(beam_kernel, level, max(len(inputs) - 1, 0), last, ratio, places),
        out_shape=tuple(outs),
        in_specs=[SM, SM, SM] + [VM] * (5 + len(inputs)),
        out_specs=tuple([VM] * len(outs)),
        scratch_shapes=[pltpu.VMEM((beams, width), jnp.float32)],
        compiler_params=params(),
        cost_estimate=cost(4),
        name=f"beam_step_{level}",
    )(at, live, parents, gain[None, :], query, out_weight, cross, code, *inputs)


def shards(
    events,
    history_cache,
    block_counts,
    semantic_ids,
    beam_parents,
    query_weight,
    keyval_weight,
    out_weight,
    cross_weight,
    decoder_query,
    decoder_out,
    code_table,
    encoder_gain,
    cross_gain,
    decoder_gain,
):
    tp, kv = lax.axis_size("tp"), lax.axis_size("kv")
    my_tp, my_kv = lax.axis_index("tp"), lax.axis_index("kv")
    group, groups = my_tp * kv + my_kv, tp * kv

    at = position()
    joined = jnp.concatenate([query_weight, keyval_weight[0], keyval_weight[1]], axis=1)
    crossing = jnp.concatenate([cross_weight[0], cross_weight[1]], axis=1)
    ringed = lax.axis_size("seq") <= RING_LIMIT
    blocks, firsts = collect_events(events)

    def look_up(waits):
        vocab_rows = code_table.shape[0]
        vocab_ids = group * vocab_rows + lax.broadcasted_iota(jnp.int32, (1, vocab_rows), 1)
        onehot = (semantic_ids.reshape(-1)[:, None] == vocab_ids).astype(jnp.bfloat16)
        onehot = after(onehot, *waits)
        rows = jnp.dot(onehot, code_table, preferred_element_type=jnp.float32).astype(jnp.bfloat16)
        for axis, size in (("kv", kv), ("tp", tp)):
            rows = sum([exchange(rows, axis, step) for step in range(1, size)], rows)
        return rows

    if ringed:
        joined, out, cross = map(Rows, (joined, out_weight, crossing))
        ways = [RING_WAYS[hop % len(RING_WAYS)] for hop in range(lax.axis_size("seq") - 1)]
        joined.hop(ways[0])
        mine = jnp.concatenate(blocks, axis=0)
        mine, joined.last[1] = lax.optimization_barrier((mine, joined.last[1]))
        joined.fresh = [(joined.last[1], 1)]
        stage = [joined.last[1]]
        event_pieces = gather_heads(mine)
        codes, turned = look_up(stage), after(decoder_out, *stage).T
        normed, source = norm_events(at, event_pieces, firsts, encoder_gain)
        for way in ways[1:]:
            joined.swap()
            swapped = joined.swapped()
            joined.hop(way, *stage)
            stage = [joined.last[way], swapped]
        normed, codes, turned, *stage = lax.optimization_barrier((normed, codes, turned, *stage))
        joined.swap(normed)
        out.start(*stage)
        normed, *_ = joined.held(normed, *out.last.values())
        joined_pieces = joined.pieces
        far = [1 + hop // 2 if hop % 2 == 0 else -(1 + hop // 2) for hop in range(len(RING_WAYS), len(ways))]
        out.swap(normed)
        out.end()
        out.keep()
        for distance in far:
            out.direct(distance, normed)
        out_pieces = out.pieces
    else:
        joined_pieces, out_pieces, cross_pieces = map(whole_rows, (joined, out_weight, crossing))
        normed, source = norm_events(at, gather_heads(blocks[0]), firsts, encoder_gain)
        codes = look_up([])
        turned = decoder_out.T
    attended = encoder_attention(
        at, normed, history_cache[:, 0], block_counts, joined_pieces
    )
    steps, beams = semantic_ids.shape
    codes = codes.reshape(steps, beams, codes.shape[1])

    def place(d, e, at):
        return partner(at[2], d, tp) * kv + partner(at[3], e, kv)

    orders = [[functools.partial(place, d, e) for d in range(tp)] for e in range(kv)]
    kept, *sent = project_out(at, attended, out_pieces, orders)
    share = normed.shape[0] // groups
    arrived = [exchange(terms, "kv", e + 1) for e, terms in enumerate(sent)]
    late = []
    if ringed:
        cross.start(*arrived)
        for distance in far:
            cross.direct(distance, *arrived)
        late = list(cross.last.values())

    def summed(d):
        rows = slice(d * share, (d + 1) * share)
        return sum([a[rows].astype(jnp.float32) for a in arrived], kept[rows].astype(jnp.float32))

    terms = [exchange(summed(d).astype(jnp.bfloat16), "tp", d) for d in range(1, tp)]
    terms = [kept[:share]] + [a[:share] for a in arrived] + [after(t, *late) if late else t for t in terms]
    encoded, crossed = merge_terms(at, source, terms, cross_gain)


    def finish_cross():
        cross.swap(crossed)
        cross.end()
        cross.keep()
        return [piece for piece, _ in cross.pieces[1:]]

    crossed_pieces = gather_heads(crossed, finish_cross if ringed else None)
    keys_values = cross_project(at, crossed_pieces, cross.pieces if ringed else cross_pieces)

    places = [functools.partial(place, 0, 0)]
    moves = []
    for d in range(tp):
        for e in range(kv):
            if d or e:
                places.append(functools.partial(place, d, e))
                moves.append(
                    [
                        (a * kv + b, partner(a, d, tp) * kv + partner(b, e, kv))
                        for a in range(tp)
                        for b in range(kv)
                    ]
                )
    inputs = []
    for level in range(steps):
        last = level == steps - 1
        kept, *sent = beam_step(
            at, level, block_counts, beam_parents, places, decoder_gain, decoder_query, turned,
            keys_values, codes[level], inputs, last,
        )
        if not last:
            sent = sent * len(moves)
        arrived = [lax.ppermute(v, ("tp", "kv"), move) for v, move in zip(sent, moves)]
        inputs = [kept] + sent[:1] + arrived
    beam_out = sum([a.astype(jnp.float32) for a in arrived], kept).astype(jnp.bfloat16)
    return (encoded[None], beam_out)


def solution(mesh):
    in_specs = (
        P("groups", "seq", ("tp", "kv")),
        P(None, ("groups", "seq"), None, ("tp", "kv")),
        P(("groups", "seq")),
        P(None, ("groups", "seq")),
        P(None, ("groups", "seq")),
        P("seq", ("tp", "kv")),
        P(None, "seq", ("tp", "kv")),
        P("seq", ("tp", "kv")),
        P(None, "seq", ("tp", "kv")),
        P(None, ("tp", "kv")),
        P(None, ("tp", "kv")),
        P(("tp", "kv"), None),
        P(),
        P(),
        P(),
    )
    out_specs = (P(("groups", "seq"), ("tp", "kv"), None), P(("groups", "seq"), ("tp", "kv")))
    return jax.shard_map(shards, mesh=mesh, in_specs=in_specs, out_specs=out_specs, check_vma=False)
```

```python
import functools

import jax
import jax.numpy as jnp
from jax import lax
from jax.experimental import pallas as pl
from jax.experimental.pallas import tpu as pltpu
from jax.sharding import PartitionSpec as P

H = 16
DH = 128
KVH = 8
BLK = 128
STEPS = 4
RING_LIMIT = 8
RING_WAYS = (1, -1)
VMEM_BYTES = 16 * 1024 * 1024

eps = 1e-06

VM = pl.BlockSpec(memory_space=pltpu.VMEM)
SM = pl.BlockSpec(memory_space=pltpu.SMEM)
HB = pl.BlockSpec(memory_space=pl.ANY)


def params():
    return pltpu.CompilerParams(vmem_limit_bytes=VMEM_BYTES)


def cost(micros):
    return pl.CostEstimate(flops=0, bytes_accessed=int(micros * 3.0e6), transcendentals=0)


def partner(index, step, size):
    if size & (size - 1) == 0:
        return index ^ step
    return (index + step) % size


def origin(index, step, size):
    if size & (size - 1) == 0:
        return index ^ step
    return (index - step) % size


def exchange(value, axis, step):
    size = lax.axis_size(axis)
    return lax.ppermute(value, axis, [(i, partner(i, step, size)) for i in range(size)])


def shift(value, axis, step):
    size = lax.axis_size(axis)
    return lax.ppermute(value, axis, [(i, (i + step) % size) for i in range(size)])


def after(value, *others):
    return lax.optimization_barrier((value, *others))[0]


def position():
    return jnp.stack([lax.axis_index(axis) for axis in ("seq", "groups", "tp", "kv")])


def gather_heads(value, beside=None):
    tp, kv = lax.axis_size("tp"), lax.axis_size("kv")
    along = [(value, lambda at: at[2])]
    for step in range(1, tp):
        along.append(
            (exchange(value, "tp", step), functools.partial(lambda d, at: origin(at[2], d, tp), step))
        )
    waits = beside() if beside else []
    if waits:
        along = along[:1] + [(after(piece, *waits), where) for piece, where in along[1:]]
    pieces = []
    for piece, where in along:
        pieces.append((piece, functools.partial(lambda f, at: f(at) * kv + at[3], where)))
    for piece, where in along:
        for step in range(1, kv):
            pieces.append(
                (
                    exchange(piece, "kv", step),
                    functools.partial(
                        lambda f, e, at: f(at) * kv + origin(at[3], e, kv), where, step
                    ),
                )
            )
    return pieces


class Rows:
    def __init__(self, value, *waits):
        self.size = lax.axis_size("seq")
        self.rows = value.shape[0]
        self.shared = lax.axis_size("groups") == 2 and self.rows % 32 == 0
        self.pieces = [(value, [functools.partial(lambda r, at: at[0] * r, self.rows)])]
        half = self.rows // 2
        if self.shared:
            value = lax.dynamic_slice_in_dim(value, lax.axis_index("groups") * half, half, 0)
        if waits:
            value = after(value, *waits)
        self.last = {1: value, -1: value}
        self.hops = {1: 0, -1: 0}
        self.fresh = []

    def hop(self, way, *waits):
        arrived = shift(after(self.last[way], *waits) if waits else self.last[way], "seq", way)
        self.last[way] = arrived
        self.hops[way] += 1
        self.fresh.append((arrived, way * self.hops[way]))

    def place(self, distance, twin):
        size, rows = self.size, self.rows

        def first(at):
            row = lax.rem(at[0] + size - distance, size) * rows
            return row + (at[1] ^ twin) * (rows // 2) if self.shared else row

        return [first]

    def keep(self):
        for arrived, distance in self.fresh:
            self.pieces.append((arrived, self.place(distance, 0)))
        self.fresh = []

    def swap(self, *waits):
        for arrived, distance in self.fresh:
            self.pieces.append((arrived, self.place(distance, 0)))
            if self.shared:
                other = exchange(after(arrived, *waits) if waits else arrived, "groups", 1)
                self.pieces.append((other, self.place(distance, 1)))
        self.fresh = []

    def direct(self, distance, *waits):
        if self.shared:
            half = self.rows // 2
            rest = 1 - lax.axis_index("groups")
            other = lax.dynamic_slice_in_dim(self.pieces[0][0], rest * half, half, 0)
            other = shift(after(other, *waits) if waits else other, "seq", distance)
            self.pieces.append((other, self.place(distance, 1)))

    def start(self, *waits):
        for way in RING_WAYS[: self.size - 1]:
            self.hop(way, *waits)

    def swapped(self):
        return self.pieces[-1][0]

    def end(self, *waits):
        for hop in range(len(RING_WAYS), self.size - 1):
            self.hop(RING_WAYS[hop % len(RING_WAYS)], *waits)

    def held(self, *waits):
        arrays = lax.optimization_barrier((*[piece for piece, _ in self.pieces], *waits))
        self.pieces = [(piece, places) for piece, (_, places) in zip(arrays, self.pieces)]
        return arrays[len(self.pieces) :]


def whole_rows(value):
    return [(lax.all_gather(value, "seq", axis=0, tiled=True), [lambda at: 0])]


def collect_events(events):
    size = lax.axis_size("seq")
    here = lax.axis_index("seq")
    rows = events.shape[1]
    if size > RING_LIMIT:
        return [lax.all_to_all(events, "seq", split_axis=0, concat_axis=1, tiled=True)[0]], [lambda at: 0]
    blocks = [lax.dynamic_index_in_dim(events, here, 0, False)]
    firsts = [lambda at: at[0] * rows]
    for step in range(1, size):
        block = lax.dynamic_index_in_dim(events, (here + step) % size, 0, False)
        blocks.append(shift(block, "seq", step))
        firsts.append(
            functools.partial(lambda d, at: lax.rem(at[0] + size - d, size) * rows, step)
        )
    return blocks, firsts


def norm_kernel(places, firsts, at_ref, gain_ref, *refs):
    count, blocks = len(places), len(firsts)
    pieces, (normed_ref, source_ref) = refs[:count], refs[count:]
    width = normed_ref.shape[1]
    cols = pieces[0].shape[1]
    rows = pieces[0].shape[0] // blocks
    for block in range(blocks):
        first = pl.multiple_of(firsts[block](at_ref), rows)
        parts = [p[block * rows : (block + 1) * rows, :].astype(jnp.float32) for p in pieces]
        square = sum(jnp.sum(v * v, axis=-1, keepdims=True) for v in parts)
        scale = lax.rsqrt(square / width + eps)
        for index in range(count):
            col = pl.ds(pl.multiple_of(places[index](at_ref) * cols, cols), cols)
            source_ref[pl.ds(first, rows), col] = parts[index].astype(jnp.bfloat16)
            normed_ref[pl.ds(first, rows), col] = (
                parts[index] * scale * gain_ref[:, col]
            ).astype(jnp.bfloat16)


def norm_events(at, pieces, firsts, gain):
    length = pieces[0][0].shape[0]
    width = gain.shape[0]
    shape = jax.ShapeDtypeStruct((length, width), jnp.bfloat16)
    return pl.pallas_call(
        functools.partial(norm_kernel, [where for _, where in pieces], firsts),
        out_shape=(shape, shape),
        in_specs=[SM] + [VM] * (1 + len(pieces)),
        out_specs=(VM, VM),
        compiler_params=params(),
        cost_estimate=cost(4),
        name="norm_events",
    )(
        at,
        gain[None, :],
        *[piece for piece, _ in pieces],
    )


def load_pieces(pieces, firsts, at_ref, base, whole, columns, sems):
    copies = []
    for piece, places in zip(pieces, firsts):
        rows = piece.shape[0] // len(places)
        for block, place in enumerate(places):
            first = pl.multiple_of(place(at_ref), rows)
            copy = pltpu.make_async_copy(
                piece.at[pl.ds(block * rows, rows)],
                whole.at[pl.ds(first, rows), columns],
                sems.at[base + len(copies)],
            )
            copy.start()
            copies.append(copy)
    return copies


def block_count(pieces):
    return sum(len(places) for _, places in pieces)


def encoder_kernel(
    firsts, ratio, at_ref, live_ref, normed_ref, history_ref, *refs
):
    pieces, (out_ref, whole, projected, sems) = refs[:-4], refs[-4:]
    length = normed_ref.shape[0]
    heads = out_ref.shape[1] // DH
    kv_heads = heads // ratio
    query_cols = heads * DH
    key_cols = kv_heads * DH
    past = history_ref.shape[1]
    copies = load_pieces(pieces, firsts, at_ref, 0, whole, slice(None), sems)
    for copy in copies:
        copy.wait()
    tile = min(256, length)
    for row in range(0, length, tile):
        projected[row : row + tile, :] = jnp.dot(
            normed_ref[row : row + tile, :], whole[...], preferred_element_type=jnp.float32
        ).astype(jnp.bfloat16)
    live = live_ref[0] * BLK
    contract = (((1,), (1,)), ((), ()))
    for group in range(kv_heads):
        keys = slice(query_cols + group * DH, query_cols + (group + 1) * DH)
        values = slice(query_cols + key_cols + group * DH, query_cols + key_cols + (group + 1) * DH)
        cached = slice(group * DH, (group + 1) * DH)
        for row in range(0, length, tile):
            reach = row + tile
            for head in range(group * ratio, (group + 1) * ratio):
                query = projected[row:reach, head * DH : (head + 1) * DH]
                old = lax.dot_general(
                    query, history_ref[0, :, cached], contract, preferred_element_type=jnp.float32
                )
                new = lax.dot_general(
                    query, projected[:reach, keys], contract, preferred_element_type=jnp.float32
                )
                query_index = row + lax.broadcasted_iota(jnp.int32, (tile, reach), 0)
                key_index = lax.broadcasted_iota(jnp.int32, (tile, reach), 1)
                new = jnp.where((key_index <= query_index) & (key_index < live), new, -1e30)
                top = jnp.maximum(
                    jnp.max(old, axis=-1, keepdims=True), jnp.max(new, axis=-1, keepdims=True)
                )
                scale = DH ** (-0.5)
                old = jnp.exp((old - top) * scale)
                new = jnp.exp((new - top) * scale)
                total_weight = jnp.sum(old, axis=-1, keepdims=True) + jnp.sum(
                    new, axis=-1, keepdims=True
                )
                mixed = jnp.dot(
                    old.astype(jnp.bfloat16),
                    history_ref[1, :, cached],
                    preferred_element_type=jnp.float32,
                ) + jnp.dot(
                    new.astype(jnp.bfloat16),
                    projected[:reach, values],
                    preferred_element_type=jnp.float32,
                )
                out_ref[row:reach, head * DH : (head + 1) * DH] = (mixed / total_weight).astype(
                    jnp.bfloat16
                )


def encoder_attention(at, normed, history, block_counts, pieces):
    length, width = normed.shape
    key_cols = history.shape[2]
    joined = pieces[0][0].shape[1]
    query_cols = joined - 2 * key_cols
    return pl.pallas_call(
        functools.partial(
            encoder_kernel, [places for _, places in pieces], query_cols // key_cols
        ),
        out_shape=jax.ShapeDtypeStruct((length, query_cols), jnp.bfloat16),
        in_specs=[SM, SM, VM, VM] + [HB] * len(pieces),
        out_specs=VM,
        scratch_shapes=[
            pltpu.VMEM((width, joined), jnp.bfloat16),
            pltpu.VMEM((length, joined), jnp.bfloat16),
            pltpu.SemaphoreType.DMA((block_count(pieces),)),
        ],
        compiler_params=params(),
        cost_estimate=cost(11),
        name="encoder_attention",
    )(
        at,
        block_counts,
        normed,
        history,
        *[piece for piece, _ in pieces],
    )


def project_kernel(firsts, orders, at_ref, attended_ref, *refs):
    count = len(firsts)
    pieces, outs, (whole, sems) = refs[:count], refs[count:-2], refs[-2:]
    copies = load_pieces(pieces, firsts, at_ref, 0, whole, slice(None), sems)
    share = outs[0].shape[0] // len(orders[0])
    for copy in copies:
        copy.wait()
    for index, out_ref in enumerate(outs):
        parts = []
        for where in orders[index]:
            first = pl.multiple_of(where(at_ref) * share, share)
            parts.append(attended_ref[pl.ds(first, share), :])
        rows = jnp.concatenate(parts, axis=0)
        out_ref[...] = lax.dot_general(
            rows, whole[...], (((1,), (1,)), ((), ())), preferred_element_type=jnp.float32
        ).astype(jnp.bfloat16)


def project_out(at, attended, pieces, orders):
    length, cols = attended.shape
    groups = lax.axis_size("tp")
    share = length // (groups * len(orders))
    width = sum(piece.shape[0] for piece, _ in pieces)
    shape = jax.ShapeDtypeStruct((groups * share, width), jnp.bfloat16)
    return pl.pallas_call(
        functools.partial(project_kernel, [first for _, first in pieces], orders),
        out_shape=tuple([shape] * len(orders)),
        in_specs=[SM, VM] + [HB] * len(pieces),
        out_specs=tuple([VM] * len(orders)),
        scratch_shapes=[
            pltpu.VMEM((width, cols), jnp.bfloat16),
            pltpu.SemaphoreType.DMA((block_count(pieces),)),
        ],
        compiler_params=params(),
        cost_estimate=cost(5),
        name="project_out",
    )(
        at,
        attended,
        *[piece for piece, _ in pieces],
    )


def merge_kernel(count, at_ref, gain_ref, source_ref, *refs):
    terms, (encoded_ref, crossed_ref) = refs[:count], refs[count:]
    rows = encoded_ref.shape[0]
    first = pl.multiple_of((at_ref[2] * lax.axis_size("kv") + at_ref[3]) * rows, rows)
    total = source_ref[pl.ds(first, rows), :].astype(jnp.float32)
    for term in terms:
        total = total + term[...].astype(jnp.float32)
    encoded_ref[...] = total.astype(jnp.bfloat16)
    square = jnp.mean(total * total, axis=-1, keepdims=True)
    crossed_ref[...] = (total * lax.rsqrt(square + eps) * gain_ref[...]).astype(jnp.bfloat16)


def merge_terms(at, source, terms, gain):
    shape = jax.ShapeDtypeStruct(terms[0].shape, jnp.bfloat16)
    return pl.pallas_call(
        functools.partial(merge_kernel, len(terms)),
        out_shape=(shape, shape),
        in_specs=[SM] + [VM] * (2 + len(terms)),
        out_specs=(VM, VM),
        compiler_params=params(),
        cost_estimate=cost(3),
        name="merge_terms",
    )(at, gain[None, :], source, *terms)


def cross_kernel(places, firsts, at_ref, *refs):
    row_count, count = len(places), len(firsts)
    rows_refs, pieces = refs[:row_count], refs[row_count : row_count + count]
    out_ref, whole, sems = refs[row_count + count :]
    copies = load_pieces(pieces, firsts, at_ref, 0, whole, slice(None), sems)
    for copy in copies:
        copy.wait()
    rows = rows_refs[0].shape[0]
    for index, rows_ref in enumerate(rows_refs):
        first = pl.multiple_of(places[index](at_ref) * rows, rows)
        out_ref[pl.ds(first, rows), :] = jnp.dot(
            rows_ref[...], whole[...], preferred_element_type=jnp.float32
        ).astype(jnp.bfloat16)


def cross_project(at, row_pieces, pieces):
    width = row_pieces[0][0].shape[1]
    rows = row_pieces[0][0].shape[0]
    cols = pieces[0][0].shape[1]
    return pl.pallas_call(
        functools.partial(
            cross_kernel, [where for _, where in row_pieces], [first for _, first in pieces]
        ),
        out_shape=jax.ShapeDtypeStruct((rows * len(row_pieces), cols), jnp.bfloat16),
        in_specs=[SM] + [VM] * len(row_pieces) + [HB] * len(pieces),
        out_specs=VM,
        scratch_shapes=[
            pltpu.VMEM((width, cols), jnp.bfloat16),
            pltpu.SemaphoreType.DMA((block_count(pieces),)),
        ],
        compiler_params=params(),
        cost_estimate=cost(5),
        name="cross_project",
    )(
        at,
        *[rows for rows, _ in row_pieces],
        *[piece for piece, _ in pieces],
    )


def beam_kernel(
    level, count, last, ratio, places,
    at_ref, live_ref, parent_ref, gain_ref, query_ref, out_weight_ref, cross_ref, code_ref,
    *refs,
):
    inputs, outs, moved = refs[: count + 1 if level else 0], refs[count + 1 if level else 0 : -1], refs[-1]
    beams = code_ref.shape[0]
    code = code_ref[...].astype(jnp.float32)
    if level:
        total = inputs[0][...]
        for term in inputs[1:]:
            total = total + term[...].astype(jnp.float32)
        moved[...] = total
        rows = [moved[pl.ds(parent_ref[level - 1, row], 1), :] for row in range(beams)]
        hidden = jnp.concatenate(rows, axis=0) + code
    else:
        hidden = code
    square = jnp.mean(hidden * hidden, axis=-1, keepdims=True)
    normed = (hidden * lax.rsqrt(square + eps) * gain_ref[...]).astype(jnp.bfloat16)
    queries = jnp.dot(normed, query_ref[...], preferred_element_type=jnp.float32)
    queries = queries.astype(jnp.bfloat16)
    key_cols = cross_ref.shape[1] // 2
    events = cross_ref.shape[0]
    live = live_ref[0] * BLK
    attended = []
    for group in range(key_cols // DH):
        first = group * ratio
        stacked = jnp.concatenate(
            [queries[:, h * DH : (h + 1) * DH] for h in range(first, first + ratio)], axis=0
        )
        scores = lax.dot_general(
            stacked,
            cross_ref[:, group * DH : (group + 1) * DH],
            (((1,), (1,)), ((), ())),
            preferred_element_type=jnp.float32,
        )
        index = lax.broadcasted_iota(jnp.int32, scores.shape, 1)
        scores = jnp.where(index < live, scores, -1e30)
        top = jnp.max(scores, axis=-1, keepdims=True)
        raised = jnp.exp((scores - top) * DH ** (-0.5))
        weight = jnp.sum(raised, axis=-1, keepdims=True)
        mixed = jnp.dot(
            raised.astype(jnp.bfloat16),
            cross_ref[:, key_cols + group * DH : key_cols + (group + 1) * DH],
            preferred_element_type=jnp.float32,
        )
        mixed = (mixed / weight).astype(jnp.bfloat16)
        attended += [mixed[h * beams : (h + 1) * beams, :] for h in range(ratio)]
    terms = jnp.dot(
        jnp.concatenate(attended, axis=1), out_weight_ref[...], preferred_element_type=jnp.float32
    )
    if not last:
        outs[0][...] = hidden
        outs[1][...] = terms.astype(jnp.bfloat16)
    else:
        cols = outs[0].shape[1]
        moved[...] = terms
        for index in range(1, len(outs)):
            col = pl.ds(pl.multiple_of(places[index](at_ref) * cols, cols), cols)
            outs[index][...] = moved[:, col].astype(jnp.bfloat16)
        moved[...] = hidden + terms
        outs[0][...] = moved[:, pl.ds(pl.multiple_of(places[0](at_ref) * cols, cols), cols)]


def beam_step(at, level, live, parents, places, gain, query, out_weight, cross, code, inputs, last):
    beams, width = code.shape
    ratio = H // KVH
    if last:
        cols = width // len(places)
        outs = [jax.ShapeDtypeStruct((beams, cols), jnp.float32)] + [
            jax.ShapeDtypeStruct((beams, cols), jnp.bfloat16)
        ] * (len(places) - 1)
    else:
        outs = [
            jax.ShapeDtypeStruct((beams, width), jnp.float32),
            jax.ShapeDtypeStruct((beams, width), jnp.bfloat16),
        ]
    return pl.pallas_call(
        functools.partial(beam_kernel, level, max(len(inputs) - 1, 0), last, ratio, places),
        out_shape=tuple(outs),
        in_specs=[SM, SM, SM] + [VM] * (5 + len(inputs)),
        out_specs=tuple([VM] * len(outs)),
        scratch_shapes=[pltpu.VMEM((beams, width), jnp.float32)],
        compiler_params=params(),
        cost_estimate=cost(4),
        name=f"beam_step_{level}",
    )(at, live, parents, gain[None, :], query, out_weight, cross, code, *inputs)


def shards(
    events,
    history_cache,
    block_counts,
    semantic_ids,
    beam_parents,
    query_weight,
    keyval_weight,
    out_weight,
    cross_weight,
    decoder_query,
    decoder_out,
    code_table,
    encoder_gain,
    cross_gain,
    decoder_gain,
):
    tp, kv = lax.axis_size("tp"), lax.axis_size("kv")
    my_tp, my_kv = lax.axis_index("tp"), lax.axis_index("kv")
    group, groups = my_tp * kv + my_kv, tp * kv

    at = position()
    joined = jnp.concatenate([query_weight, keyval_weight[0], keyval_weight[1]], axis=1)
    crossing = jnp.concatenate([cross_weight[0], cross_weight[1]], axis=1)
    ringed = lax.axis_size("seq") <= RING_LIMIT
    blocks, firsts = collect_events(events)

    def look_up(waits):
        vocab_rows = code_table.shape[0]
        vocab_ids = group * vocab_rows + lax.broadcasted_iota(jnp.int32, (1, vocab_rows), 1)
        onehot = (semantic_ids.reshape(-1)[:, None] == vocab_ids).astype(jnp.bfloat16)
        onehot = after(onehot, *waits)
        rows = jnp.dot(onehot, code_table, preferred_element_type=jnp.float32).astype(jnp.bfloat16)
        for axis, size in (("kv", kv), ("tp", tp)):
            rows = sum([exchange(rows, axis, step) for step in range(1, size)], rows)
        return rows

    if ringed:
        joined, out, cross = map(Rows, (joined, out_weight, crossing))
        ways = [RING_WAYS[hop % len(RING_WAYS)] for hop in range(lax.axis_size("seq") - 1)]
        joined.hop(ways[0])
        mine = jnp.concatenate(blocks, axis=0)
        mine, joined.last[1] = lax.optimization_barrier((mine, joined.last[1]))
        joined.fresh = [(joined.last[1], 1)]
        stage = [joined.last[1]]
        event_pieces = gather_heads(mine)
        codes, turned = look_up(stage), after(decoder_out, *stage).T
        normed, source = norm_events(at, event_pieces, firsts, encoder_gain)
        for way in ways[1:]:
            joined.swap()
            swapped = joined.swapped()
            joined.hop(way, *stage)
            stage = [joined.last[way], swapped]
        normed, codes, turned, *stage = lax.optimization_barrier((normed, codes, turned, *stage))
        joined.swap(normed)
        out.start(*stage)
        normed, *_ = joined.held(normed, *out.last.values())
        joined_pieces = joined.pieces
        far = [1 + hop // 2 if hop % 2 == 0 else -(1 + hop // 2) for hop in range(len(RING_WAYS), len(ways))]
        out.swap(normed)
        out.end()
        out.keep()
        for distance in far:
            out.direct(distance, normed)
        out_pieces = out.pieces
    else:
        joined_pieces, out_pieces, cross_pieces = map(whole_rows, (joined, out_weight, crossing))
        normed, source = norm_events(at, gather_heads(blocks[0]), firsts, encoder_gain)
        codes = look_up([])
        turned = decoder_out.T
    attended = encoder_attention(
        at, normed, history_cache[:, 0], block_counts, joined_pieces
    )
    steps, beams = semantic_ids.shape
    codes = codes.reshape(steps, beams, codes.shape[1])

    def place(d, e, at):
        return partner(at[2], d, tp) * kv + partner(at[3], e, kv)

    orders = [[functools.partial(place, d, e) for d in range(tp)] for e in range(kv)]
    kept, *sent = project_out(at, attended, out_pieces, orders)
    share = normed.shape[0] // groups
    arrived = [exchange(terms, "kv", e + 1) for e, terms in enumerate(sent)]
    late = []
    if ringed:
        cross.start(*arrived)
        for distance in far:
            cross.direct(distance, *arrived)
        late = list(cross.last.values())

    def summed(d):
        rows = slice(d * share, (d + 1) * share)
        return sum([a[rows].astype(jnp.float32) for a in arrived], kept[rows].astype(jnp.float32))

    terms = [exchange(summed(d).astype(jnp.bfloat16), "tp", d) for d in range(1, tp)]
    terms = [kept[:share]] + [a[:share] for a in arrived] + [after(t, *late) if late else t for t in terms]
    encoded, crossed = merge_terms(at, source, terms, cross_gain)


    def finish_cross():
        cross.swap(crossed)
        cross.end()
        cross.keep()
        return [piece for piece, _ in cross.pieces[1:]]

    crossed_pieces = gather_heads(crossed, finish_cross if ringed else None)
    keys_values = cross_project(at, crossed_pieces, cross.pieces if ringed else cross_pieces)

    places = [functools.partial(place, 0, 0)]
    moves = []
    for d in range(tp):
        for e in range(kv):
            if d or e:
                places.append(functools.partial(place, d, e))
                moves.append(
                    [
                        (a * kv + b, partner(a, d, tp) * kv + partner(b, e, kv))
                        for a in range(tp)
                        for b in range(kv)
                    ]
                )
    inputs = []
    for level in range(steps):
        last = level == steps - 1
        kept, *sent = beam_step(
            at, level, block_counts, beam_parents, places, decoder_gain, decoder_query, turned,
            keys_values, codes[level], inputs, last,
        )
        if not last:
            sent = sent * len(moves)
        arrived = [lax.ppermute(v, ("tp", "kv"), move) for v, move in zip(sent, moves)]
        inputs = [kept] + sent[:1] + arrived
    beam_out = sum([a.astype(jnp.float32) for a in arrived], kept).astype(jnp.bfloat16)
    return (encoded[None], beam_out)


def solution(mesh):
    in_specs = (
        P("groups", "seq", ("tp", "kv")),
        P(None, ("groups", "seq"), None, ("tp", "kv")),
        P(("groups", "seq")),
        P(None, ("groups", "seq")),
        P(None, ("groups", "seq")),
        P("seq", ("tp", "kv")),
        P(None, "seq", ("tp", "kv")),
        P("seq", ("tp", "kv")),
        P(None, "seq", ("tp", "kv")),
        P(None, ("tp", "kv")),
        P(None, ("tp", "kv")),
        P(("tp", "kv"), None),
        P(),
        P(),
        P(),
    )
    out_specs = (P(("groups", "seq"), ("tp", "kv"), None), P(("groups", "seq"), ("tp", "kv")))
    return jax.shard_map(shards, mesh=mesh, in_specs=in_specs, out_specs=out_specs, check_vma=False)
```

```python
import functools

import jax
import jax.numpy as jnp
from jax import lax
from jax.experimental import pallas as pl
from jax.experimental.pallas import tpu as pltpu
from jax.sharding import PartitionSpec as P

H = 16
DH = 128
KVH = 8
BLK = 128
STEPS = 4
RING_LIMIT = 8
RING_WAYS = (1, -1)
VMEM_BYTES = 16 * 1024 * 1024

eps = 1e-06

VM = pl.BlockSpec(memory_space=pltpu.VMEM)
SM = pl.BlockSpec(memory_space=pltpu.SMEM)
HB = pl.BlockSpec(memory_space=pl.ANY)


def params():
    return pltpu.CompilerParams(vmem_limit_bytes=VMEM_BYTES)


def cost(micros):
    return pl.CostEstimate(flops=0, bytes_accessed=int(micros * 3.0e6), transcendentals=0)


def partner(index, step, size):
    if size & (size - 1) == 0:
        return index ^ step
    return (index + step) % size


def origin(index, step, size):
    if size & (size - 1) == 0:
        return index ^ step
    return (index - step) % size


def exchange(value, axis, step):
    size = lax.axis_size(axis)
    return lax.ppermute(value, axis, [(i, partner(i, step, size)) for i in range(size)])


def shift(value, axis, step):
    size = lax.axis_size(axis)
    return lax.ppermute(value, axis, [(i, (i + step) % size) for i in range(size)])


def after(value, *others):
    return lax.optimization_barrier((value, *others))[0]


def position():
    return jnp.stack([lax.axis_index(axis) for axis in ("seq", "groups", "tp", "kv")])


def gather_heads(value, waits=()):
    tp, kv = lax.axis_size("tp"), lax.axis_size("kv")
    along = [(value, lambda at: at[2])]
    for step in range(1, tp):
        along.append(
            (exchange(value, "tp", step), functools.partial(lambda d, at: origin(at[2], d, tp), step))
        )
    if waits:
        along = along[:1] + [(after(piece, *waits), where) for piece, where in along[1:]]
    pieces = []
    for piece, where in along:
        pieces.append((piece, functools.partial(lambda f, at: f(at) * kv + at[3], where)))
    for piece, where in along:
        for step in range(1, kv):
            pieces.append(
                (
                    exchange(piece, "kv", step),
                    functools.partial(
                        lambda f, e, at: f(at) * kv + origin(at[3], e, kv), where, step
                    ),
                )
            )
    return pieces


class Rows:
    def __init__(self, value, *waits):
        self.size = lax.axis_size("seq")
        self.rows = value.shape[0]
        self.shared = lax.axis_size("groups") == 2 and self.rows % 32 == 0
        self.pieces = [(value, [functools.partial(lambda r, at: at[0] * r, self.rows)])]
        half = self.rows // 2
        if self.shared:
            value = lax.dynamic_slice_in_dim(value, lax.axis_index("groups") * half, half, 0)
        if waits:
            value = after(value, *waits)
        self.last = {1: value, -1: value}
        self.hops = {1: 0, -1: 0}
        self.fresh = []

    def hop(self, way, *waits):
        arrived = shift(after(self.last[way], *waits) if waits else self.last[way], "seq", way)
        self.last[way] = arrived
        self.hops[way] += 1
        self.fresh.append((arrived, way * self.hops[way]))

    def place(self, distance, twin):
        size, rows = self.size, self.rows

        def first(at):
            row = lax.rem(at[0] + size - distance, size) * rows
            return row + (at[1] ^ twin) * (rows // 2) if self.shared else row

        return [first]

    def keep(self):
        for arrived, distance in self.fresh:
            self.pieces.append((arrived, self.place(distance, 0)))
        self.fresh = []

    def swap(self, *waits):
        for arrived, distance in self.fresh:
            self.pieces.append((arrived, self.place(distance, 0)))
            if self.shared:
                other = exchange(after(arrived, *waits) if waits else arrived, "groups", 1)
                self.pieces.append((other, self.place(distance, 1)))
        self.fresh = []

    def direct(self, distance, *waits):
        if self.shared:
            half = self.rows // 2
            rest = 1 - lax.axis_index("groups")
            other = lax.dynamic_slice_in_dim(self.pieces[0][0], rest * half, half, 0)
            other = shift(after(other, *waits) if waits else other, "seq", distance)
            self.pieces.append((other, self.place(distance, 1)))

    def start(self, *waits):
        for way in RING_WAYS[: self.size - 1]:
            self.hop(way, *waits)

    def swapped(self):
        return self.pieces[-1][0]

    def end(self, *waits):
        for hop in range(len(RING_WAYS), self.size - 1):
            self.hop(RING_WAYS[hop % len(RING_WAYS)], *waits)

    def held(self, *waits):
        arrays = lax.optimization_barrier((*[piece for piece, _ in self.pieces], *waits))
        self.pieces = [(piece, places) for piece, (_, places) in zip(arrays, self.pieces)]
        return arrays[len(self.pieces) :]


def whole_rows(value):
    return [(lax.all_gather(value, "seq", axis=0, tiled=True), [lambda at: 0])]


def collect_events(events):
    size = lax.axis_size("seq")
    here = lax.axis_index("seq")
    rows = events.shape[1]
    if size > RING_LIMIT:
        return [lax.all_to_all(events, "seq", split_axis=0, concat_axis=1, tiled=True)[0]], [lambda at: 0]
    blocks = [lax.dynamic_index_in_dim(events, here, 0, False)]
    firsts = [lambda at: at[0] * rows]
    for step in range(1, size):
        block = lax.dynamic_index_in_dim(events, (here + step) % size, 0, False)
        blocks.append(shift(block, "seq", step))
        firsts.append(
            functools.partial(lambda d, at: lax.rem(at[0] + size - d, size) * rows, step)
        )
    return blocks, firsts


def norm_kernel(places, firsts, at_ref, gain_ref, *refs):
    count, blocks = len(places), len(firsts)
    pieces, (normed_ref, share_ref, source_ref) = refs[:count], refs[count:]
    width = normed_ref.shape[1]
    cols = pieces[0].shape[1]
    rows = pieces[0].shape[0] // blocks
    for block in range(blocks):
        first = pl.multiple_of(firsts[block](at_ref), rows)
        parts = [p[block * rows : (block + 1) * rows, :].astype(jnp.float32) for p in pieces]
        square = sum(jnp.sum(v * v, axis=-1, keepdims=True) for v in parts)
        scale = lax.rsqrt(square / width + eps)
        for index in range(count):
            col = pl.ds(pl.multiple_of(places[index](at_ref) * cols, cols), cols)
            source_ref[pl.ds(first, rows), col] = parts[index].astype(jnp.bfloat16)
            normed_ref[pl.ds(first, rows), col] = (
                parts[index] * scale * gain_ref[:, col]
            ).astype(jnp.bfloat16)
    mine = share_ref.shape[0]
    first = pl.multiple_of((at_ref[2] * lax.axis_size("kv") + at_ref[3]) * mine, mine)
    share_ref[...] = source_ref[pl.ds(first, mine), :]


def norm_events(at, pieces, firsts, gain):
    length = pieces[0][0].shape[0]
    width = gain.shape[0]
    mine = length // (lax.axis_size("tp") * lax.axis_size("kv"))
    return pl.pallas_call(
        functools.partial(norm_kernel, [where for _, where in pieces], firsts),
        out_shape=(
            jax.ShapeDtypeStruct((length, width), jnp.bfloat16),
            jax.ShapeDtypeStruct((mine, width), jnp.bfloat16),
        ),
        in_specs=[SM] + [VM] * (1 + len(pieces)),
        out_specs=(VM, VM),
        scratch_shapes=[pltpu.VMEM((length, width), jnp.bfloat16)],
        compiler_params=params(),
        cost_estimate=cost(4),
        name="norm_events",
    )(
        at,
        gain[None, :],
        *[piece for piece, _ in pieces],
    )


def load_pieces(pieces, firsts, at_ref, base, whole, columns, sems):
    copies = []
    for piece, places in zip(pieces, firsts):
        rows = piece.shape[0] // len(places)
        for block, place in enumerate(places):
            first = pl.multiple_of(place(at_ref), rows)
            copy = pltpu.make_async_copy(
                piece.at[pl.ds(block * rows, rows)],
                whole.at[pl.ds(first, rows), columns],
                sems.at[base + len(copies)],
            )
            copy.start()
            copies.append(copy)
    return copies


def block_count(pieces):
    return sum(len(places) for _, places in pieces)


def encoder_kernel(
    firsts, ratio, at_ref, live_ref, rows_ref, cache_ref, *refs
):
    pieces, (out_ref, whole, projected, normed_ref, history_ref, sems) = refs[:-6], refs[-6:]
    length = rows_ref.shape[0]
    heads = out_ref.shape[1] // DH
    kv_heads = heads // ratio
    query_cols = heads * DH
    key_cols = kv_heads * DH
    past = history_ref.shape[1]
    spare = sems.shape[0] - 2
    early = pltpu.make_async_copy(rows_ref, normed_ref, sems.at[spare])
    later = pltpu.make_async_copy(cache_ref, history_ref, sems.at[spare + 1])
    early.start()
    copies = load_pieces(pieces, firsts, at_ref, 0, whole, slice(None), sems)
    later.start()
    for copy in copies:
        copy.wait()
    early.wait()
    tile = min(256, length)
    for row in range(0, length, tile):
        projected[row : row + tile, :] = jnp.dot(
            normed_ref[row : row + tile, :], whole[...], preferred_element_type=jnp.float32
        ).astype(jnp.bfloat16)
    later.wait()
    live = live_ref[0] * BLK
    contract = (((1,), (1,)), ((), ()))
    for group in range(kv_heads):
        keys = slice(query_cols + group * DH, query_cols + (group + 1) * DH)
        values = slice(query_cols + key_cols + group * DH, query_cols + key_cols + (group + 1) * DH)
        cached = slice(group * DH, (group + 1) * DH)
        for row in range(0, length, tile):
            reach = row + tile
            for head in range(group * ratio, (group + 1) * ratio):
                query = projected[row:reach, head * DH : (head + 1) * DH]
                old = lax.dot_general(
                    query, history_ref[0, :, cached], contract, preferred_element_type=jnp.float32
                )
                new = lax.dot_general(
                    query, projected[:reach, keys], contract, preferred_element_type=jnp.float32
                )
                query_index = row + lax.broadcasted_iota(jnp.int32, (tile, reach), 0)
                key_index = lax.broadcasted_iota(jnp.int32, (tile, reach), 1)
                new = jnp.where((key_index <= query_index) & (key_index < live), new, -1e30)
                top = jnp.maximum(
                    jnp.max(old, axis=-1, keepdims=True), jnp.max(new, axis=-1, keepdims=True)
                )
                scale = DH ** (-0.5)
                old = jnp.exp((old - top) * scale)
                new = jnp.exp((new - top) * scale)
                total_weight = jnp.sum(old, axis=-1, keepdims=True) + jnp.sum(
                    new, axis=-1, keepdims=True
                )
                mixed = jnp.dot(
                    old.astype(jnp.bfloat16),
                    history_ref[1, :, cached],
                    preferred_element_type=jnp.float32,
                ) + jnp.dot(
                    new.astype(jnp.bfloat16),
                    projected[:reach, values],
                    preferred_element_type=jnp.float32,
                )
                out_ref[row:reach, head * DH : (head + 1) * DH] = (mixed / total_weight).astype(
                    jnp.bfloat16
                )


def encoder_attention(at, normed, history, block_counts, pieces):
    length, width = normed.shape
    key_cols = history.shape[2]
    joined = pieces[0][0].shape[1]
    query_cols = joined - 2 * key_cols
    return pl.pallas_call(
        functools.partial(
            encoder_kernel, [places for _, places in pieces], query_cols // key_cols
        ),
        out_shape=jax.ShapeDtypeStruct((length, query_cols), jnp.bfloat16),
        in_specs=[SM, SM, HB, HB] + [HB] * len(pieces),
        out_specs=VM,
        scratch_shapes=[
            pltpu.VMEM((width, joined), jnp.bfloat16),
            pltpu.VMEM((length, joined), jnp.bfloat16),
            pltpu.VMEM((length, width), jnp.bfloat16),
            pltpu.VMEM(history.shape, jnp.bfloat16),
            pltpu.SemaphoreType.DMA((block_count(pieces) + 2,)),
        ],
        compiler_params=params(),
        cost_estimate=cost(11),
        name="encoder_attention",
    )(
        at,
        block_counts,
        normed,
        history,
        *[piece for piece, _ in pieces],
    )


def project_kernel(firsts, orders, at_ref, attended_ref, *refs):
    count = len(firsts)
    pieces, outs, (whole, sems) = refs[:count], refs[count:-2], refs[-2:]
    copies = load_pieces(pieces, firsts, at_ref, 0, whole, slice(None), sems)
    share = outs[0].shape[0] // len(orders[0])
    for copy in copies:
        copy.wait()
    for index, out_ref in enumerate(outs):
        parts = []
        for where in orders[index]:
            first = pl.multiple_of(where(at_ref) * share, share)
            parts.append(attended_ref[pl.ds(first, share), :])
        rows = jnp.concatenate(parts, axis=0)
        out_ref[...] = lax.dot_general(
            rows, whole[...], (((1,), (1,)), ((), ())), preferred_element_type=jnp.float32
        ).astype(jnp.bfloat16)


def project_out(at, attended, pieces, orders):
    length, cols = attended.shape
    groups = lax.axis_size("tp")
    share = length // (groups * len(orders))
    width = sum(piece.shape[0] for piece, _ in pieces)
    shape = jax.ShapeDtypeStruct((groups * share, width), jnp.bfloat16)
    return pl.pallas_call(
        functools.partial(project_kernel, [first for _, first in pieces], orders),
        out_shape=tuple([shape] * len(orders)),
        in_specs=[SM, VM] + [HB] * len(pieces),
        out_specs=tuple([VM] * len(orders)),
        scratch_shapes=[
            pltpu.VMEM((width, cols), jnp.bfloat16),
            pltpu.SemaphoreType.DMA((block_count(pieces),)),
        ],
        compiler_params=params(),
        cost_estimate=cost(5),
        name="project_out",
    )(
        at,
        attended,
        *[piece for piece, _ in pieces],
    )


def merge_kernel(first, gain_ref, source_ref, *refs):
    near, (far, encoded_ref, crossed_ref) = refs[:-3], refs[-3:]
    rows = slice(first, first + encoded_ref.shape[0])
    total = source_ref[rows, :].astype(jnp.float32)
    for term in near:
        total = total + term[rows, :].astype(jnp.float32)
    for term in range(far.shape[0]):
        total = total + far[term].astype(jnp.float32)
    encoded_ref[...] = total.astype(jnp.bfloat16)
    square = jnp.mean(total * total, axis=-1, keepdims=True)
    crossed_ref[...] = (total * lax.rsqrt(square + eps) * gain_ref[...]).astype(jnp.bfloat16)


def merge_terms(first, source, near, far, gain):
    shape = jax.ShapeDtypeStruct(far.shape[1:], jnp.bfloat16)
    return pl.pallas_call(
        functools.partial(merge_kernel, first),
        out_shape=(shape, shape),
        in_specs=[VM] * (3 + len(near)),
        out_specs=(VM, VM),
        compiler_params=params(),
        cost_estimate=cost(1),
        name=f"merge_terms_{first}",
    )(gain[None, :], source, *near, far)


def cross_kernel(places, firsts, at_ref, *refs):
    count = len(places)
    pieces, (out_ref, source, whole, sems) = refs[:-4], refs[-4:]
    copies = load_pieces(pieces[count:], firsts, at_ref, 0, whole, slice(None), sems)
    copies += load_pieces(pieces[:count], places, at_ref, len(copies), source, slice(None), sems)
    for copy in copies:
        copy.wait()
    tile = min(256, out_ref.shape[0])
    for row in range(0, out_ref.shape[0], tile):
        out_ref[row : row + tile, :] = jnp.dot(
            source[row : row + tile, :], whole[...], preferred_element_type=jnp.float32
        ).astype(jnp.bfloat16)


def cross_project(at, row_pieces, pieces):
    width = row_pieces[0][0].shape[1]
    length = sum(rows.shape[0] for rows, _ in row_pieces)
    cols = pieces[0][0].shape[1]
    return pl.pallas_call(
        functools.partial(
            cross_kernel, [places for _, places in row_pieces], [places for _, places in pieces]
        ),
        out_shape=jax.ShapeDtypeStruct((length, cols), jnp.bfloat16),
        in_specs=[SM] + [HB] * (len(row_pieces) + len(pieces)),
        out_specs=VM,
        scratch_shapes=[
            pltpu.VMEM((length, width), jnp.bfloat16),
            pltpu.VMEM((width, cols), jnp.bfloat16),
            pltpu.SemaphoreType.DMA((block_count(row_pieces) + block_count(pieces),)),
        ],
        compiler_params=params(),
        cost_estimate=cost(2),
        name="cross_project",
    )(at, *[rows for rows, _ in row_pieces], *[piece for piece, _ in pieces])


def beam_kernel(
    level, count, last, ratio, places,
    at_ref, live_ref, parent_ref, gain_ref, query_ref, out_weight_ref, cross_ref, code_ref,
    *refs,
):
    inputs, outs, moved = refs[: count + 1 if level else 0], refs[count + 1 if level else 0 : -1], refs[-1]
    beams = code_ref.shape[0]
    code = code_ref[...].astype(jnp.float32)
    if level:
        total = inputs[0][...]
        for term in inputs[1:]:
            total = total + term[...].astype(jnp.float32)
        moved[...] = total
        rows = [moved[pl.ds(parent_ref[level - 1, row], 1), :] for row in range(beams)]
        hidden = jnp.concatenate(rows, axis=0) + code
    else:
        hidden = code
    square = jnp.mean(hidden * hidden, axis=-1, keepdims=True)
    normed = (hidden * lax.rsqrt(square + eps) * gain_ref[...]).astype(jnp.bfloat16)
    queries = jnp.dot(normed, query_ref[...], preferred_element_type=jnp.float32)
    queries = queries.astype(jnp.bfloat16)
    key_cols = cross_ref.shape[1] // 2
    events = cross_ref.shape[0]
    live = live_ref[0] * BLK
    attended = []
    for group in range(key_cols // DH):
        first = group * ratio
        stacked = jnp.concatenate(
            [queries[:, h * DH : (h + 1) * DH] for h in range(first, first + ratio)], axis=0
        )
        scores = lax.dot_general(
            stacked,
            cross_ref[:, group * DH : (group + 1) * DH],
            (((1,), (1,)), ((), ())),
            preferred_element_type=jnp.float32,
        )
        index = lax.broadcasted_iota(jnp.int32, scores.shape, 1)
        scores = jnp.where(index < live, scores, -1e30)
        top = jnp.max(scores, axis=-1, keepdims=True)
        raised = jnp.exp((scores - top) * DH ** (-0.5))
        weight = jnp.sum(raised, axis=-1, keepdims=True)
        mixed = jnp.dot(
            raised.astype(jnp.bfloat16),
            cross_ref[:, key_cols + group * DH : key_cols + (group + 1) * DH],
            preferred_element_type=jnp.float32,
        )
        mixed = (mixed / weight).astype(jnp.bfloat16)
        attended += [mixed[h * beams : (h + 1) * beams, :] for h in range(ratio)]
    terms = jnp.dot(
        jnp.concatenate(attended, axis=1), out_weight_ref[...], preferred_element_type=jnp.float32
    )
    if not last:
        outs[0][...] = hidden
        outs[1][...] = terms.astype(jnp.bfloat16)
    else:
        cols = outs[0].shape[1]
        moved[...] = terms
        for index in range(1, len(outs)):
            col = pl.ds(pl.multiple_of(places[index](at_ref) * cols, cols), cols)
            outs[index][...] = moved[:, col].astype(jnp.bfloat16)
        moved[...] = hidden + terms
        outs[0][...] = moved[:, pl.ds(pl.multiple_of(places[0](at_ref) * cols, cols), cols)]


def beam_step(at, level, live, parents, places, gain, query, out_weight, cross, code, inputs, last):
    beams, width = code.shape
    ratio = H // KVH
    if last:
        cols = width // len(places)
        outs = [jax.ShapeDtypeStruct((beams, cols), jnp.float32)] + [
            jax.ShapeDtypeStruct((beams, cols), jnp.bfloat16)
        ] * (len(places) - 1)
    else:
        outs = [
            jax.ShapeDtypeStruct((beams, width), jnp.float32),
            jax.ShapeDtypeStruct((beams, width), jnp.bfloat16),
        ]
    return pl.pallas_call(
        functools.partial(beam_kernel, level, max(len(inputs) - 1, 0), last, ratio, places),
        out_shape=tuple(outs),
        in_specs=[SM, SM, SM] + [VM] * (5 + len(inputs)),
        out_specs=tuple([VM] * len(outs)),
        scratch_shapes=[pltpu.VMEM((beams, width), jnp.float32)],
        compiler_params=params(),
        cost_estimate=cost(4),
        name=f"beam_step_{level}",
    )(at, live, parents, gain[None, :], query, out_weight, cross, code, *inputs)


def shards(
    events,
    history_cache,
    block_counts,
    semantic_ids,
    beam_parents,
    query_weight,
    keyval_weight,
    out_weight,
    cross_weight,
    decoder_query,
    decoder_out,
    code_table,
    encoder_gain,
    cross_gain,
    decoder_gain,
):
    tp, kv = lax.axis_size("tp"), lax.axis_size("kv")
    my_tp, my_kv = lax.axis_index("tp"), lax.axis_index("kv")
    group, groups = my_tp * kv + my_kv, tp * kv

    at = position()
    joined = jnp.concatenate([query_weight, keyval_weight[0], keyval_weight[1]], axis=1)
    crossing = jnp.concatenate([cross_weight[0], cross_weight[1]], axis=1)
    ringed = lax.axis_size("seq") <= RING_LIMIT
    blocks, firsts = collect_events(events)

    def look_up(waits):
        vocab_rows = code_table.shape[0]
        vocab_ids = group * vocab_rows + lax.broadcasted_iota(jnp.int32, (1, vocab_rows), 1)
        onehot = (semantic_ids.reshape(-1)[:, None] == vocab_ids).astype(jnp.bfloat16)
        onehot = after(onehot, *waits)
        rows = jnp.dot(onehot, code_table, preferred_element_type=jnp.float32).astype(jnp.bfloat16)
        for axis, size in (("kv", kv), ("tp", tp)):
            rows = sum([exchange(rows, axis, step) for step in range(1, size)], rows)
        return rows

    if ringed:
        joined, out, cross = map(Rows, (joined, out_weight, crossing))
        ways = [RING_WAYS[hop % len(RING_WAYS)] for hop in range(lax.axis_size("seq") - 1)]
        joined.hop(ways[0])
        blocks[1], joined.last[1] = lax.optimization_barrier((blocks[1], joined.last[1]))
        mine = jnp.concatenate(blocks, axis=0)
        joined.fresh = [(joined.last[1], 1)]
        stage = [joined.last[1]]
        event_pieces = gather_heads(mine)
        codes, turned = look_up(stage), after(decoder_out, *stage).T
        normed, source = norm_events(at, event_pieces, firsts, encoder_gain)
        for way in ways[1:]:
            joined.swap()
            swapped = joined.swapped()
            joined.hop(way, *stage)
            stage = [joined.last[way], swapped]
        normed, codes, turned, *stage = lax.optimization_barrier((normed, codes, turned, *stage))
        joined.swap(normed)
        out.start(*stage)
        normed, *_ = joined.held(normed, *out.last.values())
        joined_pieces = joined.pieces
        out.swap(normed)
        out.end()
        cross.start(normed)
    else:
        joined_pieces, out_pieces, cross_pieces = map(whole_rows, (joined, out_weight, crossing))
        normed, source = norm_events(at, gather_heads(blocks[0]), firsts, encoder_gain)
        codes = look_up([])
        turned = decoder_out.T
    attended = encoder_attention(
        at, normed, history_cache[:, 0], block_counts, joined_pieces
    )
    if ringed:
        out.swap(attended)
        out_pieces = out.pieces
        attended, *_ = lax.optimization_barrier((attended, *cross.last.values()))
    steps, beams = semantic_ids.shape
    codes = codes.reshape(steps, beams, codes.shape[1])

    def place(d, e, at):
        return partner(at[2], d, tp) * kv + partner(at[3], e, kv)

    orders = [[functools.partial(place, d, e) for d in range(tp)] for e in range(kv)]
    kept, *sent = project_out(at, attended, out_pieces, orders)
    share = normed.shape[0] // groups
    arrived = [exchange(terms, "kv", e + 1) for e, terms in enumerate(sent)]
    late = []
    if ringed:
        cross.swap(attended)
        cross.end(attended)
        late = [piece for piece, _ in cross.pieces[1:]] + list(cross.last.values())

    parts = 2 if share % 32 == 0 else 1
    part = share // parts

    def summed(d, first):
        rows = slice(d * share + first, d * share + first + part)
        return sum([a[rows].astype(jnp.float32) for a in arrived], kept[rows].astype(jnp.float32))

    far = [
        [exchange(summed(d, first).astype(jnp.bfloat16), "tp", d) for d in range(1, tp)]
        for first in range(0, share, part)
    ]
    merged = [
        merge_terms(index * part, source, [kept, *arrived], jnp.stack(terms), cross_gain)
        for index, terms in enumerate(far)
    ]
    encoded = jnp.concatenate([encoded for encoded, _ in merged], axis=0)
    if ringed:
        cross.swap(merged[-1][1])
        cross_pieces = cross.pieces
    crossed_pieces = []
    for index, (_, crossed) in enumerate(merged):
        waits = late if index == 0 else []
        if ringed and index == parts - 1:
            waits = [*waits, cross_pieces[-1][0]]
        for rows, where in gather_heads(crossed, waits):
            crossed_pieces.append(
                (rows, [functools.partial(lambda f, i, at: f(at) * share + i, where, index * part)])
            )
    keys_values = cross_project(at, crossed_pieces, cross_pieces)

    places = [functools.partial(place, 0, 0)]
    moves = []
    for d in range(tp):
        for e in range(kv):
            if d or e:
                places.append(functools.partial(place, d, e))
                moves.append(
                    [
                        (a * kv + b, partner(a, d, tp) * kv + partner(b, e, kv))
                        for a in range(tp)
                        for b in range(kv)
                    ]
                )
    inputs = []
    for level in range(steps):
        last = level == steps - 1
        kept, *sent = beam_step(
            at, level, block_counts, beam_parents, places, decoder_gain, decoder_query, turned,
            keys_values, codes[level], inputs, last,
        )
        if not last:
            sent = sent * len(moves)
        arrived = [lax.ppermute(v, ("tp", "kv"), move) for v, move in zip(sent, moves)]
        inputs = [kept] + sent[:1] + arrived
    beam_out = sum([a.astype(jnp.float32) for a in arrived], kept).astype(jnp.bfloat16)
    return (encoded[None], beam_out)


def solution(mesh):
    in_specs = (
        P("groups", "seq", ("tp", "kv")),
        P(None, ("groups", "seq"), None, ("tp", "kv")),
        P(("groups", "seq")),
        P(None, ("groups", "seq")),
        P(None, ("groups", "seq")),
        P("seq", ("tp", "kv")),
        P(None, "seq", ("tp", "kv")),
        P("seq", ("tp", "kv")),
        P(None, "seq", ("tp", "kv")),
        P(None, ("tp", "kv")),
        P(None, ("tp", "kv")),
        P(("tp", "kv"), None),
        P(),
        P(),
        P(),
    )
    out_specs = (P(("groups", "seq"), ("tp", "kv"), None), P(("groups", "seq"), ("tp", "kv")))
    return jax.shard_map(shards, mesh=mesh, in_specs=in_specs, out_specs=out_specs, check_vma=False)
```

```python
import functools

import jax
import jax.numpy as jnp
from jax import lax
from jax.experimental import pallas as pl
from jax.experimental.pallas import tpu as pltpu
from jax.sharding import PartitionSpec as P

H = 16
DH = 128
KVH = 8
BLK = 128
STEPS = 4
RING_LIMIT = 8
RING_WAYS = (1, -1)
VMEM_BYTES = 16 * 1024 * 1024

eps = 1e-06

VM = pl.BlockSpec(memory_space=pltpu.VMEM)
SM = pl.BlockSpec(memory_space=pltpu.SMEM)
HB = pl.BlockSpec(memory_space=pl.ANY)


def params():
    return pltpu.CompilerParams(vmem_limit_bytes=VMEM_BYTES)


def cost(micros):
    return pl.CostEstimate(flops=0, bytes_accessed=int(micros * 3.0e6), transcendentals=0)


def partner(index, step, size):
    if size & (size - 1) == 0:
        return index ^ step
    return (index + step) % size


def origin(index, step, size):
    if size & (size - 1) == 0:
        return index ^ step
    return (index - step) % size


def exchange(value, axis, step):
    size = lax.axis_size(axis)
    return lax.ppermute(value, axis, [(i, partner(i, step, size)) for i in range(size)])


def shift(value, axis, step):
    size = lax.axis_size(axis)
    return lax.ppermute(value, axis, [(i, (i + step) % size) for i in range(size)])


def after(value, *others):
    return lax.optimization_barrier((value, *others))[0]


def position():
    return jnp.stack([lax.axis_index(axis) for axis in ("seq", "groups", "tp", "kv")])


def gather_heads(value, waits=()):
    tp, kv = lax.axis_size("tp"), lax.axis_size("kv")
    along = [(value, lambda at: at[2])]
    for step in range(1, tp):
        along.append(
            (exchange(value, "tp", step), functools.partial(lambda d, at: origin(at[2], d, tp), step))
        )
    if waits:
        along = along[:1] + [(after(piece, *waits), where) for piece, where in along[1:]]
    pieces = []
    for piece, where in along:
        pieces.append((piece, functools.partial(lambda f, at: f(at) * kv + at[3], where)))
    for piece, where in along:
        for step in range(1, kv):
            pieces.append(
                (
                    exchange(piece, "kv", step),
                    functools.partial(
                        lambda f, e, at: f(at) * kv + origin(at[3], e, kv), where, step
                    ),
                )
            )
    return pieces


class Rows:
    def __init__(self, columns):
        columns = columns if isinstance(columns, list) else [columns]
        value = jnp.concatenate(columns, axis=1)
        self.size = lax.axis_size("seq")
        self.rows = value.shape[0]
        self.shared = lax.axis_size("groups") == 2 and self.rows % 32 == 0
        self.pieces = [(value, [functools.partial(lambda r, at: at[0] * r, self.rows)])]
        half = self.rows // 2
        if self.shared:
            first = lax.axis_index("groups") * half
            columns = [lax.dynamic_slice_in_dim(column, first, half, 0) for column in columns]
            value = jnp.concatenate(columns, axis=1)
        self.last = {1: value, -1: value}
        self.hops = {1: 0, -1: 0}
        self.fresh = []

    def hop(self, way, *waits):
        arrived = shift(after(self.last[way], *waits) if waits else self.last[way], "seq", way)
        self.last[way] = arrived
        self.hops[way] += 1
        self.fresh.append((arrived, way * self.hops[way]))

    def place(self, distance, twin):
        size, rows = self.size, self.rows

        def first(at):
            row = lax.rem(at[0] + size - distance, size) * rows
            return row + (at[1] ^ twin) * (rows // 2) if self.shared else row

        return [first]

    def keep(self):
        for arrived, distance in self.fresh:
            self.pieces.append((arrived, self.place(distance, 0)))
        self.fresh = []

    def swap(self, *waits):
        for arrived, distance in self.fresh:
            self.pieces.append((arrived, self.place(distance, 0)))
            if self.shared:
                other = exchange(after(arrived, *waits) if waits else arrived, "groups", 1)
                self.pieces.append((other, self.place(distance, 1)))
        self.fresh = []

    def direct(self, distance, *waits):
        if self.shared:
            half = self.rows // 2
            rest = 1 - lax.axis_index("groups")
            other = lax.dynamic_slice_in_dim(self.pieces[0][0], rest * half, half, 0)
            other = shift(after(other, *waits) if waits else other, "seq", distance)
            self.pieces.append((other, self.place(distance, 1)))

    def start(self, *waits):
        for way in RING_WAYS[: self.size - 1]:
            self.hop(way, *waits)

    def swapped(self):
        return self.pieces[-1][0]

    def end(self, *waits):
        for hop in range(len(RING_WAYS), self.size - 1):
            self.hop(RING_WAYS[hop % len(RING_WAYS)], *waits)

    def held(self, *waits):
        arrays = lax.optimization_barrier((*[piece for piece, _ in self.pieces], *waits))
        self.pieces = [(piece, places) for piece, (_, places) in zip(arrays, self.pieces)]
        return arrays[len(self.pieces) :]


def whole_rows(value):
    return [(lax.all_gather(value, "seq", axis=0, tiled=True), [lambda at: 0])]


def collect_events(events):
    size = lax.axis_size("seq")
    here = lax.axis_index("seq")
    rows = events.shape[1]
    if size > RING_LIMIT:
        return [lax.all_to_all(events, "seq", split_axis=0, concat_axis=1, tiled=True)[0]], [lambda at: 0]
    blocks = [lax.dynamic_index_in_dim(events, here, 0, False)]
    firsts = [lambda at: at[0] * rows]
    for step in range(1, size):
        block = lax.dynamic_index_in_dim(events, (here + step) % size, 0, False)
        blocks.append(shift(block, "seq", step))
        firsts.append(
            functools.partial(lambda d, at: lax.rem(at[0] + size - d, size) * rows, step)
        )
    return blocks, firsts


def norm_kernel(places, firsts, at_ref, gain_ref, *refs):
    count, blocks = len(places), len(firsts)
    pieces, (normed_ref, share_ref, source_ref) = refs[:count], refs[count:]
    width = normed_ref.shape[1]
    cols = pieces[0].shape[1]
    rows = pieces[0].shape[0] // blocks
    for block in range(blocks):
        first = pl.multiple_of(firsts[block](at_ref), rows)
        parts = [p[block * rows : (block + 1) * rows, :].astype(jnp.float32) for p in pieces]
        square = sum(jnp.sum(v * v, axis=-1, keepdims=True) for v in parts)
        scale = lax.rsqrt(square / width + eps)
        for index in range(count):
            col = pl.ds(pl.multiple_of(places[index](at_ref) * cols, cols), cols)
            source_ref[pl.ds(first, rows), col] = parts[index].astype(jnp.bfloat16)
            normed_ref[pl.ds(first, rows), col] = (
                parts[index] * scale * gain_ref[:, col]
            ).astype(jnp.bfloat16)
    mine = share_ref.shape[0]
    first = pl.multiple_of((at_ref[2] * lax.axis_size("kv") + at_ref[3]) * mine, mine)
    share_ref[...] = source_ref[pl.ds(first, mine), :]


def norm_events(at, pieces, firsts, gain):
    length = pieces[0][0].shape[0]
    width = gain.shape[0]
    mine = length // (lax.axis_size("tp") * lax.axis_size("kv"))
    return pl.pallas_call(
        functools.partial(norm_kernel, [where for _, where in pieces], firsts),
        out_shape=(
            jax.ShapeDtypeStruct((length, width), jnp.bfloat16),
            jax.ShapeDtypeStruct((mine, width), jnp.bfloat16),
        ),
        in_specs=[SM] + [VM] * (1 + len(pieces)),
        out_specs=(VM, VM),
        scratch_shapes=[pltpu.VMEM((length, width), jnp.bfloat16)],
        compiler_params=params(),
        cost_estimate=cost(4),
        name="norm_events",
    )(
        at,
        gain[None, :],
        *[piece for piece, _ in pieces],
    )


def load_pieces(pieces, firsts, at_ref, base, whole, columns, sems):
    copies = []
    for piece, places in zip(pieces, firsts):
        rows = piece.shape[0] // len(places)
        for block, place in enumerate(places):
            first = pl.multiple_of(place(at_ref), rows)
            copy = pltpu.make_async_copy(
                piece.at[pl.ds(block * rows, rows)],
                whole.at[pl.ds(first, rows), columns],
                sems.at[base + len(copies)],
            )
            copy.start()
            copies.append(copy)
    return copies


def block_count(pieces):
    return sum(len(places) for _, places in pieces)


def encoder_kernel(
    firsts, ratio, at_ref, live_ref, rows_ref, cache_ref, *refs
):
    pieces, (out_ref, whole, projected, normed_ref, history_ref, sems) = refs[:-6], refs[-6:]
    length = rows_ref.shape[0]
    heads = out_ref.shape[1] // DH
    kv_heads = heads // ratio
    query_cols = heads * DH
    key_cols = kv_heads * DH
    past = history_ref.shape[1]
    spare = sems.shape[0] - 2
    early = pltpu.make_async_copy(rows_ref, normed_ref, sems.at[spare])
    later = pltpu.make_async_copy(cache_ref, history_ref, sems.at[spare + 1])
    early.start()
    copies = load_pieces(pieces, firsts, at_ref, 0, whole, slice(None), sems)
    later.start()
    for copy in copies:
        copy.wait()
    early.wait()
    tile = min(256, length)
    for row in range(0, length, tile):
        projected[row : row + tile, :] = jnp.dot(
            normed_ref[row : row + tile, :], whole[...], preferred_element_type=jnp.float32
        ).astype(jnp.bfloat16)
    later.wait()
    live = live_ref[0] * BLK
    contract = (((1,), (1,)), ((), ()))
    for group in range(kv_heads):
        keys = slice(query_cols + group * DH, query_cols + (group + 1) * DH)
        values = slice(query_cols + key_cols + group * DH, query_cols + key_cols + (group + 1) * DH)
        cached = slice(group * DH, (group + 1) * DH)
        for row in range(0, length, tile):
            reach = row + tile
            for head in range(group * ratio, (group + 1) * ratio):
                query = projected[row:reach, head * DH : (head + 1) * DH]
                old = lax.dot_general(
                    query, history_ref[0, :, cached], contract, preferred_element_type=jnp.float32
                )
                new = lax.dot_general(
                    query, projected[:reach, keys], contract, preferred_element_type=jnp.float32
                )
                query_index = row + lax.broadcasted_iota(jnp.int32, (tile, reach), 0)
                key_index = lax.broadcasted_iota(jnp.int32, (tile, reach), 1)
                new = jnp.where((key_index <= query_index) & (key_index < live), new, -1e30)
                top = jnp.maximum(
                    jnp.max(old, axis=-1, keepdims=True), jnp.max(new, axis=-1, keepdims=True)
                )
                scale = DH ** (-0.5)
                old = jnp.exp((old - top) * scale)
                new = jnp.exp((new - top) * scale)
                total_weight = jnp.sum(old, axis=-1, keepdims=True) + jnp.sum(
                    new, axis=-1, keepdims=True
                )
                mixed = jnp.dot(
                    old.astype(jnp.bfloat16),
                    history_ref[1, :, cached],
                    preferred_element_type=jnp.float32,
                ) + jnp.dot(
                    new.astype(jnp.bfloat16),
                    projected[:reach, values],
                    preferred_element_type=jnp.float32,
                )
                out_ref[row:reach, head * DH : (head + 1) * DH] = (mixed / total_weight).astype(
                    jnp.bfloat16
                )


def encoder_attention(at, normed, history, block_counts, pieces):
    length, width = normed.shape
    key_cols = history.shape[2]
    joined = pieces[0][0].shape[1]
    query_cols = joined - 2 * key_cols
    return pl.pallas_call(
        functools.partial(
            encoder_kernel, [places for _, places in pieces], query_cols // key_cols
        ),
        out_shape=jax.ShapeDtypeStruct((length, query_cols), jnp.bfloat16),
        in_specs=[SM, SM, HB, HB] + [HB] * len(pieces),
        out_specs=VM,
        scratch_shapes=[
            pltpu.VMEM((width, joined), jnp.bfloat16),
            pltpu.VMEM((length, joined), jnp.bfloat16),
            pltpu.VMEM((length, width), jnp.bfloat16),
            pltpu.VMEM(history.shape, jnp.bfloat16),
            pltpu.SemaphoreType.DMA((block_count(pieces) + 2,)),
        ],
        compiler_params=params(),
        cost_estimate=cost(11),
        name="encoder_attention",
    )(
        at,
        block_counts,
        normed,
        history,
        *[piece for piece, _ in pieces],
    )


def project_kernel(firsts, orders, parts, at_ref, attended_ref, *refs):
    count = len(firsts)
    pieces, outs, (whole, sems) = refs[:count], refs[count:-2], refs[-2:]
    copies = load_pieces(pieces, firsts, at_ref, 0, whole, slice(None), sems)
    part = outs[0].shape[0] // len(orders[0])
    for copy in copies:
        copy.wait()
    for index, order in enumerate(orders):
        rows = []
        for step in range(parts):
            for where in order:
                first = pl.multiple_of((where(at_ref) * parts + step) * part, part)
                rows.append(attended_ref[pl.ds(first, part), :])
        terms = lax.dot_general(
            jnp.concatenate(rows, axis=0),
            whole[...],
            (((1,), (1,)), ((), ())),
            preferred_element_type=jnp.float32,
        ).astype(jnp.bfloat16)
        size = part * len(order)
        for step in range(parts):
            outs[index * parts + step][...] = terms[step * size : (step + 1) * size, :]


def project_out(at, attended, pieces, orders, part, parts):
    cols = attended.shape[1]
    width = pieces[0][0].shape[0] * lax.axis_size("seq")
    if len(pieces) == 1:
        width = pieces[0][0].shape[0]
    shape = jax.ShapeDtypeStruct((len(orders[0]) * part, width), jnp.bfloat16)
    outs = pl.pallas_call(
        functools.partial(project_kernel, [places for _, places in pieces], orders, parts),
        out_shape=tuple([shape] * len(orders) * parts),
        in_specs=[SM, VM] + [HB] * len(pieces),
        out_specs=tuple([VM] * len(orders) * parts),
        scratch_shapes=[
            pltpu.VMEM((width, cols), jnp.bfloat16),
            pltpu.SemaphoreType.DMA((block_count(pieces),)),
        ],
        compiler_params=params(),
        cost_estimate=cost(2),
        name="project_out",
    )(at, attended, *[piece for piece, _ in pieces])
    return [outs[index * parts : (index + 1) * parts] for index in range(len(orders))]


def merge_kernel(first, gain_ref, source_ref, *refs):
    near, (far, encoded_ref, crossed_ref) = refs[:-3], refs[-3:]
    rows = encoded_ref.shape[0]
    total = source_ref[first : first + rows, :].astype(jnp.float32)
    for term in near:
        total = total + term[:rows, :].astype(jnp.float32)
    for term in range(far.shape[0]):
        total = total + far[term].astype(jnp.float32)
    encoded_ref[...] = total.astype(jnp.bfloat16)
    square = jnp.mean(total * total, axis=-1, keepdims=True)
    crossed_ref[...] = (total * lax.rsqrt(square + eps) * gain_ref[...]).astype(jnp.bfloat16)


def merge_terms(first, source, near, far, gain):
    shape = jax.ShapeDtypeStruct(far.shape[1:], jnp.bfloat16)
    return pl.pallas_call(
        functools.partial(merge_kernel, first),
        out_shape=(shape, shape),
        in_specs=[VM] * (3 + len(near)),
        out_specs=(VM, VM),
        compiler_params=params(),
        cost_estimate=cost(1),
        name=f"merge_terms_{first}",
    )(gain[None, :], source, *near, far)


def cross_kernel(places, firsts, at_ref, *refs):
    count = len(places)
    pieces, (out_ref, source, whole, sems) = refs[:-4], refs[-4:]
    copies = load_pieces(pieces[count:], firsts, at_ref, 0, whole, slice(None), sems)
    copies += load_pieces(pieces[:count], places, at_ref, len(copies), source, slice(None), sems)
    for copy in copies:
        copy.wait()
    tile = min(256, out_ref.shape[0])
    for row in range(0, out_ref.shape[0], tile):
        out_ref[row : row + tile, :] = jnp.dot(
            source[row : row + tile, :], whole[...], preferred_element_type=jnp.float32
        ).astype(jnp.bfloat16)


def cross_project(at, row_pieces, pieces):
    width = row_pieces[0][0].shape[1]
    length = sum(rows.shape[0] for rows, _ in row_pieces)
    cols = pieces[0][0].shape[1]
    return pl.pallas_call(
        functools.partial(
            cross_kernel, [places for _, places in row_pieces], [places for _, places in pieces]
        ),
        out_shape=jax.ShapeDtypeStruct((length, cols), jnp.bfloat16),
        in_specs=[SM] + [HB] * (len(row_pieces) + len(pieces)),
        out_specs=VM,
        scratch_shapes=[
            pltpu.VMEM((length, width), jnp.bfloat16),
            pltpu.VMEM((width, cols), jnp.bfloat16),
            pltpu.SemaphoreType.DMA((block_count(row_pieces) + block_count(pieces),)),
        ],
        compiler_params=params(),
        cost_estimate=cost(2),
        name="cross_project",
    )(at, *[rows for rows, _ in row_pieces], *[piece for piece, _ in pieces])


def beam_kernel(
    level, count, last, ratio, places,
    at_ref, live_ref, parent_ref, gain_ref, query_ref, out_weight_ref, cross_ref, code_ref,
    *refs,
):
    inputs, outs, moved = refs[: count + 1 if level else 0], refs[count + 1 if level else 0 : -1], refs[-1]
    beams = code_ref.shape[0]
    code = code_ref[...].astype(jnp.float32)
    if level:
        total = inputs[0][...]
        for term in inputs[1:]:
            total = total + term[...].astype(jnp.float32)
        moved[...] = total
        rows = [moved[pl.ds(parent_ref[level - 1, row], 1), :] for row in range(beams)]
        hidden = jnp.concatenate(rows, axis=0) + code
    else:
        hidden = code
    square = jnp.mean(hidden * hidden, axis=-1, keepdims=True)
    normed = (hidden * lax.rsqrt(square + eps) * gain_ref[...]).astype(jnp.bfloat16)
    queries = jnp.dot(normed, query_ref[...], preferred_element_type=jnp.float32)
    queries = queries.astype(jnp.bfloat16)
    key_cols = cross_ref.shape[1] // 2
    events = cross_ref.shape[0]
    live = live_ref[0] * BLK
    attended = []
    for group in range(key_cols // DH):
        first = group * ratio
        stacked = jnp.concatenate(
            [queries[:, h * DH : (h + 1) * DH] for h in range(first, first + ratio)], axis=0
        )
        scores = lax.dot_general(
            stacked,
            cross_ref[:, group * DH : (group + 1) * DH],
            (((1,), (1,)), ((), ())),
            preferred_element_type=jnp.float32,
        )
        index = lax.broadcasted_iota(jnp.int32, scores.shape, 1)
        scores = jnp.where(index < live, scores, -1e30)
        top = jnp.max(scores, axis=-1, keepdims=True)
        raised = jnp.exp((scores - top) * DH ** (-0.5))
        weight = jnp.sum(raised, axis=-1, keepdims=True)
        mixed = jnp.dot(
            raised.astype(jnp.bfloat16),
            cross_ref[:, key_cols + group * DH : key_cols + (group + 1) * DH],
            preferred_element_type=jnp.float32,
        )
        mixed = (mixed / weight).astype(jnp.bfloat16)
        attended += [mixed[h * beams : (h + 1) * beams, :] for h in range(ratio)]
    terms = jnp.dot(
        jnp.concatenate(attended, axis=1), out_weight_ref[...], preferred_element_type=jnp.float32
    )
    if not last:
        outs[0][...] = hidden
        outs[1][...] = terms.astype(jnp.bfloat16)
    else:
        cols = outs[0].shape[1]
        moved[...] = terms
        for index in range(1, len(outs)):
            col = pl.ds(pl.multiple_of(places[index](at_ref) * cols, cols), cols)
            outs[index][...] = moved[:, col].astype(jnp.bfloat16)
        moved[...] = hidden + terms
        outs[0][...] = moved[:, pl.ds(pl.multiple_of(places[0](at_ref) * cols, cols), cols)]


def beam_step(at, level, live, parents, places, gain, query, out_weight, cross, code, inputs, last):
    beams, width = code.shape
    ratio = H // KVH
    if last:
        cols = width // len(places)
        outs = [jax.ShapeDtypeStruct((beams, cols), jnp.float32)] + [
            jax.ShapeDtypeStruct((beams, cols), jnp.bfloat16)
        ] * (len(places) - 1)
    else:
        outs = [
            jax.ShapeDtypeStruct((beams, width), jnp.float32),
            jax.ShapeDtypeStruct((beams, width), jnp.bfloat16),
        ]
    return pl.pallas_call(
        functools.partial(beam_kernel, level, max(len(inputs) - 1, 0), last, ratio, places),
        out_shape=tuple(outs),
        in_specs=[SM, SM, SM] + [VM] * (5 + len(inputs)),
        out_specs=tuple([VM] * len(outs)),
        scratch_shapes=[pltpu.VMEM((beams, width), jnp.float32)],
        compiler_params=params(),
        cost_estimate=cost(4),
        name=f"beam_step_{level}",
    )(at, live, parents, gain[None, :], query, out_weight, cross, code, *inputs)


def shards(
    events,
    history_cache,
    block_counts,
    semantic_ids,
    beam_parents,
    query_weight,
    keyval_weight,
    out_weight,
    cross_weight,
    decoder_query,
    decoder_out,
    code_table,
    encoder_gain,
    cross_gain,
    decoder_gain,
):
    tp, kv = lax.axis_size("tp"), lax.axis_size("kv")
    my_tp, my_kv = lax.axis_index("tp"), lax.axis_index("kv")
    group, groups = my_tp * kv + my_kv, tp * kv

    at = position()
    joined = [query_weight, keyval_weight[0], keyval_weight[1]]
    crossing = jnp.concatenate([cross_weight[0], cross_weight[1]], axis=1)
    ringed = lax.axis_size("seq") <= RING_LIMIT
    blocks, firsts = collect_events(events)

    def look_up(waits):
        vocab_rows = code_table.shape[0]
        vocab_ids = group * vocab_rows + lax.broadcasted_iota(jnp.int32, (1, vocab_rows), 1)
        onehot = (semantic_ids.reshape(-1)[:, None] == vocab_ids).astype(jnp.bfloat16)
        onehot = after(onehot, *waits)
        rows = jnp.dot(onehot, code_table, preferred_element_type=jnp.float32).astype(jnp.bfloat16)
        for axis, size in (("kv", kv), ("tp", tp)):
            rows = sum([exchange(rows, axis, step) for step in range(1, size)], rows)
        return rows

    if ringed:
        joined, out, cross = map(Rows, (joined, out_weight, crossing))
        ways = [RING_WAYS[hop % len(RING_WAYS)] for hop in range(lax.axis_size("seq") - 1)]
        joined.hop(ways[0])
        blocks[1], joined.last[1] = lax.optimization_barrier((blocks[1], joined.last[1]))
        mine = jnp.concatenate(blocks, axis=0)
        joined.fresh = [(joined.last[1], 1)]
        stage = [joined.last[1]]
        event_pieces = gather_heads(mine)
        codes, turned = look_up(stage), after(decoder_out, *stage).T
        normed, source = norm_events(at, event_pieces, firsts, encoder_gain)
        for way in ways[1:]:
            joined.swap()
            swapped = joined.swapped()
            joined.hop(way, *stage)
            stage = [joined.last[way], swapped]
        normed, codes, turned, *stage = lax.optimization_barrier((normed, codes, turned, *stage))
        joined.swap(normed)
        out.start(*stage)
        normed, *_ = joined.held(normed, *out.last.values())
        joined_pieces = joined.pieces
        out.swap(*stage)
        out.end()
        cross.start(normed)
    else:
        joined_pieces, out_pieces, cross_pieces = map(
            whole_rows, (jnp.concatenate(joined, axis=1), out_weight, crossing)
        )
        normed, source = norm_events(at, gather_heads(blocks[0]), firsts, encoder_gain)
        codes = look_up([])
        turned = decoder_out.T
    attended = encoder_attention(
        at, normed, history_cache[:, 0], block_counts, joined_pieces
    )
    if ringed:
        out.swap(attended)
        out_pieces = out.pieces
        attended, *_ = lax.optimization_barrier((attended, *cross.last.values()))
    steps, beams = semantic_ids.shape
    codes = codes.reshape(steps, beams, codes.shape[1])

    def place(d, e, at):
        return partner(at[2], d, tp) * kv + partner(at[3], e, kv)

    orders = [[functools.partial(place, d, e) for d in range(tp)] for e in range(kv)]
    share = normed.shape[0] // groups
    parts = 2 if share % 32 == 0 else 1
    part = share // parts
    kept, *sent = project_out(at, attended, out_pieces, orders, part, parts)
    arrived = [
        [exchange(terms[step], "kv", e + 1) for e, terms in enumerate(sent)] for step in range(parts)
    ]
    late = []
    if ringed:
        cross.swap(attended)
        cross.end(attended, cross.last[-1])
        late = [piece for piece, _ in cross.pieces[1:]] + list(cross.last.values())

    def summed(d, step):
        rows = slice(d * part, (d + 1) * part)
        near = [kept[step], *arrived[step]]
        return sum(terms[rows].astype(jnp.float32) for terms in near).astype(jnp.bfloat16)

    merged = [
        merge_terms(
            step * part,
            source,
            [kept[step], *arrived[step]],
            jnp.stack([exchange(summed(d, step), "tp", d) for d in range(1, tp)]),
            cross_gain,
        )
        for step in range(parts)
    ]
    encoded = jnp.concatenate([encoded for encoded, _ in merged], axis=0)
    if ringed:
        cross.swap(merged[-1][1])
        cross_pieces = cross.pieces
    crossed_pieces = []
    for index, (_, crossed) in enumerate(merged):
        waits = late if index == 0 else []
        if ringed and index == parts - 1:
            waits = [*waits, cross_pieces[-1][0]]
        for rows, where in gather_heads(crossed, waits):
            crossed_pieces.append(
                (rows, [functools.partial(lambda f, i, at: f(at) * share + i, where, index * part)])
            )
    keys_values = cross_project(at, crossed_pieces, cross_pieces)

    places = [functools.partial(place, 0, 0)]
    moves = []
    for d in range(tp):
        for e in range(kv):
            if d or e:
                places.append(functools.partial(place, d, e))
                moves.append(
                    [
                        (a * kv + b, partner(a, d, tp) * kv + partner(b, e, kv))
                        for a in range(tp)
                        for b in range(kv)
                    ]
                )
    inputs = []
    for level in range(steps):
        last = level == steps - 1
        kept, *sent = beam_step(
            at, level, block_counts, beam_parents, places, decoder_gain, decoder_query, turned,
            keys_values, codes[level], inputs, last,
        )
        if last:
            arrived = [lax.ppermute(v, ("tp", "kv"), move) for v, move in zip(sent, moves)]
        else:
            inputs = [kept] + [terms for terms, _ in gather_heads(sent[0])]
    beam_out = sum([a.astype(jnp.float32) for a in arrived], kept).astype(jnp.bfloat16)
    return (encoded[None], beam_out)


def solution(mesh):
    in_specs = (
        P("groups", "seq", ("tp", "kv")),
        P(None, ("groups", "seq"), None, ("tp", "kv")),
        P(("groups", "seq")),
        P(None, ("groups", "seq")),
        P(None, ("groups", "seq")),
        P("seq", ("tp", "kv")),
        P(None, "seq", ("tp", "kv")),
        P("seq", ("tp", "kv")),
        P(None, "seq", ("tp", "kv")),
        P(None, ("tp", "kv")),
        P(None, ("tp", "kv")),
        P(("tp", "kv"), None),
        P(),
        P(),
        P(),
    )
    out_specs = (P(("groups", "seq"), ("tp", "kv"), None), P(("groups", "seq"), ("tp", "kv")))
    return jax.shard_map(shards, mesh=mesh, in_specs=in_specs, out_specs=out_specs, check_vma=False)
```

```python
import functools

import jax
import jax.numpy as jnp
from jax import lax
from jax.experimental import pallas as pl
from jax.experimental.pallas import tpu as pltpu
from jax.sharding import PartitionSpec as P

H = 16
DH = 128
KVH = 8
BLK = 128
STEPS = 4
RING_LIMIT = 8
RING_WAYS = (1, -1)
VMEM_BYTES = 16 * 1024 * 1024

eps = 1e-06

VM = pl.BlockSpec(memory_space=pltpu.VMEM)
SM = pl.BlockSpec(memory_space=pltpu.SMEM)
HB = pl.BlockSpec(memory_space=pl.ANY)


def params():
    return pltpu.CompilerParams(vmem_limit_bytes=VMEM_BYTES)


def cost(micros):
    return pl.CostEstimate(flops=0, bytes_accessed=int(micros * 3.0e6), transcendentals=0)


def partner(index, step, size):
    if size & (size - 1) == 0:
        return index ^ step
    return (index + step) % size


def origin(index, step, size):
    if size & (size - 1) == 0:
        return index ^ step
    return (index - step) % size


def exchange(value, axis, step):
    size = lax.axis_size(axis)
    return lax.ppermute(value, axis, [(i, partner(i, step, size)) for i in range(size)])


def shift(value, axis, step):
    size = lax.axis_size(axis)
    return lax.ppermute(value, axis, [(i, (i + step) % size) for i in range(size)])


def after(value, *others):
    return lax.optimization_barrier((value, *others))[0]


def position():
    return jnp.stack([lax.axis_index(axis) for axis in ("seq", "groups", "tp", "kv")])


def gather_heads(value, waits=()):
    tp, kv = lax.axis_size("tp"), lax.axis_size("kv")
    along = [(value, lambda at: at[2])]
    for step in range(1, tp):
        along.append(
            (exchange(value, "tp", step), functools.partial(lambda d, at: origin(at[2], d, tp), step))
        )
    if waits:
        along = along[:1] + [(after(piece, *waits), where) for piece, where in along[1:]]
    pieces = []
    for piece, where in along:
        pieces.append((piece, functools.partial(lambda f, at: f(at) * kv + at[3], where)))
    for piece, where in along:
        for step in range(1, kv):
            pieces.append(
                (
                    exchange(piece, "kv", step),
                    functools.partial(
                        lambda f, e, at: f(at) * kv + origin(at[3], e, kv), where, step
                    ),
                )
            )
    return pieces


class Rows:
    def __init__(self, columns):
        columns = columns if isinstance(columns, list) else [columns]
        value = jnp.concatenate(columns, axis=1)
        self.size = lax.axis_size("seq")
        self.rows = value.shape[0]
        self.shared = lax.axis_size("groups") == 2 and self.rows % 32 == 0
        self.pieces = [(value, [functools.partial(lambda r, at: at[0] * r, self.rows)])]
        half = self.rows // 2
        if self.shared:
            first = lax.axis_index("groups") * half
            columns = [lax.dynamic_slice_in_dim(column, first, half, 0) for column in columns]
            value = jnp.concatenate(columns, axis=1)
        self.last = {1: value, -1: value}
        self.hops = {1: 0, -1: 0}
        self.fresh = []

    def hop(self, way, *waits):
        arrived = shift(after(self.last[way], *waits) if waits else self.last[way], "seq", way)
        self.last[way] = arrived
        self.hops[way] += 1
        self.fresh.append((arrived, way * self.hops[way]))

    def place(self, distance, twin):
        size, rows = self.size, self.rows

        def first(at):
            row = lax.rem(at[0] + size - distance, size) * rows
            return row + (at[1] ^ twin) * (rows // 2) if self.shared else row

        return [first]

    def keep(self):
        for arrived, distance in self.fresh:
            self.pieces.append((arrived, self.place(distance, 0)))
        self.fresh = []

    def swap(self, *waits):
        for arrived, distance in self.fresh:
            self.pieces.append((arrived, self.place(distance, 0)))
            if self.shared:
                other = exchange(after(arrived, *waits) if waits else arrived, "groups", 1)
                self.pieces.append((other, self.place(distance, 1)))
        self.fresh = []

    def direct(self, distance, *waits):
        if self.shared:
            half = self.rows // 2
            rest = 1 - lax.axis_index("groups")
            other = lax.dynamic_slice_in_dim(self.pieces[0][0], rest * half, half, 0)
            other = shift(after(other, *waits) if waits else other, "seq", distance)
            self.pieces.append((other, self.place(distance, 1)))

    def start(self, *waits):
        for way in RING_WAYS[: self.size - 1]:
            self.hop(way, *waits)

    def swapped(self):
        return self.pieces[-1][0]

    def end(self, *waits):
        for hop in range(len(RING_WAYS), self.size - 1):
            self.hop(RING_WAYS[hop % len(RING_WAYS)], *waits)

    def held(self, *waits):
        arrays = lax.optimization_barrier((*[piece for piece, _ in self.pieces], *waits))
        self.pieces = [(piece, places) for piece, (_, places) in zip(arrays, self.pieces)]
        return arrays[len(self.pieces) :]


def whole_rows(value):
    return [(lax.all_gather(value, "seq", axis=0, tiled=True), [lambda at: 0])]


def collect_events(events):
    size = lax.axis_size("seq")
    here = lax.axis_index("seq")
    rows = events.shape[1]
    if size > RING_LIMIT:
        return [lax.all_to_all(events, "seq", split_axis=0, concat_axis=1, tiled=True)[0]], [lambda at: 0]
    blocks = [lax.dynamic_index_in_dim(events, here, 0, False)]
    firsts = [lambda at: at[0] * rows]
    for step in range(1, size):
        block = lax.dynamic_index_in_dim(events, (here + step) % size, 0, False)
        blocks.append(shift(block, "seq", step))
        firsts.append(
            functools.partial(lambda d, at: lax.rem(at[0] + size - d, size) * rows, step)
        )
    return blocks, firsts


def norm_kernel(places, firsts, at_ref, gain_ref, *refs):
    count, blocks = len(places), len(firsts)
    pieces, (normed_ref, share_ref, source_ref) = refs[:count], refs[count:]
    width = normed_ref.shape[1]
    cols = pieces[0].shape[1]
    rows = pieces[0].shape[0] // blocks
    for block in range(blocks):
        first = pl.multiple_of(firsts[block](at_ref), rows)
        parts = [p[block * rows : (block + 1) * rows, :].astype(jnp.float32) for p in pieces]
        square = sum(jnp.sum(v * v, axis=-1, keepdims=True) for v in parts)
        scale = lax.rsqrt(square / width + eps)
        for index in range(count):
            col = pl.ds(pl.multiple_of(places[index](at_ref) * cols, cols), cols)
            source_ref[pl.ds(first, rows), col] = parts[index].astype(jnp.bfloat16)
            normed_ref[pl.ds(first, rows), col] = (
                parts[index] * scale * gain_ref[:, col]
            ).astype(jnp.bfloat16)
    mine = share_ref.shape[0]
    first = pl.multiple_of((at_ref[2] * lax.axis_size("kv") + at_ref[3]) * mine, mine)
    share_ref[...] = source_ref[pl.ds(first, mine), :]


def norm_events(at, pieces, firsts, gain):
    length = pieces[0][0].shape[0]
    width = gain.shape[0]
    mine = length // (lax.axis_size("tp") * lax.axis_size("kv"))
    return pl.pallas_call(
        functools.partial(norm_kernel, [where for _, where in pieces], firsts),
        out_shape=(
            jax.ShapeDtypeStruct((length, width), jnp.bfloat16),
            jax.ShapeDtypeStruct((mine, width), jnp.bfloat16),
        ),
        in_specs=[SM] + [VM] * (1 + len(pieces)),
        out_specs=(VM, VM),
        scratch_shapes=[pltpu.VMEM((length, width), jnp.bfloat16)],
        compiler_params=params(),
        cost_estimate=cost(4),
        name="norm_events",
    )(
        at,
        gain[None, :],
        *[piece for piece, _ in pieces],
    )


def load_pieces(pieces, firsts, at_ref, base, whole, columns, sems):
    copies = []
    for piece, places in zip(pieces, firsts):
        rows = piece.shape[0] // len(places)
        for block, place in enumerate(places):
            first = pl.multiple_of(place(at_ref), rows)
            copy = pltpu.make_async_copy(
                piece.at[pl.ds(block * rows, rows)],
                whole.at[pl.ds(first, rows), columns],
                sems.at[base + len(copies)],
            )
            copy.start()
            copies.append(copy)
    return copies


def block_count(pieces):
    return sum(len(places) for _, places in pieces)


def encoder_kernel(
    firsts, ratio, at_ref, live_ref, rows_ref, cache_ref, *refs
):
    pieces, (out_ref, whole, projected, normed_ref, history_ref, sems) = refs[:-6], refs[-6:]
    length = rows_ref.shape[0]
    heads = out_ref.shape[1] // DH
    kv_heads = heads // ratio
    query_cols = heads * DH
    key_cols = kv_heads * DH
    past = history_ref.shape[1]
    spare = sems.shape[0] - 2
    early = pltpu.make_async_copy(rows_ref, normed_ref, sems.at[spare])
    later = pltpu.make_async_copy(cache_ref, history_ref, sems.at[spare + 1])
    early.start()
    copies = load_pieces(pieces, firsts, at_ref, 0, whole, slice(None), sems)
    later.start()
    for copy in copies:
        copy.wait()
    early.wait()
    tile = min(256, length)
    for row in range(0, length, tile):
        projected[row : row + tile, :] = jnp.dot(
            normed_ref[row : row + tile, :], whole[...], preferred_element_type=jnp.float32
        ).astype(jnp.bfloat16)
    later.wait()
    live = live_ref[0] * BLK
    contract = (((1,), (1,)), ((), ()))
    for group in range(kv_heads):
        keys = slice(query_cols + group * DH, query_cols + (group + 1) * DH)
        values = slice(query_cols + key_cols + group * DH, query_cols + key_cols + (group + 1) * DH)
        cached = slice(group * DH, (group + 1) * DH)
        for row in range(0, length, tile):
            reach = row + tile
            heads_here = range(group * ratio, (group + 1) * ratio)
            query = jnp.concatenate(
                [projected[row:reach, head * DH : (head + 1) * DH] for head in heads_here], axis=0
            )
            old = lax.dot_general(
                query, history_ref[0, :, cached], contract, preferred_element_type=jnp.float32
            )
            new = lax.dot_general(
                query, projected[:reach, keys], contract, preferred_element_type=jnp.float32
            )
            query_index = row + lax.broadcasted_iota(jnp.int32, (tile, reach), 0)
            key_index = lax.broadcasted_iota(jnp.int32, (tile, reach), 1)
            visible = (key_index <= query_index) & (key_index < live)
            new = jnp.where(jnp.concatenate([visible] * ratio, axis=0), new, -1e30)
            top = jnp.maximum(
                jnp.max(old, axis=-1, keepdims=True), jnp.max(new, axis=-1, keepdims=True)
            )
            scale = DH ** (-0.5)
            old = jnp.exp((old - top) * scale)
            new = jnp.exp((new - top) * scale)
            total_weight = jnp.sum(old, axis=-1, keepdims=True) + jnp.sum(
                new, axis=-1, keepdims=True
            )
            mixed = jnp.dot(
                old.astype(jnp.bfloat16),
                history_ref[1, :, cached],
                preferred_element_type=jnp.float32,
            ) + jnp.dot(
                new.astype(jnp.bfloat16),
                projected[:reach, values],
                preferred_element_type=jnp.float32,
            )
            mixed = (mixed / total_weight).astype(jnp.bfloat16)
            for index, head in enumerate(heads_here):
                out_ref[row:reach, head * DH : (head + 1) * DH] = mixed[
                    index * tile : (index + 1) * tile, :
                ]


def encoder_attention(at, normed, history, block_counts, pieces):
    length, width = normed.shape
    key_cols = history.shape[2]
    joined = pieces[0][0].shape[1]
    query_cols = joined - 2 * key_cols
    return pl.pallas_call(
        functools.partial(
            encoder_kernel, [places for _, places in pieces], query_cols // key_cols
        ),
        out_shape=jax.ShapeDtypeStruct((length, query_cols), jnp.bfloat16),
        in_specs=[SM, SM, HB, HB] + [HB] * len(pieces),
        out_specs=VM,
        scratch_shapes=[
            pltpu.VMEM((width, joined), jnp.bfloat16),
            pltpu.VMEM((length, joined), jnp.bfloat16),
            pltpu.VMEM((length, width), jnp.bfloat16),
            pltpu.VMEM(history.shape, jnp.bfloat16),
            pltpu.SemaphoreType.DMA((block_count(pieces) + 2,)),
        ],
        compiler_params=params(),
        cost_estimate=cost(11),
        name="encoder_attention",
    )(
        at,
        block_counts,
        normed,
        history,
        *[piece for piece, _ in pieces],
    )


def project_kernel(firsts, orders, parts, at_ref, attended_ref, *refs):
    count = len(firsts)
    pieces, outs, (whole, sems) = refs[:count], refs[count:-2], refs[-2:]
    copies = load_pieces(pieces, firsts, at_ref, 0, whole, slice(None), sems)
    part = outs[0].shape[0] // len(orders[0])
    for copy in copies:
        copy.wait()
    for index, order in enumerate(orders):
        rows = []
        for step in range(parts):
            for where in order:
                first = pl.multiple_of((where(at_ref) * parts + step) * part, part)
                rows.append(attended_ref[pl.ds(first, part), :])
        terms = lax.dot_general(
            jnp.concatenate(rows, axis=0),
            whole[...],
            (((1,), (1,)), ((), ())),
            preferred_element_type=jnp.float32,
        ).astype(jnp.bfloat16)
        size = part * len(order)
        for step in range(parts):
            outs[index * parts + step][...] = terms[step * size : (step + 1) * size, :]


def project_out(at, attended, pieces, orders, part, parts):
    cols = attended.shape[1]
    width = pieces[0][0].shape[0] * lax.axis_size("seq")
    if len(pieces) == 1:
        width = pieces[0][0].shape[0]
    shape = jax.ShapeDtypeStruct((len(orders[0]) * part, width), jnp.bfloat16)
    outs = pl.pallas_call(
        functools.partial(project_kernel, [places for _, places in pieces], orders, parts),
        out_shape=tuple([shape] * len(orders) * parts),
        in_specs=[SM, VM] + [HB] * len(pieces),
        out_specs=tuple([VM] * len(orders) * parts),
        scratch_shapes=[
            pltpu.VMEM((width, cols), jnp.bfloat16),
            pltpu.SemaphoreType.DMA((block_count(pieces),)),
        ],
        compiler_params=params(),
        cost_estimate=cost(2),
        name="project_out",
    )(at, attended, *[piece for piece, _ in pieces])
    return [outs[index * parts : (index + 1) * parts] for index in range(len(orders))]


def merge_kernel(first, gain_ref, source_ref, *refs):
    near, (far, encoded_ref, crossed_ref) = refs[:-3], refs[-3:]
    rows = encoded_ref.shape[0]
    total = source_ref[first : first + rows, :].astype(jnp.float32)
    for term in near:
        total = total + term[:rows, :].astype(jnp.float32)
    for term in range(far.shape[0]):
        total = total + far[term].astype(jnp.float32)
    encoded_ref[...] = total.astype(jnp.bfloat16)
    square = jnp.mean(total * total, axis=-1, keepdims=True)
    crossed_ref[...] = (total * lax.rsqrt(square + eps) * gain_ref[...]).astype(jnp.bfloat16)


def merge_terms(first, source, near, far, gain):
    shape = jax.ShapeDtypeStruct(far.shape[1:], jnp.bfloat16)
    return pl.pallas_call(
        functools.partial(merge_kernel, first),
        out_shape=(shape, shape),
        in_specs=[VM] * (3 + len(near)),
        out_specs=(VM, VM),
        compiler_params=params(),
        cost_estimate=cost(1),
        name=f"merge_terms_{first}",
    )(gain[None, :], source, *near, far)


def cross_kernel(places, firsts, at_ref, *refs):
    count = len(places)
    pieces, (out_ref, source, whole, sems) = refs[:-4], refs[-4:]
    copies = load_pieces(pieces[count:], firsts, at_ref, 0, whole, slice(None), sems)
    copies += load_pieces(pieces[:count], places, at_ref, len(copies), source, slice(None), sems)
    for copy in copies:
        copy.wait()
    tile = min(256, out_ref.shape[0])
    for row in range(0, out_ref.shape[0], tile):
        out_ref[row : row + tile, :] = jnp.dot(
            source[row : row + tile, :], whole[...], preferred_element_type=jnp.float32
        ).astype(jnp.bfloat16)


def cross_project(at, row_pieces, pieces):
    width = row_pieces[0][0].shape[1]
    length = sum(rows.shape[0] for rows, _ in row_pieces)
    cols = pieces[0][0].shape[1]
    return pl.pallas_call(
        functools.partial(
            cross_kernel, [places for _, places in row_pieces], [places for _, places in pieces]
        ),
        out_shape=jax.ShapeDtypeStruct((length, cols), jnp.bfloat16),
        in_specs=[SM] + [HB] * (len(row_pieces) + len(pieces)),
        out_specs=VM,
        scratch_shapes=[
            pltpu.VMEM((length, width), jnp.bfloat16),
            pltpu.VMEM((width, cols), jnp.bfloat16),
            pltpu.SemaphoreType.DMA((block_count(row_pieces) + block_count(pieces),)),
        ],
        compiler_params=params(),
        cost_estimate=cost(2),
        name="cross_project",
    )(at, *[rows for rows, _ in row_pieces], *[piece for piece, _ in pieces])


def beam_kernel(
    level, count, last, ratio, places,
    at_ref, live_ref, parent_ref, gain_ref, query_ref, out_weight_ref, cross_ref, code_ref,
    *refs,
):
    inputs, outs, moved = refs[: count + 1 if level else 0], refs[count + 1 if level else 0 : -1], refs[-1]
    beams = code_ref.shape[0]
    code = code_ref[...].astype(jnp.float32)
    if level:
        total = inputs[0][...]
        for term in inputs[1:]:
            total = total + term[...].astype(jnp.float32)
        moved[...] = total
        rows = [moved[pl.ds(parent_ref[level - 1, row], 1), :] for row in range(beams)]
        hidden = jnp.concatenate(rows, axis=0) + code
    else:
        hidden = code
    square = jnp.mean(hidden * hidden, axis=-1, keepdims=True)
    normed = (hidden * lax.rsqrt(square + eps) * gain_ref[...]).astype(jnp.bfloat16)
    queries = jnp.dot(normed, query_ref[...], preferred_element_type=jnp.float32)
    queries = queries.astype(jnp.bfloat16)
    key_cols = cross_ref.shape[1] // 2
    events = cross_ref.shape[0]
    live = live_ref[0] * BLK
    attended = []
    for group in range(key_cols // DH):
        first = group * ratio
        stacked = jnp.concatenate(
            [queries[:, h * DH : (h + 1) * DH] for h in range(first, first + ratio)], axis=0
        )
        scores = lax.dot_general(
            stacked,
            cross_ref[:, group * DH : (group + 1) * DH],
            (((1,), (1,)), ((), ())),
            preferred_element_type=jnp.float32,
        )
        index = lax.broadcasted_iota(jnp.int32, scores.shape, 1)
        scores = jnp.where(index < live, scores, -1e30)
        top = jnp.max(scores, axis=-1, keepdims=True)
        raised = jnp.exp((scores - top) * DH ** (-0.5))
        weight = jnp.sum(raised, axis=-1, keepdims=True)
        mixed = jnp.dot(
            raised.astype(jnp.bfloat16),
            cross_ref[:, key_cols + group * DH : key_cols + (group + 1) * DH],
            preferred_element_type=jnp.float32,
        )
        mixed = (mixed / weight).astype(jnp.bfloat16)
        attended += [mixed[h * beams : (h + 1) * beams, :] for h in range(ratio)]
    terms = jnp.dot(
        jnp.concatenate(attended, axis=1), out_weight_ref[...], preferred_element_type=jnp.float32
    )
    if not last:
        outs[0][...] = hidden
        outs[1][...] = terms.astype(jnp.bfloat16)
    else:
        cols = outs[0].shape[1]
        moved[...] = terms
        for index in range(1, len(outs)):
            col = pl.ds(pl.multiple_of(places[index](at_ref) * cols, cols), cols)
            outs[index][...] = moved[:, col].astype(jnp.bfloat16)
        moved[...] = hidden + terms
        outs[0][...] = moved[:, pl.ds(pl.multiple_of(places[0](at_ref) * cols, cols), cols)]


def beam_step(at, level, live, parents, places, gain, query, out_weight, cross, code, inputs, last):
    beams, width = code.shape
    ratio = H // KVH
    if last:
        cols = width // len(places)
        outs = [jax.ShapeDtypeStruct((beams, cols), jnp.float32)] + [
            jax.ShapeDtypeStruct((beams, cols), jnp.bfloat16)
        ] * (len(places) - 1)
    else:
        outs = [
            jax.ShapeDtypeStruct((beams, width), jnp.float32),
            jax.ShapeDtypeStruct((beams, width), jnp.bfloat16),
        ]
    return pl.pallas_call(
        functools.partial(beam_kernel, level, max(len(inputs) - 1, 0), last, ratio, places),
        out_shape=tuple(outs),
        in_specs=[SM, SM, SM] + [VM] * (5 + len(inputs)),
        out_specs=tuple([VM] * len(outs)),
        scratch_shapes=[pltpu.VMEM((beams, width), jnp.float32)],
        compiler_params=params(),
        cost_estimate=cost(4),
        name=f"beam_step_{level}",
    )(at, live, parents, gain[None, :], query, out_weight, cross, code, *inputs)


def shards(
    events,
    history_cache,
    block_counts,
    semantic_ids,
    beam_parents,
    query_weight,
    keyval_weight,
    out_weight,
    cross_weight,
    decoder_query,
    decoder_out,
    code_table,
    encoder_gain,
    cross_gain,
    decoder_gain,
):
    tp, kv = lax.axis_size("tp"), lax.axis_size("kv")
    my_tp, my_kv = lax.axis_index("tp"), lax.axis_index("kv")
    group, groups = my_tp * kv + my_kv, tp * kv

    at = position()
    joined = [query_weight, keyval_weight[0], keyval_weight[1]]
    crossing = jnp.concatenate([cross_weight[0], cross_weight[1]], axis=1)
    ringed = lax.axis_size("seq") <= RING_LIMIT
    blocks, firsts = collect_events(events)

    def look_up(waits):
        vocab_rows = code_table.shape[0]
        vocab_ids = group * vocab_rows + lax.broadcasted_iota(jnp.int32, (1, vocab_rows), 1)
        onehot = (semantic_ids.reshape(-1)[:, None] == vocab_ids).astype(jnp.bfloat16)
        onehot = after(onehot, *waits)
        rows = jnp.dot(onehot, code_table, preferred_element_type=jnp.float32).astype(jnp.bfloat16)
        for axis, size in (("kv", kv), ("tp", tp)):
            rows = sum([exchange(rows, axis, step) for step in range(1, size)], rows)
        return rows

    if ringed:
        joined, out, cross = map(Rows, (joined, out_weight, crossing))
        ways = [RING_WAYS[hop % len(RING_WAYS)] for hop in range(lax.axis_size("seq") - 1)]
        joined.hop(ways[0])
        blocks[1], joined.last[1] = lax.optimization_barrier((blocks[1], joined.last[1]))
        mine = jnp.concatenate(blocks, axis=0)
        joined.fresh = [(joined.last[1], 1)]
        stage = [joined.last[1]]
        event_pieces = gather_heads(mine)
        codes, turned = look_up(stage), after(decoder_out, *stage).T
        normed, source = norm_events(at, event_pieces, firsts, encoder_gain)
        for way in ways[1:]:
            joined.swap()
            swapped = joined.swapped()
            joined.hop(way, *stage)
            stage = [joined.last[way], swapped]
        normed, codes, turned, *stage = lax.optimization_barrier((normed, codes, turned, *stage))
        joined.swap(normed)
        out.start(*stage)
        normed, *_ = joined.held(normed, *out.last.values())
        joined_pieces = joined.pieces
        out.swap(*stage)
        out.end()
        cross.start(normed)
    else:
        joined_pieces, out_pieces, cross_pieces = map(
            whole_rows, (jnp.concatenate(joined, axis=1), out_weight, crossing)
        )
        normed, source = norm_events(at, gather_heads(blocks[0]), firsts, encoder_gain)
        codes = look_up([])
        turned = decoder_out.T
    attended = encoder_attention(
        at, normed, history_cache[:, 0], block_counts, joined_pieces
    )
    if ringed:
        out.swap(attended)
        out_pieces = out.pieces
        attended, *_ = lax.optimization_barrier((attended, *cross.last.values()))
    steps, beams = semantic_ids.shape
    codes = codes.reshape(steps, beams, codes.shape[1])

    def place(d, e, at):
        return partner(at[2], d, tp) * kv + partner(at[3], e, kv)

    orders = [[functools.partial(place, d, e) for d in range(tp)] for e in range(kv)]
    share = normed.shape[0] // groups
    parts = 2 if share % 32 == 0 else 1
    part = share // parts
    kept, *sent = project_out(at, attended, out_pieces, orders, part, parts)
    arrived = [
        [exchange(terms[step], "kv", e + 1) for e, terms in enumerate(sent)] for step in range(parts)
    ]
    late = []
    if ringed:
        cross.swap(attended)
        cross.end(attended, cross.last[-1])
        late = [piece for piece, _ in cross.pieces[1:]] + list(cross.last.values())

    def summed(d, step):
        rows = slice(d * part, (d + 1) * part)
        near = [kept[step], *arrived[step]]
        return sum(terms[rows].astype(jnp.float32) for terms in near).astype(jnp.bfloat16)

    merged = [
        merge_terms(
            step * part,
            source,
            [kept[step], *arrived[step]],
            jnp.stack([exchange(summed(d, step), "tp", d) for d in range(1, tp)]),
            cross_gain,
        )
        for step in range(parts)
    ]
    encoded = jnp.concatenate([encoded for encoded, _ in merged], axis=0)
    if ringed:
        cross.swap(merged[-1][1])
        cross_pieces = cross.pieces
    crossed_pieces = []
    for index, (_, crossed) in enumerate(merged):
        waits = late if index == 0 else []
        if ringed and index == parts - 1:
            waits = [*waits, cross_pieces[-1][0]]
        for rows, where in gather_heads(crossed, waits):
            crossed_pieces.append(
                (rows, [functools.partial(lambda f, i, at: f(at) * share + i, where, index * part)])
            )
    keys_values = cross_project(at, crossed_pieces, cross_pieces)

    places = [functools.partial(place, 0, 0)]
    moves = []
    for d in range(tp):
        for e in range(kv):
            if d or e:
                places.append(functools.partial(place, d, e))
                moves.append(
                    [
                        (a * kv + b, partner(a, d, tp) * kv + partner(b, e, kv))
                        for a in range(tp)
                        for b in range(kv)
                    ]
                )
    inputs = []
    for level in range(steps):
        last = level == steps - 1
        kept, *sent = beam_step(
            at, level, block_counts, beam_parents, places, decoder_gain, decoder_query, turned,
            keys_values, codes[level], inputs, last,
        )
        if last:
            arrived = [lax.ppermute(v, ("tp", "kv"), move) for v, move in zip(sent, moves)]
        else:
            inputs = [kept] + [terms for terms, _ in gather_heads(sent[0])]
    beam_out = sum([a.astype(jnp.float32) for a in arrived], kept).astype(jnp.bfloat16)
    return (encoded[None], beam_out)


def solution(mesh):
    in_specs = (
        P("groups", "seq", ("tp", "kv")),
        P(None, ("groups", "seq"), None, ("tp", "kv")),
        P(("groups", "seq")),
        P(None, ("groups", "seq")),
        P(None, ("groups", "seq")),
        P("seq", ("tp", "kv")),
        P(None, "seq", ("tp", "kv")),
        P("seq", ("tp", "kv")),
        P(None, "seq", ("tp", "kv")),
        P(None, ("tp", "kv")),
        P(None, ("tp", "kv")),
        P(("tp", "kv"), None),
        P(),
        P(),
        P(),
    )
    out_specs = (P(("groups", "seq"), ("tp", "kv"), None), P(("groups", "seq"), ("tp", "kv")))
    return jax.shard_map(shards, mesh=mesh, in_specs=in_specs, out_specs=out_specs, check_vma=False)
```

```python
import functools

import jax
import jax.numpy as jnp
from jax import lax
from jax.experimental import pallas as pl
from jax.experimental.pallas import tpu as pltpu
from jax.sharding import PartitionSpec as P

H = 16
DH = 128
KVH = 8
BLK = 128
STEPS = 4
RING_LIMIT = 8
RING_WAYS = (1, -1)
VMEM_BYTES = 16 * 1024 * 1024

eps = 1e-06

VM = pl.BlockSpec(memory_space=pltpu.VMEM)
SM = pl.BlockSpec(memory_space=pltpu.SMEM)
HB = pl.BlockSpec(memory_space=pl.ANY)


def params():
    return pltpu.CompilerParams(vmem_limit_bytes=VMEM_BYTES)


def cost(micros):
    return pl.CostEstimate(flops=0, bytes_accessed=int(micros * 3.0e6), transcendentals=0)


def partner(index, step, size):
    if size & (size - 1) == 0:
        return index ^ step
    return (index + step) % size


def origin(index, step, size):
    if size & (size - 1) == 0:
        return index ^ step
    return (index - step) % size


def exchange(value, axis, step):
    size = lax.axis_size(axis)
    return lax.ppermute(value, axis, [(i, partner(i, step, size)) for i in range(size)])


def shift(value, axis, step):
    size = lax.axis_size(axis)
    return lax.ppermute(value, axis, [(i, (i + step) % size) for i in range(size)])


def after(value, *others):
    return lax.optimization_barrier((value, *others))[0]


def position():
    return jnp.stack([lax.axis_index(axis) for axis in ("seq", "groups", "tp", "kv")])


def gather_heads(value, waits=()):
    tp, kv = lax.axis_size("tp"), lax.axis_size("kv")
    along = [(value, lambda at: at[2])]
    for step in range(1, tp):
        along.append(
            (exchange(value, "tp", step), functools.partial(lambda d, at: origin(at[2], d, tp), step))
        )
    if waits:
        along = along[:1] + [(after(piece, *waits), where) for piece, where in along[1:]]
    pieces = []
    for piece, where in along:
        pieces.append((piece, functools.partial(lambda f, at: f(at) * kv + at[3], where)))
    for piece, where in along:
        for step in range(1, kv):
            pieces.append(
                (
                    exchange(piece, "kv", step),
                    functools.partial(
                        lambda f, e, at: f(at) * kv + origin(at[3], e, kv), where, step
                    ),
                )
            )
    return pieces


class Rows:
    def __init__(self, columns):
        columns = columns if isinstance(columns, list) else [columns]
        value = jnp.concatenate(columns, axis=1)
        self.size = lax.axis_size("seq")
        self.rows = value.shape[0]
        self.shared = lax.axis_size("groups") == 2 and self.rows % 32 == 0
        self.pieces = [(value, [functools.partial(lambda r, at: at[0] * r, self.rows)])]
        half = self.rows // 2
        if self.shared:
            first = lax.axis_index("groups") * half
            columns = [lax.dynamic_slice_in_dim(column, first, half, 0) for column in columns]
            value = jnp.concatenate(columns, axis=1)
        self.last = {1: value, -1: value}
        self.hops = {1: 0, -1: 0}
        self.fresh = []

    def hop(self, way, *waits):
        arrived = shift(after(self.last[way], *waits) if waits else self.last[way], "seq", way)
        self.last[way] = arrived
        self.hops[way] += 1
        self.fresh.append((arrived, way * self.hops[way]))

    def place(self, distance, twin):
        size, rows = self.size, self.rows

        def first(at):
            row = lax.rem(at[0] + size - distance, size) * rows
            return row + (at[1] ^ twin) * (rows // 2) if self.shared else row

        return [first]

    def keep(self):
        for arrived, distance in self.fresh:
            self.pieces.append((arrived, self.place(distance, 0)))
        self.fresh = []

    def swap(self, *waits):
        for arrived, distance in self.fresh:
            self.pieces.append((arrived, self.place(distance, 0)))
            if self.shared:
                other = exchange(after(arrived, *waits) if waits else arrived, "groups", 1)
                self.pieces.append((other, self.place(distance, 1)))
        self.fresh = []

    def direct(self, distance, *waits):
        if self.shared:
            half = self.rows // 2
            rest = 1 - lax.axis_index("groups")
            other = lax.dynamic_slice_in_dim(self.pieces[0][0], rest * half, half, 0)
            other = shift(after(other, *waits) if waits else other, "seq", distance)
            self.pieces.append((other, self.place(distance, 1)))

    def start(self, *waits):
        for way in RING_WAYS[: self.size - 1]:
            self.hop(way, *waits)

    def swapped(self):
        return self.pieces[-1][0]

    def end(self, *waits):
        for hop in range(len(RING_WAYS), self.size - 1):
            self.hop(RING_WAYS[hop % len(RING_WAYS)], *waits)

    def held(self, *waits):
        arrays = lax.optimization_barrier((*[piece for piece, _ in self.pieces], *waits))
        self.pieces = [(piece, places) for piece, (_, places) in zip(arrays, self.pieces)]
        return arrays[len(self.pieces) :]


def whole_rows(value):
    return [(lax.all_gather(value, "seq", axis=0, tiled=True), [lambda at: 0])]


def collect_events(events):
    size = lax.axis_size("seq")
    here = lax.axis_index("seq")
    rows = events.shape[1]
    if size > RING_LIMIT:
        return [lax.all_to_all(events, "seq", split_axis=0, concat_axis=1, tiled=True)[0]], [lambda at: 0]
    blocks = [lax.dynamic_index_in_dim(events, here, 0, False)]
    firsts = [lambda at: at[0] * rows]
    for step in range(1, size):
        block = lax.dynamic_index_in_dim(events, (here + step) % size, 0, False)
        blocks.append(shift(block, "seq", step))
        firsts.append(
            functools.partial(lambda d, at: lax.rem(at[0] + size - d, size) * rows, step)
        )
    return blocks, firsts


def norm_kernel(places, firsts, at_ref, gain_ref, *refs):
    count, blocks = len(places), len(firsts)
    pieces, (normed_ref, share_ref, source_ref) = refs[:count], refs[count:]
    width = normed_ref.shape[1]
    cols = pieces[0].shape[1]
    rows = pieces[0].shape[0] // blocks
    for block in range(blocks):
        first = pl.multiple_of(firsts[block](at_ref), rows)
        parts = [p[block * rows : (block + 1) * rows, :].astype(jnp.float32) for p in pieces]
        square = sum(jnp.sum(v * v, axis=-1, keepdims=True) for v in parts)
        scale = lax.rsqrt(square / width + eps)
        for index in range(count):
            col = pl.ds(pl.multiple_of(places[index](at_ref) * cols, cols), cols)
            source_ref[pl.ds(first, rows), col] = parts[index].astype(jnp.bfloat16)
            normed_ref[pl.ds(first, rows), col] = (
                parts[index] * scale * gain_ref[:, col]
            ).astype(jnp.bfloat16)
    mine = share_ref.shape[0]
    first = pl.multiple_of((at_ref[2] * lax.axis_size("kv") + at_ref[3]) * mine, mine)
    share_ref[...] = source_ref[pl.ds(first, mine), :]


def norm_events(at, pieces, firsts, gain):
    length = pieces[0][0].shape[0]
    width = gain.shape[0]
    mine = length // (lax.axis_size("tp") * lax.axis_size("kv"))
    return pl.pallas_call(
        functools.partial(norm_kernel, [where for _, where in pieces], firsts),
        out_shape=(
            jax.ShapeDtypeStruct((length, width), jnp.bfloat16),
            jax.ShapeDtypeStruct((mine, width), jnp.bfloat16),
        ),
        in_specs=[SM] + [VM] * (1 + len(pieces)),
        out_specs=(VM, VM),
        scratch_shapes=[pltpu.VMEM((length, width), jnp.bfloat16)],
        compiler_params=params(),
        cost_estimate=cost(4),
        name="norm_events",
    )(
        at,
        gain[None, :],
        *[piece for piece, _ in pieces],
    )


def load_pieces(pieces, firsts, at_ref, base, whole, columns, sems):
    copies = []
    for piece, places in zip(pieces, firsts):
        rows = piece.shape[0] // len(places)
        for block, place in enumerate(places):
            first = pl.multiple_of(place(at_ref), rows)
            copy = pltpu.make_async_copy(
                piece.at[pl.ds(block * rows, rows)],
                whole.at[pl.ds(first, rows), columns],
                sems.at[base + len(copies)],
            )
            copy.start()
            copies.append(copy)
    return copies


def block_count(pieces):
    return sum(len(places) for _, places in pieces)


def encoder_kernel(
    firsts, ratio, at_ref, live_ref, rows_ref, cache_ref, *refs
):
    pieces, (out_ref, whole, projected, normed_ref, history_ref, sems) = refs[:-6], refs[-6:]
    length = rows_ref.shape[0]
    heads = out_ref.shape[1] // DH
    kv_heads = heads // ratio
    query_cols = heads * DH
    key_cols = kv_heads * DH
    past = history_ref.shape[1]
    spare = sems.shape[0] - 2
    early = pltpu.make_async_copy(rows_ref, normed_ref, sems.at[spare])
    later = pltpu.make_async_copy(cache_ref, history_ref, sems.at[spare + 1])
    early.start()
    copies = load_pieces(pieces, firsts, at_ref, 0, whole, slice(None), sems)
    later.start()
    for copy in copies:
        copy.wait()
    early.wait()
    tile = min(256, length)
    for row in range(0, length, tile):
        projected[row : row + tile, :] = jnp.dot(
            normed_ref[row : row + tile, :], whole[...], preferred_element_type=jnp.float32
        ).astype(jnp.bfloat16)
    later.wait()
    live = live_ref[0] * BLK
    contract = (((1,), (1,)), ((), ()))
    for group in range(kv_heads):
        keys = slice(query_cols + group * DH, query_cols + (group + 1) * DH)
        values = slice(query_cols + key_cols + group * DH, query_cols + key_cols + (group + 1) * DH)
        cached = slice(group * DH, (group + 1) * DH)
        for row in range(0, length, tile):
            reach = row + tile
            heads_here = range(group * ratio, (group + 1) * ratio)
            query = jnp.concatenate(
                [projected[row:reach, head * DH : (head + 1) * DH] for head in heads_here], axis=0
            )
            old = lax.dot_general(
                query, history_ref[0, :, cached], contract, preferred_element_type=jnp.float32
            )
            new = lax.dot_general(
                query, projected[:reach, keys], contract, preferred_element_type=jnp.float32
            )
            query_index = row + lax.broadcasted_iota(jnp.int32, (tile, reach), 0)
            key_index = lax.broadcasted_iota(jnp.int32, (tile, reach), 1)
            visible = (key_index <= query_index) & (key_index < live)
            new = jnp.where(jnp.concatenate([visible] * ratio, axis=0), new, -1e30)
            top = jnp.maximum(
                jnp.max(old, axis=-1, keepdims=True), jnp.max(new, axis=-1, keepdims=True)
            )
            scale = DH ** (-0.5)
            old = jnp.exp((old - top) * scale)
            new = jnp.exp((new - top) * scale)
            total_weight = jnp.sum(old, axis=-1, keepdims=True) + jnp.sum(
                new, axis=-1, keepdims=True
            )
            mixed = jnp.dot(
                old.astype(jnp.bfloat16),
                history_ref[1, :, cached],
                preferred_element_type=jnp.float32,
            ) + jnp.dot(
                new.astype(jnp.bfloat16),
                projected[:reach, values],
                preferred_element_type=jnp.float32,
            )
            mixed = (mixed / total_weight).astype(jnp.bfloat16)
            for index, head in enumerate(heads_here):
                out_ref[row:reach, head * DH : (head + 1) * DH] = mixed[
                    index * tile : (index + 1) * tile, :
                ]


def encoder_attention(at, normed, history, block_counts, pieces):
    length, width = normed.shape
    key_cols = history.shape[2]
    joined = pieces[0][0].shape[1]
    query_cols = joined - 2 * key_cols
    return pl.pallas_call(
        functools.partial(
            encoder_kernel, [places for _, places in pieces], query_cols // key_cols
        ),
        out_shape=jax.ShapeDtypeStruct((length, query_cols), jnp.bfloat16),
        in_specs=[SM, SM, HB, HB] + [HB] * len(pieces),
        out_specs=VM,
        scratch_shapes=[
            pltpu.VMEM((width, joined), jnp.bfloat16),
            pltpu.VMEM((length, joined), jnp.bfloat16),
            pltpu.VMEM((length, width), jnp.bfloat16),
            pltpu.VMEM(history.shape, jnp.bfloat16),
            pltpu.SemaphoreType.DMA((block_count(pieces) + 2,)),
        ],
        compiler_params=params(),
        cost_estimate=cost(11),
        name="encoder_attention",
    )(
        at,
        block_counts,
        normed,
        history,
        *[piece for piece, _ in pieces],
    )


def project_kernel(firsts, orders, parts, at_ref, attended_ref, *refs):
    count = len(firsts)
    pieces, outs, (whole, sems) = refs[:count], refs[count:-2], refs[-2:]
    copies = load_pieces(pieces, firsts, at_ref, 0, whole, slice(None), sems)
    part = outs[0].shape[0] // len(orders[0])
    for copy in copies:
        copy.wait()
    for index, order in enumerate(orders):
        rows = []
        for step in range(parts):
            for where in order:
                first = pl.multiple_of((where(at_ref) * parts + step) * part, part)
                rows.append(attended_ref[pl.ds(first, part), :])
        terms = lax.dot_general(
            jnp.concatenate(rows, axis=0),
            whole[...],
            (((1,), (1,)), ((), ())),
            preferred_element_type=jnp.float32,
        ).astype(jnp.bfloat16)
        size = part * len(order)
        for step in range(parts):
            outs[index * parts + step][...] = terms[step * size : (step + 1) * size, :]


def project_out(at, attended, pieces, orders, part, parts):
    cols = attended.shape[1]
    width = pieces[0][0].shape[0] * lax.axis_size("seq")
    if len(pieces) == 1:
        width = pieces[0][0].shape[0]
    shape = jax.ShapeDtypeStruct((len(orders[0]) * part, width), jnp.bfloat16)
    outs = pl.pallas_call(
        functools.partial(project_kernel, [places for _, places in pieces], orders, parts),
        out_shape=tuple([shape] * len(orders) * parts),
        in_specs=[SM, VM] + [HB] * len(pieces),
        out_specs=tuple([VM] * len(orders) * parts),
        scratch_shapes=[
            pltpu.VMEM((width, cols), jnp.bfloat16),
            pltpu.SemaphoreType.DMA((block_count(pieces),)),
        ],
        compiler_params=params(),
        cost_estimate=cost(2),
        name="project_out",
    )(at, attended, *[piece for piece, _ in pieces])
    return [outs[index * parts : (index + 1) * parts] for index in range(len(orders))]


def merge_kernel(first, gain_ref, source_ref, *refs):
    near, (far, encoded_ref, crossed_ref) = refs[:-3], refs[-3:]
    rows = encoded_ref.shape[0]
    total = source_ref[first : first + rows, :].astype(jnp.float32)
    for term in near:
        total = total + term[:rows, :].astype(jnp.float32)
    for term in range(far.shape[0]):
        total = total + far[term].astype(jnp.float32)
    encoded_ref[...] = total.astype(jnp.bfloat16)
    square = jnp.mean(total * total, axis=-1, keepdims=True)
    crossed_ref[...] = (total * lax.rsqrt(square + eps) * gain_ref[...]).astype(jnp.bfloat16)


def merge_terms(first, source, near, far, gain):
    shape = jax.ShapeDtypeStruct(far.shape[1:], jnp.bfloat16)
    return pl.pallas_call(
        functools.partial(merge_kernel, first),
        out_shape=(shape, shape),
        in_specs=[VM] * (3 + len(near)),
        out_specs=(VM, VM),
        compiler_params=params(),
        cost_estimate=cost(1),
        name=f"merge_terms_{first}",
    )(gain[None, :], source, *near, far)


def cross_kernel(places, firsts, at_ref, *refs):
    count = len(places)
    pieces, (out_ref, source, whole, sems) = refs[:-4], refs[-4:]
    copies = load_pieces(pieces[count:], firsts, at_ref, 0, whole, slice(None), sems)
    copies += load_pieces(pieces[:count], places, at_ref, len(copies), source, slice(None), sems)
    for copy in copies:
        copy.wait()
    tile = min(256, out_ref.shape[0])
    for row in range(0, out_ref.shape[0], tile):
        out_ref[row : row + tile, :] = jnp.dot(
            source[row : row + tile, :], whole[...], preferred_element_type=jnp.float32
        ).astype(jnp.bfloat16)


def cross_project(at, row_pieces, pieces, name):
    width = row_pieces[0][0].shape[1]
    length = sum(rows.shape[0] for rows, _ in row_pieces)
    cols = pieces[0][0].shape[1]
    return pl.pallas_call(
        functools.partial(
            cross_kernel, [places for _, places in row_pieces], [places for _, places in pieces]
        ),
        out_shape=jax.ShapeDtypeStruct((length, cols), jnp.bfloat16),
        in_specs=[SM] + [HB] * (len(row_pieces) + len(pieces)),
        out_specs=VM,
        scratch_shapes=[
            pltpu.VMEM((length, width), jnp.bfloat16),
            pltpu.VMEM((width, cols), jnp.bfloat16),
            pltpu.SemaphoreType.DMA((block_count(row_pieces) + block_count(pieces),)),
        ],
        compiler_params=params(),
        cost_estimate=cost(2),
        name=name,
    )(at, *[rows for rows, _ in row_pieces], *[piece for piece, _ in pieces])


def beam_kernel(
    level, count, last, ratio, places, parts,
    at_ref, live_ref, parent_ref, gain_ref, query_ref, out_weight_ref, code_ref,
    *refs,
):
    crosses, refs = refs[:parts], refs[parts:]
    inputs, outs, moved = refs[: count + 1 if level else 0], refs[count + 1 if level else 0 : -1], refs[-1]
    beams = code_ref.shape[0]
    code = code_ref[...].astype(jnp.float32)
    if level:
        total = inputs[0][...]
        for term in inputs[1:]:
            total = total + term[...].astype(jnp.float32)
        moved[...] = total
        rows = [moved[pl.ds(parent_ref[level - 1, row], 1), :] for row in range(beams)]
        hidden = jnp.concatenate(rows, axis=0) + code
    else:
        hidden = code
    square = jnp.mean(hidden * hidden, axis=-1, keepdims=True)
    normed = (hidden * lax.rsqrt(square + eps) * gain_ref[...]).astype(jnp.bfloat16)
    queries = jnp.dot(normed, query_ref[...], preferred_element_type=jnp.float32)
    queries = queries.astype(jnp.bfloat16)
    key_cols = crosses[0].shape[1] // 2
    live = live_ref[0] * BLK
    groups = lax.axis_size("tp") * lax.axis_size("kv")
    part = crosses[0].shape[0] // groups
    attended = []
    for group in range(key_cols // DH):
        first = group * ratio
        stacked = jnp.concatenate(
            [queries[:, h * DH : (h + 1) * DH] for h in range(first, first + ratio)], axis=0
        )
        scores = []
        for index, cross_ref in enumerate(crosses):
            part_scores = lax.dot_general(
                stacked,
                cross_ref[:, group * DH : (group + 1) * DH],
                (((1,), (1,)), ((), ())),
                preferred_element_type=jnp.float32,
            )
            row = lax.broadcasted_iota(jnp.int32, part_scores.shape, 1)
            event = row // part * (part * parts) + index * part + row % part
            scores.append(jnp.where(event < live, part_scores, -1e30))
        top = functools.reduce(
            jnp.maximum, [jnp.max(values, axis=-1, keepdims=True) for values in scores]
        )
        raised = [jnp.exp((values - top) * DH ** (-0.5)) for values in scores]
        weight = sum(jnp.sum(values, axis=-1, keepdims=True) for values in raised)
        mixed = sum(
            jnp.dot(
                values.astype(jnp.bfloat16),
                cross_ref[:, key_cols + group * DH : key_cols + (group + 1) * DH],
                preferred_element_type=jnp.float32,
            )
            for values, cross_ref in zip(raised, crosses)
        )
        mixed = (mixed / weight).astype(jnp.bfloat16)
        attended += [mixed[h * beams : (h + 1) * beams, :] for h in range(ratio)]
    terms = jnp.dot(
        jnp.concatenate(attended, axis=1), out_weight_ref[...], preferred_element_type=jnp.float32
    )
    if not last:
        outs[0][...] = hidden
        outs[1][...] = terms.astype(jnp.bfloat16)
    else:
        cols = outs[0].shape[1]
        moved[...] = terms
        for index in range(1, len(outs)):
            col = pl.ds(pl.multiple_of(places[index](at_ref) * cols, cols), cols)
            outs[index][...] = moved[:, col].astype(jnp.bfloat16)
        moved[...] = hidden + terms
        outs[0][...] = moved[:, pl.ds(pl.multiple_of(places[0](at_ref) * cols, cols), cols)]


def beam_step(
    at, level, live, parents, places, gain, query, out_weight, crosses, code, inputs, last
):
    beams, width = code.shape
    ratio = H // KVH
    if last:
        cols = width // len(places)
        outs = [jax.ShapeDtypeStruct((beams, cols), jnp.float32)] + [
            jax.ShapeDtypeStruct((beams, cols), jnp.bfloat16)
        ] * (len(places) - 1)
    else:
        outs = [
            jax.ShapeDtypeStruct((beams, width), jnp.float32),
            jax.ShapeDtypeStruct((beams, width), jnp.bfloat16),
        ]
    return pl.pallas_call(
        functools.partial(beam_kernel, level, max(len(inputs) - 1, 0), last, ratio, places, len(crosses)),
        out_shape=tuple(outs),
        in_specs=[SM, SM, SM] + [VM] * (4 + len(crosses) + len(inputs)),
        out_specs=tuple([VM] * len(outs)),
        scratch_shapes=[pltpu.VMEM((beams, width), jnp.float32)],
        compiler_params=params(),
        cost_estimate=cost(4),
        name=f"beam_step_{level}",
    )(at, live, parents, gain[None, :], query, out_weight, code, *crosses, *inputs)


def shards(
    events,
    history_cache,
    block_counts,
    semantic_ids,
    beam_parents,
    query_weight,
    keyval_weight,
    out_weight,
    cross_weight,
    decoder_query,
    decoder_out,
    code_table,
    encoder_gain,
    cross_gain,
    decoder_gain,
):
    tp, kv = lax.axis_size("tp"), lax.axis_size("kv")
    my_tp, my_kv = lax.axis_index("tp"), lax.axis_index("kv")
    group, groups = my_tp * kv + my_kv, tp * kv

    at = position()
    joined = [query_weight, keyval_weight[0], keyval_weight[1]]
    crossing = jnp.concatenate([cross_weight[0], cross_weight[1]], axis=1)
    ringed = lax.axis_size("seq") <= RING_LIMIT
    blocks, firsts = collect_events(events)

    def look_up(waits):
        vocab_rows = code_table.shape[0]
        vocab_ids = group * vocab_rows + lax.broadcasted_iota(jnp.int32, (1, vocab_rows), 1)
        onehot = (semantic_ids.reshape(-1)[:, None] == vocab_ids).astype(jnp.bfloat16)
        onehot = after(onehot, *waits)
        rows = jnp.dot(onehot, code_table, preferred_element_type=jnp.float32).astype(jnp.bfloat16)
        for axis, size in (("kv", kv), ("tp", tp)):
            rows = sum([exchange(rows, axis, step) for step in range(1, size)], rows)
        return rows

    if ringed:
        joined, out, cross = map(Rows, (joined, out_weight, crossing))
        ways = [RING_WAYS[hop % len(RING_WAYS)] for hop in range(lax.axis_size("seq") - 1)]
        joined.hop(ways[0])
        blocks[1], joined.last[1] = lax.optimization_barrier((blocks[1], joined.last[1]))
        mine = jnp.concatenate(blocks, axis=0)
        joined.fresh = [(joined.last[1], 1)]
        stage = [joined.last[1]]
        event_pieces = gather_heads(mine)
        codes, turned = look_up(stage), after(decoder_out, *stage).T
        normed, source = norm_events(at, event_pieces, firsts, encoder_gain)
        for way in ways[1:]:
            joined.swap()
            swapped = joined.swapped()
            joined.hop(way, *stage)
            stage = [joined.last[way], swapped]
        normed, codes, turned, *stage = lax.optimization_barrier((normed, codes, turned, *stage))
        joined.swap(normed)
        out.start(*stage)
        normed, *_ = joined.held(normed, *out.last.values())
        joined_pieces = joined.pieces
        out.swap(*stage)
        out.end()
        cross.start(normed)
    else:
        joined_pieces, out_pieces, cross_pieces = map(
            whole_rows, (jnp.concatenate(joined, axis=1), out_weight, crossing)
        )
        normed, source = norm_events(at, gather_heads(blocks[0]), firsts, encoder_gain)
        codes = look_up([])
        turned = decoder_out.T
    attended = encoder_attention(
        at, normed, history_cache[:, 0], block_counts, joined_pieces
    )
    if ringed:
        out.swap(attended)
        out_pieces = out.pieces
        attended, *_ = lax.optimization_barrier((attended, *cross.last.values()))
    steps, beams = semantic_ids.shape
    codes = codes.reshape(steps, beams, codes.shape[1])

    def place(d, e, at):
        return partner(at[2], d, tp) * kv + partner(at[3], e, kv)

    orders = [[functools.partial(place, d, e) for d in range(tp)] for e in range(kv)]
    share = normed.shape[0] // groups
    parts = 2 if share % 32 == 0 else 1
    part = share // parts
    kept, *sent = project_out(at, attended, out_pieces, orders, part, parts)
    arrived = [
        [exchange(terms[step], "kv", e + 1) for e, terms in enumerate(sent)] for step in range(parts)
    ]
    late = []
    if ringed:
        cross.swap(attended)
        cross.end(attended, cross.last[-1])
        late = [piece for piece, _ in cross.pieces[1:]] + list(cross.last.values())

    def summed(d, step):
        rows = slice(d * part, (d + 1) * part)
        near = [kept[step], *arrived[step]]
        return sum(terms[rows].astype(jnp.float32) for terms in near).astype(jnp.bfloat16)

    merged = [
        merge_terms(
            step * part,
            source,
            [kept[step], *arrived[step]],
            jnp.stack([exchange(summed(d, step), "tp", d) for d in range(1, tp)]),
            cross_gain,
        )
        for step in range(parts)
    ]
    encoded = jnp.concatenate([encoded for encoded, _ in merged], axis=0)
    if ringed:
        cross.swap(merged[-1][1])
        cross_pieces = cross.pieces
    keys_values = []
    for index, (_, crossed) in enumerate(merged):
        waits = late if index == 0 else []
        if ringed and index == parts - 1:
            waits = [*waits, cross_pieces[-1][0]]
        crossed_pieces = [
            (rows, [functools.partial(lambda f, at: f(at) * part, where)])
            for rows, where in gather_heads(crossed, waits)
        ]
        keys_values.append(cross_project(at, crossed_pieces, cross_pieces, f"cross_project_{index}"))

    places = [functools.partial(place, 0, 0)]
    moves = []
    for d in range(tp):
        for e in range(kv):
            if d or e:
                places.append(functools.partial(place, d, e))
                moves.append(
                    [
                        (a * kv + b, partner(a, d, tp) * kv + partner(b, e, kv))
                        for a in range(tp)
                        for b in range(kv)
                    ]
                )
    inputs = []
    for level in range(steps):
        last = level == steps - 1
        kept, *sent = beam_step(
            at, level, block_counts, beam_parents, places, decoder_gain, decoder_query, turned,
            keys_values, codes[level], inputs, last,
        )
        if last:
            arrived = [lax.ppermute(v, ("tp", "kv"), move) for v, move in zip(sent, moves)]
        else:
            inputs = [kept] + [terms for terms, _ in gather_heads(sent[0])]
    beam_out = sum([a.astype(jnp.float32) for a in arrived], kept).astype(jnp.bfloat16)
    return (encoded[None], beam_out)


def solution(mesh):
    in_specs = (
        P("groups", "seq", ("tp", "kv")),
        P(None, ("groups", "seq"), None, ("tp", "kv")),
        P(("groups", "seq")),
        P(None, ("groups", "seq")),
        P(None, ("groups", "seq")),
        P("seq", ("tp", "kv")),
        P(None, "seq", ("tp", "kv")),
        P("seq", ("tp", "kv")),
        P(None, "seq", ("tp", "kv")),
        P(None, ("tp", "kv")),
        P(None, ("tp", "kv")),
        P(("tp", "kv"), None),
        P(),
        P(),
        P(),
    )
    out_specs = (P(("groups", "seq"), ("tp", "kv"), None), P(("groups", "seq"), ("tp", "kv")))
    return jax.shard_map(shards, mesh=mesh, in_specs=in_specs, out_specs=out_specs, check_vma=False)
```

```python
import functools
import math

import jax
import jax.numpy as jnp
from jax import lax
from jax.experimental import pallas as pl
from jax.experimental.pallas import tpu as pltpu
from jax.sharding import PartitionSpec as P

H = 16
DH = 128
KVH = 8
BLK = 128
STEPS = 4
RING_LIMIT = 8
RING_WAYS = (1, -1)
VMEM_BYTES = 16 * 1024 * 1024

eps = 1e-06

VM = pl.BlockSpec(memory_space=pltpu.VMEM)
SM = pl.BlockSpec(memory_space=pltpu.SMEM)
HB = pl.BlockSpec(memory_space=pl.ANY)


def params():
    return pltpu.CompilerParams(vmem_limit_bytes=VMEM_BYTES)


def cost(micros):
    return pl.CostEstimate(flops=0, bytes_accessed=int(micros * 3.0e6), transcendentals=0)


def partner(index, step, size):
    if size & (size - 1) == 0:
        return index ^ step
    return (index + step) % size


def origin(index, step, size):
    if size & (size - 1) == 0:
        return index ^ step
    return (index - step) % size


def exchange(value, axis, step):
    size = lax.axis_size(axis)
    return lax.ppermute(value, axis, [(i, partner(i, step, size)) for i in range(size)])


def shift(value, axis, step):
    size = lax.axis_size(axis)
    return lax.ppermute(value, axis, [(i, (i + step) % size) for i in range(size)])


def after(value, *others):
    return lax.optimization_barrier((value, *others))[0]


def position():
    return jnp.stack([lax.axis_index(axis) for axis in ("seq", "groups", "tp", "kv")])


def gather_heads(value, waits=()):
    tp, kv = lax.axis_size("tp"), lax.axis_size("kv")
    along = [(value, lambda at: at[2])]
    for step in range(1, tp):
        along.append(
            (exchange(value, "tp", step), functools.partial(lambda d, at: origin(at[2], d, tp), step))
        )
    if waits:
        along = along[:1] + [(after(piece, *waits), where) for piece, where in along[1:]]
    pieces = []
    for piece, where in along:
        pieces.append((piece, functools.partial(lambda f, at: f(at) * kv + at[3], where)))
    for piece, where in along:
        for step in range(1, kv):
            pieces.append(
                (
                    exchange(piece, "kv", step),
                    functools.partial(
                        lambda f, e, at: f(at) * kv + origin(at[3], e, kv), where, step
                    ),
                )
            )
    return pieces


class Rows:
    def __init__(self, columns):
        columns = columns if isinstance(columns, list) else [columns]
        value = jnp.concatenate(columns, axis=1)
        self.size = lax.axis_size("seq")
        self.rows = value.shape[0]
        self.shared = lax.axis_size("groups") == 2 and self.rows % 32 == 0
        self.pieces = [(value, [functools.partial(lambda r, at: at[0] * r, self.rows)])]
        half = self.rows // 2
        if self.shared:
            first = lax.axis_index("groups") * half
            columns = [lax.dynamic_slice_in_dim(column, first, half, 0) for column in columns]
            value = jnp.concatenate(columns, axis=1)
        self.last = {1: value, -1: value}
        self.hops = {1: 0, -1: 0}
        self.fresh = []

    def hop(self, way, *waits):
        arrived = shift(after(self.last[way], *waits) if waits else self.last[way], "seq", way)
        self.last[way] = arrived
        self.hops[way] += 1
        self.fresh.append((arrived, way * self.hops[way]))

    def place(self, distance, twin):
        size, rows = self.size, self.rows

        def first(at):
            row = lax.rem(at[0] + size - distance, size) * rows
            return row + (at[1] ^ twin) * (rows // 2) if self.shared else row

        return [first]

    def keep(self):
        for arrived, distance in self.fresh:
            self.pieces.append((arrived, self.place(distance, 0)))
        self.fresh = []

    def swap(self, *waits):
        for arrived, distance in self.fresh:
            self.pieces.append((arrived, self.place(distance, 0)))
            if self.shared:
                other = exchange(after(arrived, *waits) if waits else arrived, "groups", 1)
                self.pieces.append((other, self.place(distance, 1)))
        self.fresh = []

    def direct(self, distance, *waits):
        if self.shared:
            half = self.rows // 2
            rest = 1 - lax.axis_index("groups")
            other = lax.dynamic_slice_in_dim(self.pieces[0][0], rest * half, half, 0)
            other = shift(after(other, *waits) if waits else other, "seq", distance)
            self.pieces.append((other, self.place(distance, 1)))

    def start(self, *waits):
        for way in RING_WAYS[: self.size - 1]:
            self.hop(way, *waits)

    def swapped(self):
        return self.pieces[-1][0]

    def end(self, *waits):
        for hop in range(len(RING_WAYS), self.size - 1):
            self.hop(RING_WAYS[hop % len(RING_WAYS)], *waits)

    def held(self, *waits):
        arrays = lax.optimization_barrier((*[piece for piece, _ in self.pieces], *waits))
        self.pieces = [(piece, places) for piece, (_, places) in zip(arrays, self.pieces)]
        return arrays[len(self.pieces) :]


def whole_rows(value):
    return [(lax.all_gather(value, "seq", axis=0, tiled=True), [lambda at: 0])]


def collect_events(events):
    size = lax.axis_size("seq")
    here = lax.axis_index("seq")
    rows = events.shape[1]
    if size > RING_LIMIT:
        return [lax.all_to_all(events, "seq", split_axis=0, concat_axis=1, tiled=True)[0]], [lambda at: 0]
    blocks = [lax.dynamic_index_in_dim(events, here, 0, False)]
    firsts = [lambda at: at[0] * rows]
    for step in range(1, size):
        block = lax.dynamic_index_in_dim(events, (here + step) % size, 0, False)
        blocks.append(shift(block, "seq", step))
        firsts.append(
            functools.partial(lambda d, at: lax.rem(at[0] + size - d, size) * rows, step)
        )
    return blocks, firsts


def norm_kernel(places, firsts, at_ref, gain_ref, *refs):
    count, blocks = len(places), len(firsts)
    pieces, (normed_ref, share_ref, source_ref) = refs[:count], refs[count:]
    width = normed_ref.shape[1]
    cols = pieces[0].shape[1]
    rows = pieces[0].shape[0] // blocks
    for block in range(blocks):
        first = pl.multiple_of(firsts[block](at_ref), rows)
        parts = [p[block * rows : (block + 1) * rows, :].astype(jnp.float32) for p in pieces]
        square = sum(jnp.sum(v * v, axis=-1, keepdims=True) for v in parts)
        scale = lax.rsqrt(square / width + eps)
        for index in range(count):
            col = pl.ds(pl.multiple_of(places[index](at_ref) * cols, cols), cols)
            source_ref[pl.ds(first, rows), col] = parts[index].astype(jnp.bfloat16)
            normed_ref[pl.ds(first, rows), col] = (
                parts[index] * scale * gain_ref[:, col]
            ).astype(jnp.bfloat16)
    mine = share_ref.shape[0]
    first = pl.multiple_of((at_ref[2] * lax.axis_size("kv") + at_ref[3]) * mine, mine)
    share_ref[...] = source_ref[pl.ds(first, mine), :]


def norm_events(at, pieces, firsts, gain):
    length = pieces[0][0].shape[0]
    width = gain.shape[0]
    mine = length // (lax.axis_size("tp") * lax.axis_size("kv"))
    return pl.pallas_call(
        functools.partial(norm_kernel, [where for _, where in pieces], firsts),
        out_shape=(
            jax.ShapeDtypeStruct((length, width), jnp.bfloat16),
            jax.ShapeDtypeStruct((mine, width), jnp.bfloat16),
        ),
        in_specs=[SM] + [VM] * (1 + len(pieces)),
        out_specs=(VM, VM),
        scratch_shapes=[pltpu.VMEM((length, width), jnp.bfloat16)],
        compiler_params=params(),
        cost_estimate=cost(4),
        name="norm_events",
    )(
        at,
        gain[None, :],
        *[piece for piece, _ in pieces],
    )


def load_pieces(pieces, firsts, at_ref, base, whole, columns, sems):
    copies = []
    for piece, places in zip(pieces, firsts):
        rows = piece.shape[0] // len(places)
        for block, place in enumerate(places):
            first = pl.multiple_of(place(at_ref), rows)
            copy = pltpu.make_async_copy(
                piece.at[pl.ds(block * rows, rows)],
                whole.at[pl.ds(first, rows), columns],
                sems.at[base + len(copies)],
            )
            copy.start()
            copies.append(copy)
    return copies


def block_count(pieces):
    return sum(len(places) for _, places in pieces)


def encoder_kernel(
    firsts, ratio, at_ref, live_ref, rows_ref, cache_ref, *refs
):
    pieces, (out_ref, whole, projected, normed_ref, history_ref, sems) = refs[:-6], refs[-6:]
    length = rows_ref.shape[0]
    heads = out_ref.shape[1] // DH
    kv_heads = heads // ratio
    query_cols = heads * DH
    key_cols = kv_heads * DH
    past = history_ref.shape[1]
    spare = sems.shape[0] - 2
    early = pltpu.make_async_copy(rows_ref, normed_ref, sems.at[spare])
    later = pltpu.make_async_copy(cache_ref, history_ref, sems.at[spare + 1])
    early.start()
    copies = load_pieces(pieces, firsts, at_ref, 0, whole, slice(None), sems)
    later.start()
    for copy in copies:
        copy.wait()
    early.wait()
    tile = min(256, length)
    for row in range(0, length, tile):
        projected[row : row + tile, :] = jnp.dot(
            normed_ref[row : row + tile, :], whole[...], preferred_element_type=jnp.float32
        ).astype(jnp.bfloat16)
    later.wait()
    live = live_ref[0] * BLK
    contract = (((1,), (1,)), ((), ()))
    for group in range(kv_heads):
        keys = slice(query_cols + group * DH, query_cols + (group + 1) * DH)
        values = slice(query_cols + key_cols + group * DH, query_cols + key_cols + (group + 1) * DH)
        cached = slice(group * DH, (group + 1) * DH)
        for row in range(0, length, tile):
            reach = row + tile
            heads_here = range(group * ratio, (group + 1) * ratio)
            query = jnp.concatenate(
                [projected[row:reach, head * DH : (head + 1) * DH] for head in heads_here], axis=0
            )
            old = lax.dot_general(
                query, history_ref[0, :, cached], contract, preferred_element_type=jnp.float32
            )
            new = lax.dot_general(
                query, projected[:reach, keys], contract, preferred_element_type=jnp.float32
            )
            query_index = row + lax.broadcasted_iota(jnp.int32, (tile, reach), 0)
            key_index = lax.broadcasted_iota(jnp.int32, (tile, reach), 1)
            visible = (key_index <= query_index) & (key_index < live)
            new = jnp.where(jnp.concatenate([visible] * ratio, axis=0), new, -1e30)
            top = jnp.maximum(
                jnp.max(old, axis=-1, keepdims=True), jnp.max(new, axis=-1, keepdims=True)
            )
            scale = DH ** (-0.5) * math.log2(math.e)
            old = jnp.exp2((old - top) * scale)
            new = jnp.exp2((new - top) * scale)
            total_weight = jnp.sum(old, axis=-1, keepdims=True) + jnp.sum(
                new, axis=-1, keepdims=True
            )
            mixed = jnp.dot(
                old.astype(jnp.bfloat16),
                history_ref[1, :, cached],
                preferred_element_type=jnp.float32,
            ) + jnp.dot(
                new.astype(jnp.bfloat16),
                projected[:reach, values],
                preferred_element_type=jnp.float32,
            )
            mixed = (mixed / total_weight).astype(jnp.bfloat16)
            for index, head in enumerate(heads_here):
                out_ref[row:reach, head * DH : (head + 1) * DH] = mixed[
                    index * tile : (index + 1) * tile, :
                ]


def encoder_attention(at, normed, history, block_counts, pieces):
    length, width = normed.shape
    key_cols = history.shape[2]
    joined = pieces[0][0].shape[1]
    query_cols = joined - 2 * key_cols
    return pl.pallas_call(
        functools.partial(
            encoder_kernel, [places for _, places in pieces], query_cols // key_cols
        ),
        out_shape=jax.ShapeDtypeStruct((length, query_cols), jnp.bfloat16),
        in_specs=[SM, SM, HB, HB] + [HB] * len(pieces),
        out_specs=VM,
        scratch_shapes=[
            pltpu.VMEM((width, joined), jnp.bfloat16),
            pltpu.VMEM((length, joined), jnp.bfloat16),
            pltpu.VMEM((length, width), jnp.bfloat16),
            pltpu.VMEM(history.shape, jnp.bfloat16),
            pltpu.SemaphoreType.DMA((block_count(pieces) + 2,)),
        ],
        compiler_params=params(),
        cost_estimate=cost(11),
        name="encoder_attention",
    )(
        at,
        block_counts,
        normed,
        history,
        *[piece for piece, _ in pieces],
    )


def project_kernel(firsts, orders, parts, at_ref, attended_ref, *refs):
    count = len(firsts)
    pieces, outs, (whole, sems) = refs[:count], refs[count:-2], refs[-2:]
    copies = load_pieces(pieces, firsts, at_ref, 0, whole, slice(None), sems)
    part = outs[0].shape[0] // len(orders[0])
    for copy in copies:
        copy.wait()
    for index, order in enumerate(orders):
        rows = []
        for step in range(parts):
            for where in order:
                first = pl.multiple_of((where(at_ref) * parts + step) * part, part)
                rows.append(attended_ref[pl.ds(first, part), :])
        terms = lax.dot_general(
            jnp.concatenate(rows, axis=0),
            whole[...],
            (((1,), (1,)), ((), ())),
            preferred_element_type=jnp.float32,
        ).astype(jnp.bfloat16)
        size = part * len(order)
        for step in range(parts):
            outs[index * parts + step][...] = terms[step * size : (step + 1) * size, :]


def project_out(at, attended, pieces, orders, part, parts):
    cols = attended.shape[1]
    width = pieces[0][0].shape[0] * lax.axis_size("seq")
    if len(pieces) == 1:
        width = pieces[0][0].shape[0]
    shape = jax.ShapeDtypeStruct((len(orders[0]) * part, width), jnp.bfloat16)
    outs = pl.pallas_call(
        functools.partial(project_kernel, [places for _, places in pieces], orders, parts),
        out_shape=tuple([shape] * len(orders) * parts),
        in_specs=[SM, VM] + [HB] * len(pieces),
        out_specs=tuple([VM] * len(orders) * parts),
        scratch_shapes=[
            pltpu.VMEM((width, cols), jnp.bfloat16),
            pltpu.SemaphoreType.DMA((block_count(pieces),)),
        ],
        compiler_params=params(),
        cost_estimate=cost(2),
        name="project_out",
    )(at, attended, *[piece for piece, _ in pieces])
    return [outs[index * parts : (index + 1) * parts] for index in range(len(orders))]


def merge_kernel(first, gain_ref, source_ref, *refs):
    near, (far, encoded_ref, crossed_ref) = refs[:-3], refs[-3:]
    rows = encoded_ref.shape[0]
    total = source_ref[first : first + rows, :].astype(jnp.float32)
    for term in near:
        total = total + term[:rows, :].astype(jnp.float32)
    for term in range(far.shape[0]):
        total = total + far[term].astype(jnp.float32)
    encoded_ref[...] = total.astype(jnp.bfloat16)
    square = jnp.mean(total * total, axis=-1, keepdims=True)
    crossed_ref[...] = (total * lax.rsqrt(square + eps) * gain_ref[...]).astype(jnp.bfloat16)


def merge_terms(first, source, near, far, gain):
    shape = jax.ShapeDtypeStruct(far.shape[1:], jnp.bfloat16)
    return pl.pallas_call(
        functools.partial(merge_kernel, first),
        out_shape=(shape, shape),
        in_specs=[VM] * (3 + len(near)),
        out_specs=(VM, VM),
        compiler_params=params(),
        cost_estimate=cost(1),
        name=f"merge_terms_{first}",
    )(gain[None, :], source, *near, far)


def cross_kernel(places, firsts, at_ref, *refs):
    count = len(places)
    pieces, (out_ref, source, whole, sems) = refs[:-4], refs[-4:]
    copies = load_pieces(pieces[count:], firsts, at_ref, 0, whole, slice(None), sems)
    copies += load_pieces(pieces[:count], places, at_ref, len(copies), source, slice(None), sems)
    for copy in copies:
        copy.wait()
    tile = min(256, out_ref.shape[0])
    for row in range(0, out_ref.shape[0], tile):
        out_ref[row : row + tile, :] = jnp.dot(
            source[row : row + tile, :], whole[...], preferred_element_type=jnp.float32
        ).astype(jnp.bfloat16)


def cross_project(at, row_pieces, pieces, name):
    width = row_pieces[0][0].shape[1]
    length = sum(rows.shape[0] for rows, _ in row_pieces)
    cols = pieces[0][0].shape[1]
    return pl.pallas_call(
        functools.partial(
            cross_kernel, [places for _, places in row_pieces], [places for _, places in pieces]
        ),
        out_shape=jax.ShapeDtypeStruct((length, cols), jnp.bfloat16),
        in_specs=[SM] + [HB] * (len(row_pieces) + len(pieces)),
        out_specs=VM,
        scratch_shapes=[
            pltpu.VMEM((length, width), jnp.bfloat16),
            pltpu.VMEM((width, cols), jnp.bfloat16),
            pltpu.SemaphoreType.DMA((block_count(row_pieces) + block_count(pieces),)),
        ],
        compiler_params=params(),
        cost_estimate=cost(2),
        name=name,
    )(at, *[rows for rows, _ in row_pieces], *[piece for piece, _ in pieces])


def beam_kernel(
    level, count, last, ratio, places, parts,
    at_ref, live_ref, parent_ref, gain_ref, query_ref, out_weight_ref, code_ref,
    *refs,
):
    crosses, refs = refs[:parts], refs[parts:]
    inputs, outs, moved = refs[: count + 1 if level else 0], refs[count + 1 if level else 0 : -1], refs[-1]
    beams = code_ref.shape[0]
    code = code_ref[...].astype(jnp.float32)
    if level:
        total = inputs[0][...]
        for term in inputs[1:]:
            total = total + term[...].astype(jnp.float32)
        moved[...] = total
        rows = [moved[pl.ds(parent_ref[level - 1, row], 1), :] for row in range(beams)]
        hidden = jnp.concatenate(rows, axis=0) + code
    else:
        hidden = code
    square = jnp.mean(hidden * hidden, axis=-1, keepdims=True)
    normed = (hidden * lax.rsqrt(square + eps) * gain_ref[...]).astype(jnp.bfloat16)
    queries = jnp.dot(normed, query_ref[...], preferred_element_type=jnp.float32)
    queries = queries.astype(jnp.bfloat16)
    key_cols = crosses[0].shape[1] // 2
    live = live_ref[0] * BLK
    groups = lax.axis_size("tp") * lax.axis_size("kv")
    part = crosses[0].shape[0] // groups
    attended = []
    for group in range(key_cols // DH):
        first = group * ratio
        stacked = jnp.concatenate(
            [queries[:, h * DH : (h + 1) * DH] for h in range(first, first + ratio)], axis=0
        )
        scores = []
        for index, cross_ref in enumerate(crosses):
            part_scores = lax.dot_general(
                stacked,
                cross_ref[:, group * DH : (group + 1) * DH],
                (((1,), (1,)), ((), ())),
                preferred_element_type=jnp.float32,
            )
            row = lax.broadcasted_iota(jnp.int32, part_scores.shape, 1)
            event = row // part * (part * parts) + index * part + row % part
            scores.append(jnp.where(event < live, part_scores, -1e30))
        top = functools.reduce(
            jnp.maximum, [jnp.max(values, axis=-1, keepdims=True) for values in scores]
        )
        raised = [jnp.exp2((values - top) * (DH ** (-0.5) * math.log2(math.e))) for values in scores]
        weight = sum(jnp.sum(values, axis=-1, keepdims=True) for values in raised)
        mixed = sum(
            jnp.dot(
                values.astype(jnp.bfloat16),
                cross_ref[:, key_cols + group * DH : key_cols + (group + 1) * DH],
                preferred_element_type=jnp.float32,
            )
            for values, cross_ref in zip(raised, crosses)
        )
        mixed = (mixed / weight).astype(jnp.bfloat16)
        attended += [mixed[h * beams : (h + 1) * beams, :] for h in range(ratio)]
    terms = jnp.dot(
        jnp.concatenate(attended, axis=1), out_weight_ref[...], preferred_element_type=jnp.float32
    )
    if not last:
        outs[0][...] = hidden
        outs[1][...] = terms.astype(jnp.bfloat16)
    else:
        cols = outs[0].shape[1]
        moved[...] = terms
        for index in range(1, len(outs)):
            col = pl.ds(pl.multiple_of(places[index](at_ref) * cols, cols), cols)
            outs[index][...] = moved[:, col].astype(jnp.bfloat16)
        moved[...] = hidden + terms
        outs[0][...] = moved[:, pl.ds(pl.multiple_of(places[0](at_ref) * cols, cols), cols)]


def beam_step(
    at, level, live, parents, places, gain, query, out_weight, crosses, code, inputs, last
):
    beams, width = code.shape
    ratio = H // KVH
    if last:
        cols = width // len(places)
        outs = [jax.ShapeDtypeStruct((beams, cols), jnp.float32)] + [
            jax.ShapeDtypeStruct((beams, cols), jnp.bfloat16)
        ] * (len(places) - 1)
    else:
        outs = [
            jax.ShapeDtypeStruct((beams, width), jnp.float32),
            jax.ShapeDtypeStruct((beams, width), jnp.bfloat16),
        ]
    return pl.pallas_call(
        functools.partial(beam_kernel, level, max(len(inputs) - 1, 0), last, ratio, places, len(crosses)),
        out_shape=tuple(outs),
        in_specs=[SM, SM, SM] + [VM] * (4 + len(crosses) + len(inputs)),
        out_specs=tuple([VM] * len(outs)),
        scratch_shapes=[pltpu.VMEM((beams, width), jnp.float32)],
        compiler_params=params(),
        cost_estimate=cost(4),
        name=f"beam_step_{level}",
    )(at, live, parents, gain[None, :], query, out_weight, code, *crosses, *inputs)


def shards(
    events,
    history_cache,
    block_counts,
    semantic_ids,
    beam_parents,
    query_weight,
    keyval_weight,
    out_weight,
    cross_weight,
    decoder_query,
    decoder_out,
    code_table,
    encoder_gain,
    cross_gain,
    decoder_gain,
):
    tp, kv = lax.axis_size("tp"), lax.axis_size("kv")
    my_tp, my_kv = lax.axis_index("tp"), lax.axis_index("kv")
    group, groups = my_tp * kv + my_kv, tp * kv

    at = position()
    joined = [query_weight, keyval_weight[0], keyval_weight[1]]
    crossing = jnp.concatenate([cross_weight[0], cross_weight[1]], axis=1)
    ringed = lax.axis_size("seq") <= RING_LIMIT
    blocks, firsts = collect_events(events)

    def look_up(waits):
        vocab_rows = code_table.shape[0]
        vocab_ids = group * vocab_rows + lax.broadcasted_iota(jnp.int32, (1, vocab_rows), 1)
        onehot = (semantic_ids.reshape(-1)[:, None] == vocab_ids).astype(jnp.bfloat16)
        onehot = after(onehot, *waits)
        rows = jnp.dot(onehot, code_table, preferred_element_type=jnp.float32).astype(jnp.bfloat16)
        for axis, size in (("kv", kv), ("tp", tp)):
            rows = sum([exchange(rows, axis, step) for step in range(1, size)], rows)
        return rows

    if ringed:
        joined, out, cross = map(Rows, (joined, out_weight, crossing))
        ways = [RING_WAYS[hop % len(RING_WAYS)] for hop in range(lax.axis_size("seq") - 1)]
        joined.hop(ways[0])
        blocks[1], joined.last[1] = lax.optimization_barrier((blocks[1], joined.last[1]))
        mine = jnp.concatenate(blocks, axis=0)
        joined.fresh = [(joined.last[1], 1)]
        stage = [joined.last[1]]
        event_pieces = gather_heads(mine)
        codes, turned = look_up(stage), after(decoder_out, *stage).T
        normed, source = norm_events(at, event_pieces, firsts, encoder_gain)
        for way in ways[1:]:
            joined.swap()
            swapped = joined.swapped()
            joined.hop(way, *stage)
            stage = [joined.last[way], swapped]
        normed, codes, turned, *stage = lax.optimization_barrier((normed, codes, turned, *stage))
        joined.swap(normed)
        out.start(*stage)
        normed, *_ = joined.held(normed, *out.last.values())
        joined_pieces = joined.pieces
        out.swap(*stage)
        out.end()
        cross.start(normed)
    else:
        joined_pieces, out_pieces, cross_pieces = map(
            whole_rows, (jnp.concatenate(joined, axis=1), out_weight, crossing)
        )
        normed, source = norm_events(at, gather_heads(blocks[0]), firsts, encoder_gain)
        codes = look_up([])
        turned = decoder_out.T
    attended = encoder_attention(
        at, normed, history_cache[:, 0], block_counts, joined_pieces
    )
    if ringed:
        out.swap(attended)
        out_pieces = out.pieces
        attended, *_ = lax.optimization_barrier((attended, *cross.last.values()))
    steps, beams = semantic_ids.shape
    codes = codes.reshape(steps, beams, codes.shape[1])

    def place(d, e, at):
        return partner(at[2], d, tp) * kv + partner(at[3], e, kv)

    orders = [[functools.partial(place, d, e) for d in range(tp)] for e in range(kv)]
    share = normed.shape[0] // groups
    parts = 2 if share % 32 == 0 else 1
    part = share // parts
    kept, *sent = project_out(at, attended, out_pieces, orders, part, parts)
    arrived = [
        [exchange(terms[step], "kv", e + 1) for e, terms in enumerate(sent)] for step in range(parts)
    ]
    late = []
    if ringed:
        cross.swap(attended)
        cross.end(attended, cross.last[-1])
        late = [piece for piece, _ in cross.pieces[1:]] + list(cross.last.values())

    def summed(d, step):
        rows = slice(d * part, (d + 1) * part)
        near = [kept[step], *arrived[step]]
        return sum(terms[rows].astype(jnp.float32) for terms in near).astype(jnp.bfloat16)

    merged = [
        merge_terms(
            step * part,
            source,
            [kept[step], *arrived[step]],
            jnp.stack([exchange(summed(d, step), "tp", d) for d in range(1, tp)]),
            cross_gain,
        )
        for step in range(parts)
    ]
    encoded = jnp.concatenate([encoded for encoded, _ in merged], axis=0)
    if ringed:
        cross.swap(merged[-1][1])
        cross_pieces = cross.pieces
    keys_values = []
    for index, (_, crossed) in enumerate(merged):
        waits = late if index == 0 else []
        if ringed and index == parts - 1:
            waits = [*waits, cross_pieces[-1][0]]
        crossed_pieces = [
            (rows, [functools.partial(lambda f, at: f(at) * part, where)])
            for rows, where in gather_heads(crossed, waits)
        ]
        keys_values.append(cross_project(at, crossed_pieces, cross_pieces, f"cross_project_{index}"))

    places = [functools.partial(place, 0, 0)]
    moves = []
    for d in range(tp):
        for e in range(kv):
            if d or e:
                places.append(functools.partial(place, d, e))
                moves.append(
                    [
                        (a * kv + b, partner(a, d, tp) * kv + partner(b, e, kv))
                        for a in range(tp)
                        for b in range(kv)
                    ]
                )
    inputs = []
    for level in range(steps):
        last = level == steps - 1
        kept, *sent = beam_step(
            at, level, block_counts, beam_parents, places, decoder_gain, decoder_query, turned,
            keys_values, codes[level], inputs, last,
        )
        if last:
            arrived = [lax.ppermute(v, ("tp", "kv"), move) for v, move in zip(sent, moves)]
        else:
            inputs = [kept] + [terms for terms, _ in gather_heads(sent[0])]
    beam_out = sum([a.astype(jnp.float32) for a in arrived], kept).astype(jnp.bfloat16)
    return (encoded[None], beam_out)


def solution(mesh):
    in_specs = (
        P("groups", "seq", ("tp", "kv")),
        P(None, ("groups", "seq"), None, ("tp", "kv")),
        P(("groups", "seq")),
        P(None, ("groups", "seq")),
        P(None, ("groups", "seq")),
        P("seq", ("tp", "kv")),
        P(None, "seq", ("tp", "kv")),
        P("seq", ("tp", "kv")),
        P(None, "seq", ("tp", "kv")),
        P(None, ("tp", "kv")),
        P(None, ("tp", "kv")),
        P(("tp", "kv"), None),
        P(),
        P(),
        P(),
    )
    out_specs = (P(("groups", "seq"), ("tp", "kv"), None), P(("groups", "seq"), ("tp", "kv")))
    return jax.shard_map(shards, mesh=mesh, in_specs=in_specs, out_specs=out_specs, check_vma=False)
```
